128 devices in a mesh: grp: 4 (over y_hi, core), pen: 32 (over x, y_lo, z).
Axes of the slice: x: 4, y: 4 (y_hi: 2, y_lo: 2; y = y_hi * 2 + y_lo), z: 4, core: 2. Of those that a mesh axis runs over, the one named last changes fastest.
Arguments:
- pressure_source: float32 [16, 1024, 4096], P('grp', None, 'pen'), may hold values from -15 to 15
- solid_temp: float32 [16, 1024, 4096], P(None, 'grp', 'pen'), may hold values from -6 to 6
- gas_wall_temp: float32 [1024, 4096], P('grp', 'pen'), may hold values from -6 to 6
- phase_map: int32 [16, 1024, 4096], P(None, 'grp', 'pen'), may hold values 0 or 1
- phase_conductivity: float32 [2], replicated, may hold values from 0.3 to 1
Outputs:
- pressure: float32 [16, 1024, 4096], P('grp', None, 'pen')
- solid_final: float32 [16, 1024, 4096], P(None, 'grp', 'pen')
The draws below stay inside these ranges and needn't reach their ends.
All inputs are finite; a program needn't handle non-finite values. No bound on the sum of `phase_map` on one device may be relied on, other than what follows from the above.
Results may differ from the reference program's by a relative error of at most 0.0003.
Values sent between devices are 32-bit elements; how exact they have to be, the bound alone decides.
No kernel may reach another device: no remote copies, remote signals or barrier semaphores. Data moves between devices by JAX's collectives and lax.ppermute only.
A program may use at most 128 MiB of HBM per device.

```python
import math
import jax
import jax.numpy as jnp

NX = 4096
NY = 1024
NZ = 16
SZ = 16
PHASES = 2


def draw_pressure_source(key, part):
    key = jax.random.fold_in(key, 11)
    grid_shape = (NZ, NY, NX)
    return jnp.clip(3.0 * jax.random.normal(key, grid_shape, jnp.float32), -15.0, 15.0)


def plant(drawn, stream_key, least, top_value):
    longest = drawn.shape.index(max(drawn.shape))
    spots = []
    for shift in (0, 1):
        where = [jax.random.randint(jax.random.fold_in(stream_key, axis), (), 0, length) for axis, length in enumerate(drawn.shape)]
        where[longest] = (where[longest] + shift) % drawn.shape[longest]
        spots.append(tuple(where))
    return drawn.at[spots[0]].set(least).at[spots[1]].set(top_value)


def level_of(key, dims, shards, least, top_value):
    gain = 1.0
    for dim, shards_of in shards:
        steps = jax.random.uniform(jax.random.fold_in(jax.random.fold_in(key, 6), dim), (shards_of,), jnp.float32, least / len(shards), top_value / len(shards))
        gain = gain * jnp.repeat(jnp.exp(steps), dims[dim] // shards_of).reshape((-1,) + (1,) * (len(dims) - 1 - dim))
    return gain


def gaussian(stream_key, dims, deviation, reach, pieces=(), kind=jnp.bfloat16):
    drawn = deviation * jax.random.normal(stream_key, dims, jnp.float32)
    if pieces:
        drawn = drawn * level_of(stream_key, dims, pieces, -0.22, 0.18)
    return jnp.clip(drawn, -reach, reach).astype(kind)


def setup_inputs(seed: int = 0) -> dict:
    splits = jax.random.split(jax.random.key(seed), 6)
    pressure_source = draw_pressure_source(jax.random.fold_in(splits[5], 71), 0)
    solid_temp = gaussian(splits[1], (SZ, NY, NX), 1.0, 6.0, ((1, 4), (2, 32)), jnp.float32)
    gas_wall_temp = gaussian(splits[2], (NY, NX), 1.0, 6.0, ((0, 4), (1, 32)), jnp.float32)
    phase_map = plant((jax.random.randint(splits[3], (SZ, NY, NX), 0, 2) < 1).astype(jnp.int32), jax.random.fold_in(splits[3], 1), 0, 1)
    phase_conductivity = jnp.clip(jnp.exp(jax.random.uniform(splits[4], (PHASES,), jnp.float32, math.log(0.3), math.log(1.0))), 0.3, 1.0)
    return {"pressure_source": pressure_source, "solid_temp": solid_temp, "gas_wall_temp": gas_wall_temp, "phase_map": phase_map, "phase_conductivity": phase_conductivity}


HEAT_TRANSFER = 1.0
PRESSURE_WORK = 0.5
STEP_RATE = 0.12


def hartley(field_in, axis_num):
    complex_spec = jnp.fft.fft(field_in, axis=axis_num)
    return jnp.real(complex_spec) - jnp.imag(complex_spec)


def depth_solve(source, eigen_sum):
    depth_len = source.shape[0]
    pivot_now = eigen_sum - 1.0
    carry_now = source[0]
    pivot_list = [pivot_now]
    carry_list = [carry_now]
    for plane_idx in range(1, depth_len):
        inverse = 1.0 / pivot_now
        pivot_now = eigen_sum - 2.0 - inverse
        carry_now = source[plane_idx] - inverse * carry_now
        pivot_list.append(pivot_now)
        carry_list.append(carry_now)
    upper_val = carry_list[depth_len - 1] / pivot_list[depth_len - 1]
    result_rows = [upper_val]
    for plane_idx in range(depth_len - 2, -1, -1):
        upper_val = (carry_list[plane_idx] - upper_val) / pivot_list[plane_idx]
        result_rows.append(upper_val)
    return jnp.stack(result_rows[::-1])


def conduct(padded_temp, padded_cond, flux_src):
    centre_temp = padded_temp[:, 1:-1, 1:-1]
    centre_cond = padded_cond[:, 1:-1, 1:-1]
    net_flux = jnp.zeros_like(centre_temp)
    neighbours = ((padded_temp[:, :-2, 1:-1], padded_cond[:, :-2, 1:-1]),
                  (padded_temp[:, 2:, 1:-1], padded_cond[:, 2:, 1:-1]),
                  (padded_temp[:, 1:-1, :-2], padded_cond[:, 1:-1, :-2]),
                  (padded_temp[:, 1:-1, 2:], padded_cond[:, 1:-1, 2:]))
    for shift_temp, shift_cond in neighbours:
        net_flux = net_flux + 0.5 * (centre_cond + shift_cond) * (shift_temp - centre_temp)
    vertical = 0.5 * (centre_cond[1:] + centre_cond[:-1]) * (centre_temp[1:] - centre_temp[:-1])
    net_flux = net_flux + jnp.pad(vertical, ((0, 1), (0, 0), (0, 0))) - jnp.pad(vertical, ((1, 0), (0, 0), (0, 0)))
    surface = jnp.concatenate([flux_src[None], jnp.zeros_like(centre_temp[1:])], axis=0)
    return centre_temp + STEP_RATE * (net_flux + surface)


def reference(pressure_source, solid_temp, gas_wall_temp, phase_map, phase_conductivity):
    spectrum = hartley(hartley(pressure_source, 1), 2)
    span_wave = jnp.arange(NY, dtype=jnp.float32)
    stream_wave = jnp.arange(NX, dtype=jnp.float32)
    eigen_span = 2.0 * jnp.cos(span_wave * (2.0 * math.pi / NY)) - 2.0
    eigen_stream = 2.0 * jnp.cos(stream_wave * (2.0 * math.pi / NX)) - 2.0
    eigen_sum = eigen_span[:, None] + eigen_stream[None, :]
    solved = depth_solve(spectrum, eigen_sum) * (1.0 / (NX * NY))
    pressure = hartley(hartley(solved, 2), 1)
    surface_flux = HEAT_TRANSFER * (gas_wall_temp + PRESSURE_WORK * pressure[0] - solid_temp[0])
    cell_cond = jnp.where(phase_map == 1, phase_conductivity[1], phase_conductivity[0])
    padded_cond = jnp.pad(cell_cond, ((0, 0), (1, 1), (1, 1)), mode="wrap")
    temp_now = solid_temp
    for section_idx in range(2):
        padded_temp = jnp.pad(temp_now, ((0, 0), (1, 1), (1, 1)), mode="wrap")
        temp_now = conduct(padded_temp, padded_cond, surface_flux)
    return pressure, temp_now
```

```python
import math

import jax
import jax.numpy as jnp
import numpy as np
from jax import lax
from jax.sharding import PartitionSpec as P

HIGH = lax.Precision.HIGH
HEAT_TRANSFER = 1.0
PRESSURE_WORK = 0.5
STEP_RATE = 0.12
Z_RING, Y_PAIR, X_RING = 4, 2, 4


def make_tables(span_len, width, depth):
    half = span_len // 2
    waves = np.stack([2 * np.arange(half), 2 * np.arange(half) + 1]).astype(np.float64)
    rows = np.arange(half)
    angle = 2 * np.pi * ((rows[None, :, None] * waves[:, None, :]) % span_len) / span_len
    span = np.cos(angle) + np.sin(angle)
    lam = -4 * np.sin(np.pi * waves / span_len) ** 2
    order = np.concatenate([np.arange(0, width, 2), np.arange(1, width, 2)]) + 1.0
    cells = np.arange(width) + 1.0
    sine = np.sqrt(2 / (width + 1)) * np.sin(np.pi * cells[:, None] * order[None, :] / (width + 1))
    sigma = -4 * np.sin(np.pi * order / (2 * (width + 1))) ** 2
    modes = np.arange(depth)
    theta = np.pi * (2 * modes + 1) / (2 * depth + 1)
    depth_basis = np.cos(theta[None, :] * (np.arange(depth)[:, None] + 0.5)) / np.sqrt((2 * depth + 1) / 4)
    mu = -4 * np.sin(theta / 2) ** 2
    stretch = -(mu[None, :, None] + lam[:, None, :])
    log_rho = -2 * np.arcsinh(np.sqrt(stretch) / 2)
    f32 = lambda v: np.asarray(v, np.float32)
    return {
        "span": f32(span), "lam": f32(lam), "sine": f32(sine), "sigma": f32(sigma),
        "basis": f32(depth_basis), "mu": f32(mu), "log_rho": f32(log_rho),
    }


def mover(groups, pencils):
    def move(value, target):
        pairs = []
        for g in range(groups):
            for p in range(pencils):
                to = target(g, p)
                pairs.append((g * pencils + p, to[0] * pencils + to[1]))
        return lax.ppermute(value, ("grp", "pen"), pairs)

    return move


def with_halo(cells, sides, width):
    for axis, dim in sides:
        count = lax.axis_size(axis)
        head = lax.slice_in_dim(cells, 0, width, axis=dim)
        tail = lax.slice_in_dim(cells, cells.shape[dim] - width, cells.shape[dim], axis=dim)
        cells = jnp.concatenate(
            [
                lax.ppermute(tail, axis, [(i, (i + 1) % count) for i in range(count)]),
                cells,
                lax.ppermute(head, axis, [((i + 1) % count, i) for i in range(count)]),
            ],
            axis=dim,
        )
    return cells


def conduct(padded_temp, padded_cond, flux_src):
    centre_temp = padded_temp[:, 1:-1, 1:-1]
    centre_cond = padded_cond[:, 1:-1, 1:-1]
    net_flux = jnp.zeros_like(centre_temp)
    neighbours = (
        (padded_temp[:, :-2, 1:-1], padded_cond[:, :-2, 1:-1]),
        (padded_temp[:, 2:, 1:-1], padded_cond[:, 2:, 1:-1]),
        (padded_temp[:, 1:-1, :-2], padded_cond[:, 1:-1, :-2]),
        (padded_temp[:, 1:-1, 2:], padded_cond[:, 1:-1, 2:]),
    )
    for shift_temp, shift_cond in neighbours:
        net_flux = net_flux + 0.5 * (centre_cond + shift_cond) * (shift_temp - centre_temp)
    vertical = 0.5 * (centre_cond[1:] + centre_cond[:-1]) * (centre_temp[1:] - centre_temp[:-1])
    net_flux = (
        net_flux
        + jnp.pad(vertical, ((0, 1), (0, 0), (0, 0)))
        - jnp.pad(vertical, ((1, 0), (0, 0), (0, 0)))
    )
    surface = jnp.concatenate([flux_src[None], jnp.zeros_like(centre_temp[1:])], axis=0)
    return centre_temp + STEP_RATE * (net_flux + surface)


def forward_part(folded, span_table, sine):
    shifted = jnp.einsum("zyx,yk->zxk", folded, span_table, precision=HIGH)
    return jnp.einsum("xj,zxk->zjk", sine, shifted, precision=HIGH)


def chain(first, centre, count):
    inverse = [1.0 / (centre + first)]
    for _ in range(1, count):
        inverse.append(1.0 / (centre - inverse[-1]))
    return inverse


def per_device(pressure_source, solid_temp, gas_wall_temp, phase_map, phase_conductivity):
    groups = lax.axis_size("grp")
    pencils = lax.axis_size("pen")
    group_idx = lax.axis_index("grp")
    pencil_idx = lax.axis_index("pen")
    depth_loc, span_len, width = pressure_source.shape
    depth = depth_loc * groups
    half = span_len // 2
    own = depth // 2
    core = group_idx % 2
    low = group_idx // 2 == 1
    zi = pencil_idx % Z_RING
    yl = pencil_idx // Z_RING % Y_PAIR
    place = pencil_idx % (Z_RING * Y_PAIR)
    move = mover(groups, pencils)
    tab = make_tables(span_len, width, depth)
    span_table = jnp.asarray(tab["span"])[core]
    lam = jnp.asarray(tab["lam"])[core]
    log_rho = jnp.asarray(tab["log_rho"])[core]
    sine = jnp.asarray(tab["sine"])
    edge = sine[0][:, None]
    sigma = jnp.asarray(tab["sigma"])
    basis = jnp.asarray(tab["basis"])
    mu = jnp.asarray(tab["mu"])

    top = pressure_source[:, :half]
    bottom = pressure_source[:, half:]
    sign = jnp.where(core == 0, 1.0, -1.0).astype(jnp.float32)
    other_core = lambda g, p: (g ^ 1, p)
    other_half = lambda g, p: (g ^ 2, p)
    arrived = move(top - sign * bottom, other_core)
    held = forward_part(top + sign * bottom, span_table, sine)
    come = forward_part(arrived, span_table, sine)
    both = jnp.concatenate([held, come], axis=0) * (1.0 / span_len)
    code = jnp.where(group_idx == 0, 0, jnp.where(group_idx == 1, 4, jnp.where(group_idx == 2, 7, 3)))
    planes = [lax.dynamic_index_in_dim(both, jnp.bitwise_xor(i, code), 0, keepdims=False) for i in range(own)]
    plane_z = [jnp.where(low, depth - 1 - i, i) for i in range(own)]
    other_z = [jnp.where(low, i, depth - 1 - i) for i in range(own)]

    part = sum(basis[plane_z[i]][:, None, None] * planes[i][None] for i in range(own))
    part = part * edge[None] / (mu[:, None, None] + lam[None, None, :] + sigma[None, :, None])
    even = jnp.sum(part[:, : width // 2], axis=1)
    odd = jnp.sum(part[:, width // 2 :], axis=1)
    edge_low, edge_high = even + odd, even - odd
    power = lambda n: jnp.exp(log_rho * n)
    hop = power(float(width))
    far = power(width + 1.0)
    right = edge_high + far * edge_low
    left = edge_low + far * edge_high
    rho = power(1.0)
    per_rho = power(-1.0)

    packed = jnp.stack([right, left])
    low_sum = jnp.zeros_like(right)
    high_sum = jnp.zeros_like(right)
    wide = float(width)
    right4 = power(wide * (Z_RING - 1 - zi)) * right
    left4 = power(wide * zi) * left
    for d in range(1, Z_RING):
        got = move(packed, lambda g, p, d=d: (g, p // Z_RING * Z_RING + (p + d) % Z_RING))
        source = (zi - d) % Z_RING
        before = zi >= d
        low_sum = low_sum + jnp.where(before, power(wide * (d - 1)), 0.0) * got[0]
        high_sum = high_sum + jnp.where(before, 0.0, power(wide * (Z_RING - 1 - d))) * got[1]
        right4 = right4 + power(wide * (Z_RING - 1 - source)) * got[0]
        left4 = left4 + power(wide * source) * got[1]
    into_low = per_rho * low_sum + left + hop * high_sum
    into_high = per_rho * high_sum + right + hop * low_sum

    first = move(jnp.stack([into_low, into_high, right4, left4]), other_half)
    group4 = jnp.stack([right4, left4])
    other = move(group4, lambda g, p: (g, p ^ Z_RING)) + move(group4, lambda g, p: (g ^ 2, p ^ Z_RING))
    into_low = into_low + first[0]
    into_high = into_high + first[1]
    right4 = right4 + first[2]
    left4 = left4 + first[3]
    after = yl == 1
    low_sum = jnp.where(after, power(wide * zi), 0.0) * other[0]
    high_sum = jnp.where(after, 0.0, power(wide * (Z_RING - 1 - zi))) * other[1]
    run = power(wide * Z_RING)
    right8 = jnp.where(after, run * other[0] + right4, run * right4 + other[0])
    left8 = jnp.where(after, other[1] + run * left4, left4 + run * other[1])

    packed = jnp.stack([right8, left8])
    block = Z_RING * Y_PAIR
    right_sum = power(wide * block * (X_RING - 1)) * right8
    left_sum = power(wide * block * (X_RING - 1)) * left8
    for d in range(1, X_RING):
        got = move(packed, lambda g, p, d=d: (g, (p + block * d) % pencils))
        right_sum = right_sum + power(wide * block * (d - 1)) * got[0]
        left_sum = left_sum + power(wide * block * (X_RING - 1 - d)) * got[1]
    whole = 1.0 / (1.0 - power(wide * block * X_RING))
    low_sum = low_sum + power(wide * place) * right_sum * whole
    high_sum = high_sum + power(wide * (block - 1 - place)) * left_sum * whole
    gain = rho / (1.0 - rho * rho)
    into_low = gain * (into_low + per_rho * low_sum + hop * high_sum)
    into_high = gain * (into_high + per_rho * high_sum + hop * low_sum)
    gain_low = jnp.einsum("zm,mk->zk", basis, into_low, precision=lax.Precision.HIGHEST)
    gain_high = jnp.einsum("zm,mk->zk", basis, into_high, precision=lax.Precision.HIGHEST)

    centre = lam[None, :] + sigma[:, None] - 2.0
    inner = chain(jnp.where(low, 0.0, 1.0), centre, own)
    outer = chain(jnp.where(low, 1.0, 0.0), centre, own)
    carry = planes[0] * inner[0]
    carries = [carry]
    for i in range(1, own):
        carry = (planes[i] - carry) * inner[i]
        carries.append(carry)
    wall = carries[own - 1]
    for i in range(own - 2, -1, -1):
        wall = carries[i] - inner[i] * wall
    sent = move(jnp.stack([carries[own - 1], wall]), other_half)

    both_edges = jnp.where(
        (jnp.arange(width) < width // 2)[None, :, None],
        (gain_low + gain_high)[:, None, :],
        (gain_low - gain_high)[:, None, :],
    )
    edge_rhs = -edge[None] * both_edges
    at = lambda z: lax.dynamic_index_in_dim(edge_rhs, z, 0, keepdims=False)
    carries = []
    carry = 0.0
    for i in range(own):
        carry = (planes[i] + at(plane_z[i]) - carry) * inner[i]
        carries.append(carry)
    other_carries = []
    carry = 0.0
    for i in range(own):
        carry = (at(other_z[i]) - carry) * outer[i]
        other_carries.append(carry)
    there = sent[0] + other_carries[own - 1]
    value = (carries[own - 1] - inner[own - 1] * there) / (1.0 - inner[own - 1] * outer[own - 1])
    solved = [value]
    for i in range(own - 2, -1, -1):
        solved.append(carries[i] - inner[i] * solved[-1])
    solved = solved[::-1]
    back = value
    for i in range(own - 1, -1, -1):
        back = other_carries[i] - outer[i] * back
    first_plane = jnp.where(low, sent[1] + back, solved[0])

    stacked = jnp.stack(solved)
    ordered = jnp.stack(
        [lax.dynamic_index_in_dim(stacked, jnp.bitwise_xor(i, code), 0, keepdims=False) for i in range(own)]
    )
    to_cells = lambda v: jnp.einsum("xj,zjk->zxk", sine, v, precision=HIGH)
    to_span = lambda v: jnp.einsum("yk,zxk->zyx", span_table, v, precision=HIGH)
    wall_cells = to_cells(first_plane[None])
    wall_cells = jnp.concatenate([gain_low[0][None, None], wall_cells, gain_high[0][None, None]], axis=1)
    wall_mine = to_span(wall_cells)[0]
    wall_other = move(wall_mine, other_core)
    mine = to_span(to_cells(ordered))
    got = move(mine[depth_loc:], other_core)
    mine = mine[:depth_loc]
    even_part = jnp.where(core == 0, mine, got)
    odd_part = jnp.where(core == 0, got, mine)
    pressure = jnp.concatenate([even_part + odd_part, even_part - odd_part], axis=1)

    even_wall = jnp.where(core == 0, wall_mine, wall_other)
    odd_wall = jnp.where(core == 0, wall_other, wall_mine)
    whole_wall = jnp.concatenate([even_wall + odd_wall, even_wall - odd_wall], axis=0)
    tile_rows = span_len // groups
    begin = group_idx * tile_rows
    padded_wall = jnp.concatenate([whole_wall[-1:], whole_wall, whole_wall[:1]], axis=0)
    wall_press = lax.dynamic_slice_in_dim(padded_wall, begin, tile_rows + 2, 0)

    cell_cond = jnp.where(phase_map == 1, phase_conductivity[1], phase_conductivity[0])
    sides = (("grp", 1), ("pen", 2))
    padded_cond = with_halo(cell_cond, sides, 1)
    dry_flux = HEAT_TRANSFER * (gas_wall_temp - solid_temp[0])
    base = conduct(with_halo(solid_temp, sides, 1), padded_cond, dry_flux)
    base = conduct(with_halo(base, sides, 1), padded_cond, dry_flux)
    share = STEP_RATE * HEAT_TRANSFER * PRESSURE_WORK * wall_press
    centre_share = share[1:-1, 1:-1]
    here = padded_cond[0, 1:-1, 1:-1]
    added = 2.0 * centre_share
    for rows, cols in ((0, 1), (2, 1), (1, 0), (1, 2)):
        window = (slice(rows, rows + tile_rows), slice(cols, cols + width))
        added = added + (0.5 * STEP_RATE) * (here + padded_cond[0][window]) * (share[window] - centre_share)
    down = (0.5 * STEP_RATE) * (here + cell_cond[1]) * centre_share
    added = added - down
    final = base.at[0].add(added).at[1].add(down)
    return (pressure, final)


def solution(mesh):
    in_specs = (
        P("grp", None, "pen"),
        P(None, "grp", "pen"),
        P("grp", "pen"),
        P(None, "grp", "pen"),
        P(),
    )
    out_specs = (P("grp", None, "pen"), P(None, "grp", "pen"))
    return jax.shard_map(
        per_device, mesh=mesh, in_specs=in_specs, out_specs=out_specs, check_vma=False
    )
```

```python
import functools
import math

import jax
import jax.numpy as jnp
import numpy as np
from jax import lax
from jax.experimental import pallas as pl
from jax.experimental.pallas import tpu as pltpu
from jax.sharding import PartitionSpec as P

HIGHEST = lax.Precision.HIGHEST
HEAT_TRANSFER = 1.0
PRESSURE_WORK = 0.5
STEP_RATE = 0.12
Z_RING, Y_PAIR, X_RING = 4, 2, 4
VMEM_LIMIT = 48 * 1024 * 1024
LANES = 256


def halves(value):
    high = np.asarray(value, np.float32).astype(jnp.bfloat16)
    low = (np.asarray(value, np.float64) - high.astype(np.float64)).astype(jnp.bfloat16)
    return high, low


def make_tables(span_len, width, depth):
    half = span_len // 2
    waves = np.stack([2 * np.arange(half), 2 * np.arange(half) + 1]).astype(np.float64)
    rows = np.arange(half)
    angle = 2 * np.pi * ((rows[None, :, None] * waves[:, None, :]) % span_len) / span_len
    span = np.cos(angle) + np.sin(angle)
    lam = -4 * np.sin(np.pi * waves / span_len) ** 2
    order = np.concatenate([np.arange(0, width, 2), np.arange(1, width, 2)]) + 1.0
    cells = np.arange(width) + 1.0
    sine = np.sqrt(2 / (width + 1)) * np.sin(np.pi * cells[:, None] * order[None, :] / (width + 1))
    sigma = -4 * np.sin(np.pi * order / (2 * (width + 1))) ** 2
    modes = np.arange(depth)
    theta = np.pi * (2 * modes + 1) / (2 * depth + 1)
    basis = np.cos(theta[None, :] * (np.arange(depth)[:, None] + 0.5)) / np.sqrt((2 * depth + 1) / 4)
    mu = -4 * np.sin(theta / 2) ** 2
    stretch = -(mu[None, :, None] + lam[:, None, :])
    log_rho = -2 * np.arcsinh(np.sqrt(stretch) / 2)
    down = np.arange(depth // 2)
    up = depth - 1 - down
    ordered = np.stack([basis[np.concatenate([down, up])], basis[np.concatenate([up, down])]])
    pair = np.kron(np.eye(2), sine)
    f32 = lambda v: np.asarray(v, np.float32)
    lanes = min(LANES, half)
    return {
        "span": halves(span),
        "into": halves(pair / span_len),
        "back": halves(pair.T),
        "lam": f32(lam)[:, None, :],
        "sigma": f32(np.repeat(sigma[:, None], lanes, 1)),
        "edge": f32(np.repeat(sine[0][:, None], lanes, 1)),
        "basis": f32(ordered),
        "basis_t": f32(np.swapaxes(ordered, 1, 2)),
        "log_rho": f32(log_rho),
        "far": f32(np.exp(log_rho * (width + 1))),
    }


def product(first, second):
    return jnp.dot(first, second, preferred_element_type=jnp.float32)


def split(value):
    high = value.astype(jnp.bfloat16)
    return high, (value - high.astype(jnp.float32)).astype(jnp.bfloat16)


def times(value, high, low):
    value_high, value_low = split(value)
    return product(value_high, high) + (product(value_high, low) + product(value_low, high))


def times_turned(high, low, value):
    value_high, value_low = split(value)
    turned = lambda a, b: lax.dot_general(
        a, b, (((1,), (1,)), ((), ())), preferred_element_type=jnp.float32
    )
    return turned(high, value_high) + (turned(low, value_high) + turned(high, value_low))


def whole(array):
    return pl.BlockSpec(array.shape, lambda i, s: (0,) * len(array.shape))


def chosen(array, place):
    rest = array.shape[1:]
    return pl.BlockSpec((1,) + rest, lambda i, s: (s[place],) + (0,) * len(rest))


def run(body, scalars, arrays, specs, outs, out_specs=None, scratch=(), aliases=None, flops=0):
    outs = [jax.ShapeDtypeStruct(shape, jnp.float32) for shape in outs]
    moved = sum(math.prod(a.shape) * 4 for a in arrays) + sum(math.prod(o.shape) * 4 for o in outs)
    return pl.pallas_call(
        body,
        out_shape=outs,
        grid_spec=pltpu.PrefetchScalarGridSpec(
            num_scalar_prefetch=1,
            grid=(1,),
            in_specs=specs,
            out_specs=out_specs or [whole(o) for o in outs],
            scratch_shapes=list(scratch),
        ),
        input_output_aliases=aliases or {},
        compiler_params=pltpu.CompilerParams(vmem_limit_bytes=VMEM_LIMIT),
        cost_estimate=pl.CostEstimate(flops=flops, bytes_accessed=moved, transcendentals=0),
    )(scalars, *arrays)


def spectral(planes, into_high, into_low, span_high, span_low):
    turned = []
    for pair in range(0, len(planes), 2):
        cells = jnp.concatenate(planes[pair : pair + 2], axis=1)
        turned.append(times(cells, into_high, into_low).T)
    return times(jnp.concatenate(turned, axis=0), span_high, span_low)


def held_body(s_ref, source, into_high, into_low, span_high, span_low, out):
    count, span_len, _ = source.shape
    half = span_len // 2
    sign = (1 - 2 * s_ref[0]).astype(jnp.float32)
    planes = [source[z, :half] + sign * source[z, half:] for z in range(count)]
    out[...] = spectral(
        planes, into_high[...], into_low[...], span_high[0], span_low[0]
    ).reshape(out.shape)


def continuants(centre, first, count):
    values = [jnp.ones_like(centre), centre + first]
    for _ in range(1, count):
        values.append(centre * values[-1] - values[-2])
    return values


def arrived_body(
    s_ref, arrived, held, into_high, into_low, span_high, span_low, lam, sigma, edge, basis_t, far,
    planes, edges, sent, sums,
):
    count = held.shape[0]
    own = 2 * count
    width, half = held.shape[1:]
    lanes = sigma.shape[1]
    pieces = half // lanes
    planes[:count] = held[...]
    planes[count:] = spectral(
        [arrived[z] for z in range(count)], into_high[...], into_low[...], span_high[0], span_low[0]
    ).reshape(held.shape)
    sums[...] = jnp.zeros_like(sums)
    low = s_ref[1].astype(jnp.float32)
    code = s_ref[2]
    side = width // 16

    def tile(t, nothing):
        group = t // pieces
        rows = pl.ds(pl.multiple_of(group * 8, 8), 8)
        cols = pl.ds(pl.multiple_of(t % pieces * lanes, lanes), lanes)
        parity = group // side
        centre = lam[0, :, cols] + sigma[rows] - 2.0
        mine = continuants(centre, 1.0 - low, own)
        other = continuants(centre, low, own)
        carry = planes[code, rows, cols]
        carries = [carry]
        for i in range(1, own):
            carry = mine[i] * planes[jnp.bitwise_xor(i, code), rows, cols] - carry
            carries.append(carry)
        sent[0, rows, cols] = carry
        shared = carry / (mine[own] * other[own] - mine[own - 1] * other[own - 1])
        scale = edge[rows]
        value = shared * other[own]
        sums[parity, own - 1, :, cols] += scale * value
        for i in range(own - 2, -1, -1):
            value = (carries[i] - mine[i] * value) / mine[i + 1]
            sums[parity, i, :, cols] += scale * value
        sent[1, rows, cols] = value + other[own - 1] * shared / mine[own]
        shared = scale * shared
        for i in range(own):
            term = other[i] * shared
            sums[parity, own + i, :, cols] += term if (own - i) % 2 == 0 else -term
        return nothing

    lax.fori_loop(0, (width // 8) * pieces, tile, 0)
    total = jnp.sum(sums[...], axis=2)
    modal = lambda v: jnp.dot(basis_t[0], v, precision=HIGHEST, preferred_element_type=jnp.float32)
    even = modal(total[0])
    odd = modal(total[1])
    edge_low = even + odd
    edge_high = even - odd
    edges[0] = edge_high + far[0] * edge_low
    edges[1] = edge_low + far[0] * edge_high


def solve_body(
    s_ref, planes, got, gains, span_high, span_low, back_high, back_low, lam, sigma, edge, basis,
    wall, away, keep, solved, both, first,
):
    own, width, half = planes.shape
    count = own // 2
    lanes = sigma.shape[1]
    pieces = half // lanes
    low = s_ref[1].astype(jnp.float32)
    is_low = s_ref[1] == 1
    code = s_ref[2]
    depthwise = lambda v: jnp.dot(basis[0], v, precision=HIGHEST, preferred_element_type=jnp.float32)
    gain_low = depthwise(gains[0])
    gain_high = depthwise(gains[1])
    both[0] = gain_low + gain_high
    both[1] = gain_low - gain_high
    first[...] = jnp.zeros_like(first)
    first[width : width + 1] = jnp.where(is_low, gain_low[own : own + 1], gain_low[:1])
    first[width + 1 : width + 2] = jnp.where(is_low, gain_high[own : own + 1], gain_high[:1])
    side = width // 16

    def tile(t, nothing):
        group = t // pieces
        rows = pl.ds(pl.multiple_of(group * 8, 8), 8)
        cols = pl.ds(pl.multiple_of(t % pieces * lanes, lanes), lanes)
        parity = group // side
        centre = lam[0, :, cols] + sigma[rows] - 2.0
        mine = continuants(centre, 1.0 - low, own)
        other = continuants(centre, low, own)
        scale = edge[rows]
        rhs = lambda i: scale * both[parity, i : i + 1, cols]
        carry = planes[code, rows, cols] - rhs(0)
        carries = [carry]
        for i in range(1, own):
            carry = mine[i] * (planes[jnp.bitwise_xor(i, code), rows, cols] - rhs(i)) - carry
            carries.append(carry)
        right = rhs(own)
        there = -right
        direct = -mine[own - 1] * right
        for i in range(1, own):
            right = rhs(own + i)
            there = -other[i] * right - there
            term = mine[own - 1 - i] * right
            direct = direct - term if i % 2 == 0 else direct + term
        there = there + got[0, rows, cols]
        value = (carry * other[own] - mine[own - 1] * there) / (
            mine[own] * other[own] - mine[own - 1] * other[own - 1]
        )
        far_first = got[1, rows, cols] + (direct + value) / other[own]
        solved[jnp.bitwise_xor(own - 1, code), rows, cols] = value
        for i in range(own - 2, -1, -1):
            value = (carries[i] - mine[i] * value) / mine[i + 1]
            solved[jnp.bitwise_xor(i, code), rows, cols] = value
        first[rows, cols] = jnp.where(is_low, far_first, value)
        return nothing

    lax.fori_loop(0, (width // 8) * pieces, tile, 0)
    table_high = span_high[0]
    table_low = span_low[0]
    line = times_turned(table_high, table_low, first[...])
    main = times(line[:, :width], back_high[:width, :width], back_low[:width, :width])
    wall[...] = jnp.concatenate([main, line[:, width:]], axis=1)
    for pair in range(0, count, 2):
        values = solved[count + pair : count + pair + 2].reshape(2 * width, half)
        cells = times(times_turned(table_high, table_low, values), back_high[...], back_low[...])
        away[pair] = cells[:, :width]
        away[pair + 1] = cells[:, width:]
    keep[...] = solved[:count]


def cells_body(s_ref, keep, span_high, span_low, back_high, back_low, mine):
    count, width, half = keep.shape
    for pair in range(0, count, 2):
        values = keep[pair : pair + 2].reshape(2 * width, half)
        cells = times(times_turned(span_high[0], span_low[0], values), back_high[...], back_low[...])
        mine[pair] = cells[:, :width]
        mine[pair + 1] = cells[:, width:]


def join_body(s_ref, mine, came, out):
    half = mine.shape[1]
    sign = (1 - 2 * s_ref[0]).astype(jnp.float32)
    ours = mine[...]
    theirs = came[...]
    out[:, :half] = ours + theirs
    out[:, half:] = sign * (ours - theirs)


def edge_body(s_ref, temp, phase, conductivity, across, along):
    depth, rows, width = temp.shape
    lane = lax.broadcasted_iota(jnp.int32, (rows, width), 1)
    cold, warm = conductivity[0], conductivity[1]

    def plane(z, packed):
        cond = jnp.where(phase[z] == 1, warm, cold)
        both = (temp[z], cond)
        for k in range(2):
            at = k * depth + z
            packed = jnp.where(lane == at, pltpu.roll(both[k], at + 1, 1), packed)
            at = (2 + k) * depth + z
            packed = jnp.where(lane == at, pltpu.roll(both[k], at, 1), packed)
            place = pl.ds(k * depth + z, 1)
            along[0, place] = both[k][rows - 1 :]
            along[1, place] = both[k][:1]
        return packed

    packed = lax.fori_loop(0, depth, plane, jnp.zeros((rows, width), jnp.float32)).T
    across[0] = packed[: 2 * depth]
    across[1] = packed[2 * depth : 4 * depth]


def faces(value, row, lane, up, down, left, right):
    rows, width = value.shape
    return (
        jnp.where(row == 0, up, pltpu.roll(value, 1, 0)),
        jnp.where(row == rows - 1, down, pltpu.roll(value, rows - 1, 0)),
        jnp.where(lane == 0, left, pltpu.roll(value, 1, 1)),
        jnp.where(lane == width - 1, right, pltpu.roll(value, width - 1, 1)),
    )


def stage_columns(columns, sides, used):
    columns[...] = jnp.zeros_like(columns)
    at = 0
    for side in sides:
        columns[at : at + used] = side[...]
        at += used
    return columns[...].T


def first_body(
    s_ref, temp, phase, gas, conductivity, from_left, from_right, from_up, from_down,
    out, across, along, columns,
):
    depth, rows, width = temp.shape
    row = lax.broadcasted_iota(jnp.int32, (rows, width), 0)
    lane = lax.broadcasted_iota(jnp.int32, (rows, width), 1)
    cold, warm = conductivity[0], conductivity[1]
    halo = stage_columns(columns, (from_left, from_right), 2 * depth)
    conduct = lambda z: jnp.where(phase[z] == 1, warm, cold)

    def plane(z, packed):
        here = temp[z]
        cond = conduct(z)
        near = lambda k: (
            from_up[pl.ds(k * depth + z, 1)],
            from_down[pl.ds(k * depth + z, 1)],
            pltpu.roll(halo, width - (k * depth + z), 1),
            pltpu.roll(halo, width - 1 - ((2 + k) * depth + z), 1),
        )
        total = jnp.zeros_like(here)
        for side_temp, side_cond in zip(
            faces(here, row, lane, *near(0)), faces(cond, row, lane, *near(1))
        ):
            total = total + (cond + side_cond) * (side_temp - here)
        for beside in (jnp.maximum(z - 1, 0), jnp.minimum(z + 1, depth - 1)):
            total = total + (cond + conduct(beside)) * (temp[beside] - here)
        surface = jnp.where(z == 0, STEP_RATE * HEAT_TRANSFER, 0.0) * (gas[...] - temp[0])
        value = here + (0.5 * STEP_RATE) * total + surface
        out[z] = value
        packed = jnp.where(lane == z, pltpu.roll(value, z + 1, 1), packed)
        packed = jnp.where(lane == depth + z, pltpu.roll(value, depth + z, 1), packed)
        along[0, pl.ds(z, 1)] = value[rows - 1 :]
        along[1, pl.ds(z, 1)] = value[:1]
        return packed

    packed = lax.fori_loop(0, depth, plane, jnp.zeros((rows, width), jnp.float32)).T
    across[0] = packed[:depth]
    across[1] = packed[depth : 2 * depth]


def second_body(
    s_ref, base, temp, phase, gas, conductivity, from_left, from_right, from_up, from_down,
    base_left, base_right, base_up, base_down, out, weights, columns,
):
    depth, rows, width = base.shape
    row = lax.broadcasted_iota(jnp.int32, (rows, width), 0)
    lane = lax.broadcasted_iota(jnp.int32, (rows, width), 1)
    cold, warm = conductivity[0], conductivity[1]
    halo = stage_columns(columns, (from_left, from_right), 2 * depth)
    base_halo = stage_columns(columns, (base_left, base_right), depth)
    conduct = lambda z: jnp.where(phase[z] == 1, warm, cold)

    def plane(z, nothing):
        here = base[z]
        cond = conduct(z)
        near_base = (
            base_up[pl.ds(z, 1)],
            base_down[pl.ds(z, 1)],
            pltpu.roll(base_halo, width - z, 1),
            pltpu.roll(base_halo, width - 1 - (depth + z), 1),
        )
        near_cond = (
            from_up[pl.ds(depth + z, 1)],
            from_down[pl.ds(depth + z, 1)],
            pltpu.roll(halo, width - (depth + z), 1),
            pltpu.roll(halo, width - 1 - (3 * depth + z), 1),
        )
        total = jnp.zeros_like(here)
        pairs = []
        for side_base, side_cond in zip(
            faces(here, row, lane, *near_base), faces(cond, row, lane, *near_cond)
        ):
            pair = cond + side_cond
            pairs.append(pair)
            total = total + pair * (side_base - here)
        for beside in (jnp.maximum(z - 1, 0), jnp.minimum(z + 1, depth - 1)):
            pair = cond + conduct(beside)
            total = total + pair * (base[beside] - here)
        pairs.append(pair)
        surface = jnp.where(z == 0, STEP_RATE * HEAT_TRANSFER, 0.0) * (gas[...] - temp[0])
        out[z] = here + (0.5 * STEP_RATE) * total + surface

        @pl.when(z == 0)
        def _():
            for k in range(5):
                weights[k] = (0.5 * STEP_RATE) * pairs[k]

        return nothing

    lax.fori_loop(0, depth, plane, 0)


def wall_body(s_ref, ours, theirs, weights, base, out):
    half = ours.shape[0]
    rows, width = weights.shape[1:]
    sign = (1 - 2 * s_ref[0]).astype(jnp.float32)
    bottom = (1 - 2 * s_ref[3]).astype(jnp.float32)
    second = s_ref[4] == 1
    factor = STEP_RATE * HEAT_TRANSFER * PRESSURE_WORK

    def lines(start, count, minus):
        our_sign = jnp.where(s_ref[0] == 0, 1.0, minus) * factor
        their_sign = jnp.where(s_ref[0] == 0, minus, 1.0) * factor
        at = pl.ds(start, count)
        return our_sign * ours[at] + their_sign * theirs[at]

    begin = pl.multiple_of(s_ref[4] * rows, rows)
    middle = lines(begin, rows, bottom)
    above = lines(jnp.where(second, rows - 1, half - 1), 1, jnp.where(second, bottom, -bottom))
    below = lines(jnp.where(second, 0, rows), 1, jnp.where(second, -bottom, bottom))
    share = middle[:, :width]
    row = lax.broadcasted_iota(jnp.int32, (rows, width), 0)
    lane = lax.broadcasted_iota(jnp.int32, (rows, width), 1)
    around = faces(
        share, row, lane, above[:, :width], below[:, :width],
        middle[:, width : width + 1], middle[:, width + 1 : width + 2],
    )
    added = 2.0 * share
    for k in range(4):
        added = added + weights[k] * (around[k] - share)
    down = weights[4] * share
    out[0] = base[0] + added - down
    out[1] = base[1] + down


def mover(groups, pencils):
    def move(value, target):
        pairs = []
        for g in range(groups):
            for p in range(pencils):
                to = target(g, p)
                pairs.append((g * pencils + p, to[0] * pencils + to[1]))
        return lax.ppermute(value, ("grp", "pen"), pairs)

    return move


def per_device(pressure_source, solid_temp, gas_wall_temp, phase_map, phase_conductivity):
    groups = lax.axis_size("grp")
    pencils = lax.axis_size("pen")
    group_idx = lax.axis_index("grp")
    pencil_idx = lax.axis_index("pen")
    depth_loc, span_len, width = pressure_source.shape
    depth = depth_loc * groups
    half = span_len // 2
    own = depth // 2
    core = group_idx % 2
    low = group_idx // 2
    zi = pencil_idx % Z_RING
    yl = pencil_idx // Z_RING % Y_PAIR
    place = pencil_idx % (Z_RING * Y_PAIR)
    move = mover(groups, pencils)
    tab = make_tables(span_len, width, depth)
    const = {k: tuple(map(jnp.asarray, v)) if isinstance(v, tuple) else jnp.asarray(v) for k, v in tab.items()}
    code = jnp.where(low == 0, core * 4, 7 - 4 * core)
    scalars = jnp.stack([core, low, code, low, core]).astype(jnp.int32)
    span = list(const["span"])
    into = list(const["into"])
    back = list(const["back"])
    span_specs = [chosen(a, 0) for a in span]
    into_specs = [whole(a) for a in into]
    back_specs = [whole(a) for a in back]
    strip = [const["lam"], const["sigma"], const["edge"]]
    strip_specs = [chosen(strip[0], 0), whole(strip[1]), whole(strip[2])]
    smem = pl.BlockSpec(memory_space=pltpu.SMEM)

    tile_rows = span_len // groups
    right_on = lambda g, p: (g, (p + 1) % pencils)
    left_on = lambda g, p: (g, (p - 1) % pencils)
    down_on = lambda g, p: ((g + 1) % groups, p)
    up_on = lambda g, p: ((g - 1) % groups, p)

    def exchange(across, along):
        return [
            move(across[0], right_on), move(across[1], left_on),
            move(along[0], down_on), move(along[1], up_on),
        ]

    other_core = lambda g, p: (g ^ 1, p)
    other_half = lambda g, p: (g ^ 2, p)
    sign = jnp.where(core == 0, 1.0, -1.0).astype(jnp.float32)
    arrived = move(pressure_source[:, :half] - sign * pressure_source[:, half:], other_core)
    spectral_flops = 6 * depth_loc * width * half * (half + width)
    (held,) = run(
        held_body, scalars, [pressure_source, *into, *span],
        [whole(pressure_source), *into_specs, *span_specs],
        [(depth_loc, width, half)], flops=spectral_flops,
    )
    planes, edges, sent = run(
        arrived_body, scalars,
        [arrived, held, *into, *span, *strip, const["basis_t"], const["far"]],
        [whole(arrived), whole(held), *into_specs, *span_specs, *strip_specs,
         chosen(const["basis_t"], 1), chosen(const["far"], 0)],
        [(own, width, half), (2, depth, half), (2, width, half)],
        scratch=[pltpu.VMEM((2, depth, 8, half), jnp.float32)], flops=spectral_flops,
    )
    sent = move(sent, other_half)

    solid = [solid_temp, phase_map]
    solid_specs = [whole(solid_temp), whole(phase_map)]
    across, along = run(
        edge_body, scalars, [*solid, phase_conductivity], [*solid_specs, smem],
        [(2, 2 * depth, tile_rows), (2, 2 * depth, width)], flops=10**8,
    )
    near = exchange(across, along)
    near_specs = [whole(a) for a in near]
    column_scratch = [pltpu.VMEM((width, tile_rows), jnp.float32)]
    base, across, along = run(
        first_body, scalars, [*solid, gas_wall_temp, phase_conductivity, *near],
        [*solid_specs, whole(gas_wall_temp), smem, *near_specs],
        [(depth, tile_rows, width), (2, depth, tile_rows), (2, depth, width)],
        scratch=column_scratch, flops=10**9,
    )
    near_base = exchange(across, along)
    first_plane = pl.BlockSpec((1, tile_rows, width), lambda i, s: (0, 0, 0))
    base, weights = run(
        second_body, scalars,
        [base, solid_temp, phase_map, gas_wall_temp, phase_conductivity, *near, *near_base],
        [whole(base), first_plane, solid_specs[1], whole(gas_wall_temp), smem, *near_specs,
         *[whole(a) for a in near_base]],
        [(depth, tile_rows, width), (5, tile_rows, width)],
        scratch=column_scratch, flops=10**9,
    )

    log_rho = const["log_rho"][core]
    power = lambda n: jnp.exp(log_rho * n)
    wide = float(width)
    hop = power(wide)
    rho = power(1.0)
    per_rho = power(-1.0)
    right, left = edges[0], edges[1]

    low_sum = jnp.zeros_like(right)
    high_sum = jnp.zeros_like(right)
    right4 = power(wide * (Z_RING - 1 - zi)) * right
    left4 = power(wide * zi) * left
    for d in range(1, Z_RING):
        got = move(edges, lambda g, p, d=d: (g, p // Z_RING * Z_RING + (p + d) % Z_RING))
        source = (zi - d) % Z_RING
        before = zi >= d
        low_sum = low_sum + jnp.where(before, power(wide * (d - 1)), 0.0) * got[0]
        high_sum = high_sum + jnp.where(before, 0.0, power(wide * (Z_RING - 1 - d))) * got[1]
        right4 = right4 + power(wide * (Z_RING - 1 - source)) * got[0]
        left4 = left4 + power(wide * source) * got[1]
    into_low = per_rho * low_sum + left + hop * high_sum
    into_high = per_rho * high_sum + right + hop * low_sum

    first = move(jnp.stack([into_low, into_high, right4, left4]), other_half)
    group4 = jnp.stack([right4, left4])
    other = move(group4, lambda g, p: (g, p ^ Z_RING)) + move(group4, lambda g, p: (g ^ 2, p ^ Z_RING))
    into_low = into_low + first[0]
    into_high = into_high + first[1]
    right4 = right4 + first[2]
    left4 = left4 + first[3]
    after = yl == 1
    low_sum = jnp.where(after, power(wide * zi), 0.0) * other[0]
    high_sum = jnp.where(after, 0.0, power(wide * (Z_RING - 1 - zi))) * other[1]
    run4 = power(wide * Z_RING)
    right8 = jnp.where(after, run4 * other[0] + right4, run4 * right4 + other[0])
    left8 = jnp.where(after, other[1] + run4 * left4, left4 + run4 * other[1])

    packed = jnp.stack([right8, left8])
    block = Z_RING * Y_PAIR
    right_sum = power(wide * block * (X_RING - 1)) * right8
    left_sum = power(wide * block * (X_RING - 1)) * left8
    for d in range(1, X_RING):
        got = move(packed, lambda g, p, d=d: (g, (p + block * d) % pencils))
        right_sum = right_sum + power(wide * block * (d - 1)) * got[0]
        left_sum = left_sum + power(wide * block * (X_RING - 1 - d)) * got[1]
    periodic = 1.0 / (1.0 - power(wide * block * X_RING))
    low_sum = low_sum + power(wide * place) * right_sum * periodic
    high_sum = high_sum + power(wide * (block - 1 - place)) * left_sum * periodic
    gain = rho / (1.0 - rho * rho)
    into_low = gain * (into_low + per_rho * low_sum + hop * high_sum)
    into_high = gain * (into_high + per_rho * high_sum + hop * low_sum)
    gains = jnp.stack([into_low, into_high])

    wall, away, keep = run(
        solve_body, scalars,
        [planes, sent, gains, *span, *back, *strip, const["basis"]],
        [whole(planes), whole(sent), whole(gains), *span_specs, *back_specs, *strip_specs,
         chosen(const["basis"], 1)],
        [(half, 2 * width), (depth_loc, half, width), (depth_loc, width, half)],
        scratch=[
            pltpu.VMEM((own, width, half), jnp.float32),
            pltpu.VMEM((2, depth, half), jnp.float32),
            pltpu.VMEM((2 * width, half), jnp.float32),
        ],
        flops=spectral_flops,
    )
    wall_came = move(wall, other_core)
    came = move(away, other_core)
    (mine,) = run(
        cells_body, scalars, [keep, *span, *back], [whole(keep), *span_specs, *back_specs],
        [(depth_loc, half, width)], flops=spectral_flops,
    )
    (pressure,) = run(
        join_body, scalars, [mine, came], [whole(mine), whole(came)], [pressure_source.shape]
    )
    top_planes = pl.BlockSpec((2, tile_rows, width), lambda i, s: (0, 0, 0))
    (final,) = run(
        wall_body, scalars, [wall, wall_came, weights, base],
        [whole(wall), whole(wall_came), whole(weights), top_planes],
        [solid_temp.shape], out_specs=[top_planes], aliases={4: 0},
    )
    return (pressure, final)


def solution(mesh):
    in_specs = (
        P("grp", None, "pen"),
        P(None, "grp", "pen"),
        P("grp", "pen"),
        P(None, "grp", "pen"),
        P(),
    )
    out_specs = (P("grp", None, "pen"), P(None, "grp", "pen"))
    return jax.shard_map(
        per_device, mesh=mesh, in_specs=in_specs, out_specs=out_specs, check_vma=False
    )
```

```python
import functools
import math

import jax
import jax.numpy as jnp
import numpy as np
from jax import lax
from jax.experimental import pallas as pl
from jax.experimental.pallas import tpu as pltpu
from jax.sharding import PartitionSpec as P

HIGHEST = lax.Precision.HIGHEST
HEAT_TRANSFER = 1.0
PRESSURE_WORK = 0.5
STEP_RATE = 0.12
Z_RING, Y_PAIR, X_RING = 4, 2, 4
VMEM_LIMIT = 48 * 1024 * 1024
LANES = 256
CHUNK = 32


def halves(value):
    high = np.asarray(value, np.float32).astype(jnp.bfloat16)
    low = (np.asarray(value, np.float64) - high.astype(np.float64)).astype(jnp.bfloat16)
    return high, low


def make_tables(span_len, width, depth):
    half = span_len // 2
    waves = np.stack([2 * np.arange(half), 2 * np.arange(half) + 1]).astype(np.float64)
    rows = np.arange(half)
    angle = 2 * np.pi * ((rows[None, :, None] * waves[:, None, :]) % span_len) / span_len
    span = np.cos(angle) + np.sin(angle)
    lam = -4 * np.sin(np.pi * waves / span_len) ** 2
    order = np.concatenate([np.arange(0, width, 2), np.arange(1, width, 2)]) + 1.0
    cells = np.arange(width) + 1.0
    sine = np.sqrt(2 / (width + 1)) * np.sin(np.pi * cells[:, None] * order[None, :] / (width + 1))
    sigma = -4 * np.sin(np.pi * order / (2 * (width + 1))) ** 2
    modes = np.arange(depth)
    theta = np.pi * (2 * modes + 1) / (2 * depth + 1)
    basis = np.cos(theta[None, :] * (np.arange(depth)[:, None] + 0.5)) / np.sqrt((2 * depth + 1) / 4)
    mu = -4 * np.sin(theta / 2) ** 2
    stretch = -(mu[None, :, None] + lam[:, None, :])
    log_rho = -2 * np.arcsinh(np.sqrt(stretch) / 2)
    down = np.arange(depth // 2)
    up = depth - 1 - down
    ordered = np.stack([basis[np.concatenate([down, up])], basis[np.concatenate([up, down])]])
    pair = np.kron(np.eye(2), sine)
    f32 = lambda v: np.asarray(v, np.float32)
    lanes = min(LANES, half)
    return {
        "span": halves(span),
        "into": halves(pair / span_len),
        "back": halves(pair.T),
        "lam": f32(lam)[:, None, :],
        "sigma": f32(np.repeat(sigma[:, None], lanes, 1)),
        "edge": f32(np.repeat(sine[0][:, None], lanes, 1)),
        "basis": f32(ordered),
        "basis_t": f32(np.swapaxes(ordered, 1, 2)),
        "log_rho": f32(log_rho),
        "far": f32(np.exp(log_rho * (width + 1))),
    }


def product(first, second):
    return jnp.dot(first, second, preferred_element_type=jnp.float32)


def split(value):
    high = value.astype(jnp.bfloat16)
    return high, (value - high.astype(jnp.float32)).astype(jnp.bfloat16)


def times(value, high, low):
    value_high, value_low = split(value)
    return product(value_high, high) + (product(value_high, low) + product(value_low, high))


def times_turned(high, low, value):
    value_high, value_low = split(value)
    turned = lambda a, b: lax.dot_general(
        a, b, (((1,), (1,)), ((), ())), preferred_element_type=jnp.float32
    )
    return turned(high, value_high) + (turned(low, value_high) + turned(high, value_low))


def whole(array):
    return pl.BlockSpec(array.shape, lambda i, s: (0,) * len(array.shape))


def chosen(array, place):
    rest = array.shape[1:]
    return pl.BlockSpec((1,) + rest, lambda i, s: (s[place],) + (0,) * len(rest))


def plane_of(array):
    rest = array.shape[1:]
    return pl.BlockSpec((1,) + rest, lambda i, s: (i,) + (0,) * len(rest))


ORDER = pl.BlockSpec(memory_space=pl.ANY)


def run(
    body, scalars, arrays, specs, outs, out_specs=None, scratch=(), aliases=None, flops=0, steps=1
):
    outs = [jax.ShapeDtypeStruct(shape, jnp.float32) for shape in outs]
    moved = sum(math.prod(a.shape) * 4 for a in arrays) + sum(math.prod(o.shape) * 4 for o in outs)
    out_specs = out_specs or [whole(o) for o in outs]
    return pl.pallas_call(
        body,
        out_shape=outs,
        grid_spec=pltpu.PrefetchScalarGridSpec(
            num_scalar_prefetch=1,
            grid=(steps,),
            in_specs=specs,
            out_specs=out_specs,
            scratch_shapes=list(scratch),
        ),
        input_output_aliases=aliases or {},
        compiler_params=pltpu.CompilerParams(vmem_limit_bytes=VMEM_LIMIT),
        cost_estimate=pl.CostEstimate(flops=flops, bytes_accessed=moved, transcendentals=0),
    )(scalars, *arrays)


def fold_body(s_ref, source, away):
    half = source.shape[1] // 2
    sign = (1 - 2 * s_ref[0]).astype(jnp.float32)
    away[...] = source[:, :half] - sign * source[:, half:]


def spectral(planes, into_high, into_low, span_high, span_low):
    turned = []
    for pair in range(0, len(planes), 2):
        cells = jnp.concatenate(planes[pair : pair + 2], axis=1)
        turned.append(times(cells, into_high, into_low).T)
    return times(jnp.concatenate(turned, axis=0), span_high, span_low)


def held_body(s_ref, source, into_high, into_low, span_high, span_low, out):
    count, span_len, _ = source.shape
    half = span_len // 2
    sign = (1 - 2 * s_ref[0]).astype(jnp.float32)
    planes = [source[z, :half] + sign * source[z, half:] for z in range(count)]
    out[...] = spectral(
        planes, into_high[...], into_low[...], span_high[0], span_low[0]
    ).reshape(out.shape)


def continuants(centre, first, count):
    values = [jnp.ones_like(centre), centre + first]
    for _ in range(1, count):
        values.append(centre * values[-1] - values[-2])
    return values


def arrived_body(
    s_ref, arrived, held, into_high, into_low, span_high, span_low, lam, sigma, edge, basis_t, far,
    planes, edges, carried, opening, sums,
):
    count = held.shape[0]
    own = 2 * count
    width, half = held.shape[1:]
    lanes = sigma.shape[1]
    pieces = half // lanes
    planes[:count] = held[...]
    planes[count:] = spectral(
        [arrived[z] for z in range(count)], into_high[...], into_low[...], span_high[0], span_low[0]
    ).reshape(held.shape)
    sums[...] = jnp.zeros_like(sums)
    low = s_ref[1].astype(jnp.float32)
    code = s_ref[2]
    side = width // 16

    def tile(t, nothing):
        group = t // pieces
        rows = pl.ds(pl.multiple_of(group * 8, 8), 8)
        cols = pl.ds(pl.multiple_of(t % pieces * lanes, lanes), lanes)
        parity = group // side
        centre = lam[0, :, cols] + sigma[rows] - 2.0
        mine = continuants(centre, 1.0 - low, own)
        other = continuants(centre, low, own)
        carry = planes[code, rows, cols]
        carries = [carry]
        for i in range(1, own):
            carry = mine[i] * planes[jnp.bitwise_xor(i, code), rows, cols] - carry
            carries.append(carry)
        carried[rows, cols] = carry
        shared = carry / (mine[own] * other[own] - mine[own - 1] * other[own - 1])
        scale = edge[rows]
        value = shared * other[own]
        sums[parity, own - 1, :, cols] += scale * value
        for i in range(own - 2, -1, -1):
            value = (carries[i] - mine[i] * value) / mine[i + 1]
            sums[parity, i, :, cols] += scale * value
        opening[rows, cols] = value + other[own - 1] * shared / mine[own]
        shared = scale * shared
        for i in range(own):
            term = other[i] * shared
            sums[parity, own + i, :, cols] += term if (own - i) % 2 == 0 else -term
        return nothing

    lax.fori_loop(0, (width // 8) * pieces, tile, 0)
    total = jnp.sum(sums[...], axis=2)
    modal = lambda v: jnp.dot(basis_t[0], v, precision=HIGHEST, preferred_element_type=jnp.float32)
    even = modal(total[0])
    odd = modal(total[1])
    edge_low = even + odd
    edge_high = even - odd
    edges[0] = edge_high + far[0] * edge_low
    edges[1] = edge_low + far[0] * edge_high


def powers(log_rho):
    return lambda n: jnp.exp(log_rho[0] * n)


def scalar(value):
    return value.astype(jnp.float32)


def z_body(s_ref, wall_there, after, edges, got1, got2, got3, log_rho, four, two, *, width):
    power = powers(log_rho)
    zi = s_ref[5]
    wide = float(width)
    right, left = edges[0], edges[1]
    low_sum = jnp.zeros_like(right)
    high_sum = jnp.zeros_like(right)
    right4 = power(wide * scalar(Z_RING - 1 - zi)) * right
    left4 = power(wide * scalar(zi)) * left
    for d, got in ((1, got1), (2, got2), (3, got3)):
        before = scalar(zi >= d)
        source = jnp.where(zi >= d, zi - d, zi - d + Z_RING)
        low_sum = low_sum + before * power(wide * (d - 1)) * got[0]
        high_sum = high_sum + (1.0 - before) * power(wide * (Z_RING - 1 - d)) * got[1]
        right4 = right4 + power(wide * scalar(Z_RING - 1 - source)) * got[0]
        left4 = left4 + power(wide * scalar(source)) * got[1]
    hop = power(wide)
    per_rho = power(-1.0)
    four[0] = per_rho * low_sum + left + hop * high_sum
    four[1] = per_rho * high_sum + right + hop * low_sum
    four[2] = right4
    four[3] = left4
    two[0] = right4
    two[1] = left4


def y_body(s_ref, after, four, there, beside1, beside2, log_rho, run8, part, *, width):
    power = powers(log_rho)
    zi = s_ref[5]
    wide = float(width)
    behind = scalar(s_ref[6])
    other0 = beside1[0] + beside2[0]
    other1 = beside1[1] + beside2[1]
    right4 = four[2] + there[2]
    left4 = four[3] + there[3]
    low_sum = behind * power(wide * scalar(zi)) * other0
    high_sum = (1.0 - behind) * power(wide * scalar(Z_RING - 1 - zi)) * other1
    run4 = power(wide * Z_RING)
    is_behind = s_ref[6] == 1
    run8[0] = jnp.where(is_behind, run4 * other0 + right4, run4 * right4 + other0)
    run8[1] = jnp.where(is_behind, other1 + run4 * left4, left4 + run4 * other1)
    hop = power(wide)
    per_rho = power(-1.0)
    part[0] = four[0] + there[0] + per_rho * low_sum + hop * high_sum
    part[1] = four[1] + there[1] + per_rho * high_sum + hop * low_sum


def x_sums(s_ref, run8, part, gots, log_rho, width):
    power = powers(log_rho)
    wide = float(width)
    block = Z_RING * Y_PAIR
    right_sum = power(wide * block * (X_RING - 1)) * run8[0]
    left_sum = power(wide * block * (X_RING - 1)) * run8[1]
    for d, got in enumerate(gots, 1):
        right_sum = right_sum + power(wide * block * (d - 1)) * got[0]
        left_sum = left_sum + power(wide * block * (X_RING - 1 - d)) * got[1]
    periodic = 1.0 / (1.0 - power(wide * block * X_RING))
    low_sum = power(wide * scalar(s_ref[7])) * right_sum * periodic
    high_sum = power(wide * scalar(block - 1 - s_ref[7])) * left_sum * periodic
    rho = power(1.0)
    per_rho = power(-1.0)
    hop = power(wide)
    gain = rho / (1.0 - rho * rho)
    into_low = gain * (part[0] + per_rho * low_sum + hop * high_sum)
    into_high = gain * (part[1] + per_rho * high_sum + hop * low_sum)
    return into_low, into_high


def solve_body(
    s_ref, after, planes, carried, first_there, run8, part, got1, got2, got3, log_rho,
    span_high, span_low, back_high, back_low, lam, sigma, edge, basis,
    wall, away, keep, solved, both, first,
):
    own, width, half = planes.shape
    count = own // 2
    lanes = sigma.shape[1]
    pieces = half // lanes
    low = s_ref[1].astype(jnp.float32)
    is_low = s_ref[1] == 1
    code = s_ref[2]
    depthwise = lambda v: jnp.dot(basis[0], v, precision=HIGHEST, preferred_element_type=jnp.float32)
    into_low, into_high = x_sums(s_ref, run8, part, (got1, got2, got3), log_rho, width)
    gain_low = depthwise(into_low)
    gain_high = depthwise(into_high)
    both[0] = gain_low + gain_high
    both[1] = gain_low - gain_high
    first[...] = jnp.zeros_like(first)
    first[width : width + 1] = jnp.where(is_low, gain_low[own : own + 1], gain_low[:1])
    first[width + 1 : width + 2] = jnp.where(is_low, gain_high[own : own + 1], gain_high[:1])
    side = width // 16

    def tile(t, nothing):
        group = t // pieces
        rows = pl.ds(pl.multiple_of(group * 8, 8), 8)
        cols = pl.ds(pl.multiple_of(t % pieces * lanes, lanes), lanes)
        parity = group // side
        centre = lam[0, :, cols] + sigma[rows] - 2.0
        mine = continuants(centre, 1.0 - low, own)
        other = continuants(centre, low, own)
        scale = edge[rows]
        rhs = lambda i: scale * both[parity, i : i + 1, cols]
        carry = planes[code, rows, cols] - rhs(0)
        carries = [carry]
        for i in range(1, own):
            carry = mine[i] * (planes[jnp.bitwise_xor(i, code), rows, cols] - rhs(i)) - carry
            carries.append(carry)
        right = rhs(own)
        there = -right
        direct = -mine[own - 1] * right
        for i in range(1, own):
            right = rhs(own + i)
            there = -other[i] * right - there
            term = mine[own - 1 - i] * right
            direct = direct - term if i % 2 == 0 else direct + term
        there = there + carried[rows, cols]
        value = (carry * other[own] - mine[own - 1] * there) / (
            mine[own] * other[own] - mine[own - 1] * other[own - 1]
        )
        far_first = first_there[rows, cols] + (direct + value) / other[own]
        solved[jnp.bitwise_xor(own - 1, code), rows, cols] = value
        for i in range(own - 2, -1, -1):
            value = (carries[i] - mine[i] * value) / mine[i + 1]
            solved[jnp.bitwise_xor(i, code), rows, cols] = value
        first[rows, cols] = jnp.where(is_low, far_first, value)
        return nothing

    lax.fori_loop(0, (width // 8) * pieces, tile, 0)
    table_high = span_high[0]
    table_low = span_low[0]
    line = times_turned(table_high, table_low, first[...])
    main = times(line[:, :width], back_high[:width, :width], back_low[:width, :width])
    wall[...] = jnp.concatenate([main, line[:, width:]], axis=1)
    for pair in range(0, count, 2):
        values = solved[count + pair : count + pair + 2].reshape(2 * width, half)
        cells = times(times_turned(table_high, table_low, values), back_high[...], back_low[...])
        away[pair] = cells[:, :width]
        away[pair + 1] = cells[:, width:]
    keep[...] = solved[:count]


def cells_body(s_ref, keep, span_high, span_low, back_high, back_low, mine):
    count, width, half = keep.shape
    for pair in range(0, count, 2):
        values = keep[pair : pair + 2].reshape(2 * width, half)
        cells = times(times_turned(span_high[0], span_low[0], values), back_high[...], back_low[...])
        mine[pair] = cells[:, :width]
        mine[pair + 1] = cells[:, width:]


def join_body(s_ref, mine, came, out):
    half = mine.shape[1]
    sign = (1 - 2 * s_ref[0]).astype(jnp.float32)
    ours = mine[...]
    theirs = came[...]
    out[:, :half] = ours + theirs
    out[:, half:] = sign * (ours - theirs)


def edge_body(s_ref, after, temp, phase, conductivity, cond, across, along, packed):
    depth, rows, width = temp.shape
    lane = lax.broadcasted_iota(jnp.int32, (CHUNK, width), 1)
    cold, warm = conductivity[0], conductivity[1]
    packed[...] = jnp.zeros_like(packed)

    def plane(z, nothing):
        for start in range(0, rows, CHUNK):
            at = slice(start, start + CHUNK)
            kept = packed[at]
            value = jnp.where(phase[z, at] == 1, warm, cold)
            cond[z, at] = value
            for k, part in enumerate((temp[z, at], value)):
                spot = 2 * (k * depth + z)
                chosen_lane = (lane == spot) | (lane == spot + 1)
                kept = jnp.where(chosen_lane, pltpu.roll(part, spot + 1, 1), kept)
                if start == 0:
                    along[1, pl.ds(k * depth + z, 1)] = part[:1]
                if start + CHUNK == rows:
                    along[0, pl.ds(k * depth + z, 1)] = part[CHUNK - 1 :]
            packed[at] = kept
        return nothing

    lax.fori_loop(0, depth, plane, 0)
    across[...] = packed[...].T[: 4 * depth]


def beside(ours, from_left, from_right):
    row = lax.broadcasted_iota(jnp.int32, ours.shape, 0)
    count = ours.shape[0]
    return jnp.where(
        row % 2 == 1, pltpu.roll(from_left, 1, 0), pltpu.roll(from_right, count - 1, 0)
    )


def to_columns(packed, values):
    count = values.shape[0]
    packed[:count] = values
    return packed[...].T


def step_planes(temp, cond, up, down, cond_up, cond_down, inflow, emit):
    depth, rows, width = temp.shape
    lane = lax.broadcasted_iota(jnp.int32, (CHUNK, width), 1)
    end = width - 1

    def shifted(ref, z, start, above, below):
        if start == 0:
            upper = jnp.concatenate([above[pl.ds(z, 1)], ref[z, : CHUNK - 1]], axis=0)
        else:
            upper = ref[z, start - 1 : start + CHUNK - 1]
        if start + CHUNK == rows:
            lower = jnp.concatenate([ref[z, start + 1 :], below[pl.ds(z, 1)]], axis=0)
        else:
            lower = ref[z, start + 1 : start + CHUNK + 1]
        return upper, lower

    def plane(z, first):
        before = jnp.maximum(z - 1, 0)
        after = jnp.minimum(z + 1, depth - 1)
        for start in range(0, rows, CHUNK):
            at = slice(start, start + CHUNK)
            here = temp[z, at]
            own = cond[z, at]
            pairs = []
            total = None
            sides = list(zip(shifted(temp, z, start, up, down), shifted(cond, z, start, cond_up, cond_down)))
            sides += [(temp[before, at], cond[before, at]), (temp[after, at], cond[after, at])]
            for side_temp, side_cond in sides:
                pair = own + side_cond
                pairs.append(pair)
                term = pair * (side_temp - here)
                total = term if total is None else total + term
            pair = own + pltpu.roll(own, end, 1)
            pairs.append(pair)
            flow = jnp.where(lane == end, 0.0, pair * (pltpu.roll(here, end, 1) - here))
            total = total + (flow - pltpu.roll(flow, 1, 1))
            spot = width - (2 * z + 1)
            entering = pltpu.roll(inflow[at], spot, 1)
            total = total + jnp.where((lane == 0) | (lane == end), entering, 0.0)
            emit(z, start, first, here + (0.5 * STEP_RATE) * total, pairs)

    plane(0, True)

    def later(z, nothing):
        plane(z, False)
        return nothing

    lax.fori_loop(1, depth, later, 0)


def first_body(
    s_ref, after, temp, cond, gas, packs, from_left, from_right, from_up, from_down,
    out, across, along, packed, inflow, turned,
):
    depth, rows, width = temp.shape
    lane = lax.broadcasted_iota(jnp.int32, (CHUNK, width), 1)
    packed[...] = jnp.zeros_like(packed)
    halo = beside(packs[...], from_left[...], from_right[...])
    ours = packs[...]
    half = 2 * depth
    flow = (ours[half:] + halo[half:]) * (halo[:half] - ours[:half])
    inflow[...] = to_columns(packed, flow)

    def emit(z, start, first, value, pairs):
        at = slice(start, start + CHUNK)
        if first:
            value = value + (STEP_RATE * HEAT_TRANSFER) * (gas[at] - temp[0, at])
        out[z, at] = value
        spot = 2 * z
        kept = jnp.where((lane == spot) | (lane == spot + 1), pltpu.roll(value, spot + 1, 1), turned[at])
        turned[at] = kept
        if start == 0:
            along[1, pl.ds(z, 1)] = value[:1]
        if start + CHUNK == rows:
            along[0, pl.ds(z, 1)] = value[CHUNK - 1 :]

    turned[...] = jnp.zeros_like(turned)
    step_planes(
        temp, cond, from_up.at[:depth], from_down.at[:depth], from_up.at[depth:], from_down.at[depth:],
        inflow, emit,
    )
    across[...] = turned[...].T[:half]


def second_body(
    s_ref, after, base, cond, temp, gas, packs, from_left, from_right, from_up, from_down,
    base_packs, base_left, base_right, base_up, base_down, out, weights, packed, inflow, face,
):
    depth, rows, width = base.shape
    lane = lax.broadcasted_iota(jnp.int32, (CHUNK, width), 1)
    end = width - 1
    packed[...] = jnp.zeros_like(packed)
    half = 2 * depth
    pair = packs[half:] + beside(packs[half:], from_left[half:], from_right[half:])
    ours = base_packs[...]
    halo = beside(ours, base_left[...], base_right[...])
    inflow[...] = to_columns(packed, pair * (halo - ours))
    face[...] = to_columns(packed, pair)

    def emit(z, start, first, value, pairs):
        at = slice(start, start + CHUNK)
        if first:
            value = value + (STEP_RATE * HEAT_TRANSFER) * (gas[at] - temp[0, at])
            edge = pltpu.roll(face[at], end, 1)
            across = pairs[4]
            left = jnp.where(lane == 0, edge, pltpu.roll(across, 1, 1))
            right = jnp.where(lane == end, edge, across)
            for k, pair in enumerate((pairs[0], pairs[1], left, right, pairs[3])):
                weights[k, at] = (0.5 * STEP_RATE) * pair
        out[z, at] = value

    step_planes(
        base, cond, base_up, base_down, from_up.at[depth:], from_down.at[depth:], inflow, emit
    )


def faces(value, row, lane, up, down, left, right):
    rows, width = value.shape
    return (
        jnp.where(row == 0, up, pltpu.roll(value, 1, 0)),
        jnp.where(row == rows - 1, down, pltpu.roll(value, rows - 1, 0)),
        jnp.where(lane == 0, left, pltpu.roll(value, 1, 1)),
        jnp.where(lane == width - 1, right, pltpu.roll(value, width - 1, 1)),
    )


def wall_body(s_ref, ours, theirs, weights, base, out):
    half = ours.shape[0]
    rows, width = weights.shape[1:]
    sign = (1 - 2 * s_ref[0]).astype(jnp.float32)
    bottom = (1 - 2 * s_ref[3]).astype(jnp.float32)
    second = s_ref[4] == 1
    factor = STEP_RATE * HEAT_TRANSFER * PRESSURE_WORK

    def lines(start, count, minus):
        our_sign = jnp.where(s_ref[0] == 0, 1.0, minus) * factor
        their_sign = jnp.where(s_ref[0] == 0, minus, 1.0) * factor
        at = pl.ds(start, count)
        return our_sign * ours[at] + their_sign * theirs[at]

    begin = pl.multiple_of(s_ref[4] * rows, rows)
    middle = lines(begin, rows, bottom)
    above = lines(jnp.where(second, rows - 1, half - 1), 1, jnp.where(second, bottom, -bottom))
    below = lines(jnp.where(second, 0, rows), 1, jnp.where(second, -bottom, bottom))
    share = middle[:, :width]
    row = lax.broadcasted_iota(jnp.int32, (rows, width), 0)
    lane = lax.broadcasted_iota(jnp.int32, (rows, width), 1)
    around = faces(
        share, row, lane, above[:, :width], below[:, :width],
        middle[:, width : width + 1], middle[:, width + 1 : width + 2],
    )
    added = 2.0 * share
    for k in range(4):
        added = added + weights[k] * (around[k] - share)
    down = weights[4] * share
    out[0] = base[0] + added - down
    out[1] = base[1] + down


def mover(groups, pencils):
    def move(value, target):
        pairs = []
        for g in range(groups):
            for p in range(pencils):
                to = target(g, p)
                pairs.append((g * pencils + p, to[0] * pencils + to[1]))
        return lax.ppermute(value, ("grp", "pen"), pairs)

    return move


def per_device(pressure_source, solid_temp, gas_wall_temp, phase_map, phase_conductivity):
    groups = lax.axis_size("grp")
    pencils = lax.axis_size("pen")
    group_idx = lax.axis_index("grp")
    pencil_idx = lax.axis_index("pen")
    depth_loc, span_len, width = pressure_source.shape
    depth = depth_loc * groups
    half = span_len // 2
    own = depth // 2
    core = group_idx % 2
    low = group_idx // 2
    zi = pencil_idx % Z_RING
    yl = pencil_idx // Z_RING % Y_PAIR
    place = pencil_idx % (Z_RING * Y_PAIR)
    move = mover(groups, pencils)
    tab = make_tables(span_len, width, depth)
    const = {k: tuple(map(jnp.asarray, v)) if isinstance(v, tuple) else jnp.asarray(v) for k, v in tab.items()}
    code = jnp.where(low == 0, core * 4, 7 - 4 * core)
    scalars = jnp.stack([core, low, code, low, core, zi, yl, place]).astype(jnp.int32)
    span = list(const["span"])
    into = list(const["into"])
    back = list(const["back"])
    span_specs = [chosen(a, 0) for a in span]
    into_specs = [whole(a) for a in into]
    back_specs = [whole(a) for a in back]
    strip = [const["lam"], const["sigma"], const["edge"]]
    strip_specs = [chosen(strip[0], 0), whole(strip[1]), whole(strip[2])]
    smem = pl.BlockSpec(memory_space=pltpu.SMEM)

    tile_rows = span_len // groups
    right_on = lambda g, p: (g, (p + 1) % pencils)
    left_on = lambda g, p: (g, (p - 1) % pencils)
    down_on = lambda g, p: ((g + 1) % groups, p)
    up_on = lambda g, p: ((g - 1) % groups, p)

    def exchange(across, along):
        return [
            move(across, right_on), move(across, left_on),
            move(along[0], down_on), move(along[1], up_on),
        ]

    other_core = lambda g, p: (g ^ 1, p)
    other_half = lambda g, p: (g ^ 2, p)
    folded_shape = (depth_loc, half, width)
    folded = jax.ShapeDtypeStruct(folded_shape, jnp.float32)
    (sent,) = run(
        fold_body, scalars, [pressure_source], [plane_of(pressure_source)], [folded_shape],
        out_specs=[plane_of(folded)], steps=depth_loc,
    )
    arrived = move(sent, other_core)
    spectral_flops = 6 * depth_loc * width * half * (half + width)
    (held,) = run(
        held_body, scalars, [pressure_source, *into, *span],
        [whole(pressure_source), *into_specs, *span_specs],
        [(depth_loc, width, half)], flops=spectral_flops,
    )
    planes, edges, carried, opening = run(
        arrived_body, scalars,
        [arrived, held, *into, *span, *strip, const["basis_t"], const["far"]],
        [whole(arrived), whole(held), *into_specs, *span_specs, *strip_specs,
         chosen(const["basis_t"], 1), chosen(const["far"], 0)],
        [(own, width, half), (2, depth, half), (width, half), (width, half)],
        scratch=[pltpu.VMEM((2, depth, 8, half), jnp.float32)], flops=spectral_flops,
    )
    carried_there = move(carried, other_half)
    opening_there = move(opening, other_half)
    z_got = [
        move(edges, lambda g, p, d=d: (g, p // Z_RING * Z_RING + (p + d) % Z_RING))
        for d in range(1, Z_RING)
    ]

    column_scratch = pltpu.VMEM((tile_rows, width), jnp.float32)
    row_scratch = pltpu.VMEM((width, tile_rows), jnp.float32)
    cond, packs, along = run(
        edge_body, scalars, [edges, solid_temp, phase_map, phase_conductivity],
        [ORDER, whole(solid_temp), whole(phase_map), smem],
        [(depth, tile_rows, width), (4 * depth, tile_rows), (2, 2 * depth, width)],
        scratch=[column_scratch], flops=10**9,
    )
    near = exchange(packs, along)
    near_specs = [whole(a) for a in near]

    log_rho = const["log_rho"]
    log_spec = chosen(log_rho, 0)
    pair_shape = edges.shape
    four, two = run(
        functools.partial(z_body, width=width), scalars,
        [carried_there, along, edges, *z_got, log_rho],
        [ORDER, ORDER, whole(edges), *[whole(a) for a in z_got], log_spec],
        [(4,) + pair_shape[1:], pair_shape],
    )
    there = move(four, other_half)
    beside1 = move(two, lambda g, p: (g, p ^ Z_RING))
    beside2 = move(two, lambda g, p: (g ^ 2, p ^ Z_RING))

    base, base_packs, base_along = run(
        first_body, scalars, [two, solid_temp, cond, gas_wall_temp, packs, *near],
        [ORDER, whole(solid_temp), whole(cond), whole(gas_wall_temp), whole(packs), *near_specs],
        [(depth, tile_rows, width), (2 * depth, tile_rows), (2, depth, width)],
        scratch=[row_scratch, column_scratch, column_scratch], flops=3 * 10**9,
    )
    near_base = exchange(base_packs, base_along)
    run8, part = run(
        functools.partial(y_body, width=width), scalars,
        [base_along, four, there, beside1, beside2, log_rho],
        [ORDER, whole(four), whole(there), whole(beside1), whole(beside2), log_spec],
        [pair_shape, pair_shape],
    )
    block = Z_RING * Y_PAIR
    x_got = [move(run8, lambda g, p, d=d: (g, (p + block * d) % pencils)) for d in range(1, X_RING)]
    first_plane = pl.BlockSpec((1, tile_rows, width), lambda i, s: (0, 0, 0))
    base, weights = run(
        second_body, scalars,
        [run8, base, cond, solid_temp, gas_wall_temp, packs, *near, base_packs, *near_base],
        [ORDER, whole(base), whole(cond), first_plane, whole(gas_wall_temp), whole(packs), *near_specs,
         whole(base_packs), *[whole(a) for a in near_base]],
        [(depth, tile_rows, width), (5, tile_rows, width)],
        scratch=[row_scratch, column_scratch, column_scratch], flops=3 * 10**9,
    )

    wall, away, keep = run(
        solve_body, scalars,
        [weights, planes, carried_there, opening_there, run8, part, *x_got, log_rho, *span, *back,
         *strip, const["basis"]],
        [ORDER, whole(planes), whole(carried_there), whole(opening_there), whole(run8), whole(part),
         *[whole(a) for a in x_got], log_spec, *span_specs, *back_specs, *strip_specs,
         chosen(const["basis"], 1)],
        [(half, 2 * width), (depth_loc, half, width), (depth_loc, width, half)],
        scratch=[
            pltpu.VMEM((own, width, half), jnp.float32),
            pltpu.VMEM((2, depth, half), jnp.float32),
            pltpu.VMEM((2 * width, half), jnp.float32),
        ],
        flops=spectral_flops,
    )
    wall_came = move(wall, other_core)
    came = move(away, other_core)
    (mine,) = run(
        cells_body, scalars, [keep, *span, *back], [whole(keep), *span_specs, *back_specs],
        [(depth_loc, half, width)], flops=spectral_flops,
    )
    (pressure,) = run(
        join_body, scalars, [mine, came], [plane_of(mine), plane_of(came)], [pressure_source.shape],
        out_specs=[plane_of(pressure_source)], steps=depth_loc,
    )
    top_planes = pl.BlockSpec((2, tile_rows, width), lambda i, s: (0, 0, 0))
    (final,) = run(
        wall_body, scalars, [wall, wall_came, weights, base],
        [whole(wall), whole(wall_came), whole(weights), top_planes],
        [solid_temp.shape], out_specs=[top_planes], aliases={4: 0},
    )
    return (pressure, final)


def solution(mesh):
    in_specs = (
        P("grp", None, "pen"),
        P(None, "grp", "pen"),
        P("grp", "pen"),
        P(None, "grp", "pen"),
        P(),
    )
    out_specs = (P("grp", None, "pen"), P(None, "grp", "pen"))
    return jax.shard_map(
        per_device, mesh=mesh, in_specs=in_specs, out_specs=out_specs, check_vma=False
    )
```

```python
import functools
import math

import jax
import jax.numpy as jnp
import numpy as np
from jax import lax
from jax.experimental import pallas as pl
from jax.experimental.pallas import tpu as pltpu
from jax.sharding import PartitionSpec as P

HIGHEST = lax.Precision.HIGHEST
HEAT_TRANSFER = 1.0
PRESSURE_WORK = 0.5
STEP_RATE = 0.12
Z_RING, Y_PAIR, X_RING = 4, 2, 4
VMEM_LIMIT = 18 * 1024 * 1024
BLOCK_LIMIT = 16 * 1024 * 1024
LANES = 512
CHUNK = 32
COST_SCALE = 0.1


def halves(value):
    high = np.asarray(value, np.float32).astype(jnp.bfloat16)
    low = (np.asarray(value, np.float64) - high.astype(np.float64)).astype(jnp.bfloat16)
    return high, low


def make_tables(span_len, width, depth):
    half = span_len // 2
    waves = np.stack([2 * np.arange(half), 2 * np.arange(half) + 1]).astype(np.float64)
    rows = np.arange(half)
    angle = 2 * np.pi * ((rows[None, :, None] * waves[:, None, :]) % span_len) / span_len
    span = np.cos(angle) + np.sin(angle)
    lam = -4 * np.sin(np.pi * waves / span_len) ** 2
    order = np.concatenate([np.arange(0, width, 2), np.arange(1, width, 2)]) + 1.0
    cells = np.arange(width) + 1.0
    sine = np.sqrt(2 / (width + 1)) * np.sin(np.pi * cells[:, None] * order[None, :] / (width + 1))
    sigma = -4 * np.sin(np.pi * order / (2 * (width + 1))) ** 2
    modes = np.arange(depth)
    theta = np.pi * (2 * modes + 1) / (2 * depth + 1)
    basis = np.cos(theta[None, :] * (np.arange(depth)[:, None] + 0.5)) / np.sqrt((2 * depth + 1) / 4)
    mu = -4 * np.sin(theta / 2) ** 2
    stretch = -(mu[None, :, None] + lam[:, None, :])
    log_rho = -2 * np.arcsinh(np.sqrt(stretch) / 2)
    down = np.arange(depth // 2)
    up = depth - 1 - down
    ordered = np.stack([basis[np.concatenate([down, up])], basis[np.concatenate([up, down])]])
    pair = np.kron(np.eye(2), sine)
    f32 = lambda v: np.asarray(v, np.float32)
    lanes = min(LANES, half)
    return {
        "span": halves(span),
        "span_t": halves(np.swapaxes(span, 1, 2)),
        "into": halves(pair / span_len),
        "back": halves(pair.T),
        "lam": f32(lam)[:, None, :],
        "sigma": f32(np.repeat(sigma[:, None], lanes, 1)),
        "edge": f32(np.repeat(sine[0][:, None], lanes, 1)),
        "basis": f32(ordered),
        "basis_t": f32(np.swapaxes(ordered, 1, 2)),
        "log_rho": f32(log_rho),
        "far": f32(np.exp(log_rho * (width + 1))),
    }


def product(first, second):
    return jnp.dot(first, second, preferred_element_type=jnp.float32)


def split(value):
    high = value.astype(jnp.bfloat16)
    return high, (value - high.astype(jnp.float32)).astype(jnp.bfloat16)


def times(value, high, low):
    value_high, value_low = split(value)
    return product(value_high, high) + (product(value_high, low) + product(value_low, high))


def times_turned(high, low, value):
    value_high, value_low = split(value)
    turned = lambda a, b: lax.dot_general(
        a, b, (((1,), (1,)), ((), ())), preferred_element_type=jnp.float32
    )
    return turned(high, value_high) + (turned(low, value_high) + turned(high, value_low))


ORDER = pl.BlockSpec(memory_space=pl.ANY)
SCALARS = pl.BlockSpec(memory_space=pltpu.SMEM)
FAST = pl.BlockSpec(memory_space=pltpu.VMEM)


def plane_of(array):
    rest = array.shape[1:]
    return pl.BlockSpec((1,) + rest, lambda i, s: (i,) + (0,) * len(rest))


def cost(time_us):
    return pl.CostEstimate(flops=1, bytes_accessed=int(time_us * 3.69e6 * COST_SCALE), transcendentals=0)


def run(body, time_us, scalars, ordered, arrays, outs, scratch=(), small=(), out_specs=None, aliases=None):
    outs = [jax.ShapeDtypeStruct(shape, jnp.float32) for shape in outs]
    skip = len(ordered)
    count = len(small)
    kinds = [FAST if spec is None else spec for spec in (a[1] if type(a) is tuple else None for a in arrays)]
    arrays = [a[0] if type(a) is tuple else a for a in arrays]
    specs = [SCALARS] + [SCALARS] * count + [ORDER] * skip + kinds

    def inner(s_ref, *refs):
        body(s_ref, *refs[:count], *refs[count + skip :])

    return pl.pallas_call(
        inner,
        out_shape=outs,
        in_specs=specs,
        out_specs=out_specs or [FAST] * len(outs),
        scratch_shapes=list(scratch),
        input_output_aliases=aliases or {},
        compiler_params=pltpu.CompilerParams(vmem_limit_bytes=VMEM_LIMIT),
        cost_estimate=cost(time_us),
    )(scalars, *small, *ordered, *arrays)


def run_blocks(body, time_us, scalars, arrays, specs, outs, out_specs, steps):
    return pl.pallas_call(
        body,
        out_shape=[jax.ShapeDtypeStruct(out, jnp.float32) for out in outs],
        grid_spec=pltpu.PrefetchScalarGridSpec(
            num_scalar_prefetch=1, grid=(steps,), in_specs=specs, out_specs=out_specs
        ),
        compiler_params=pltpu.CompilerParams(vmem_limit_bytes=BLOCK_LIMIT),
        cost_estimate=cost(time_us),
    )(scalars, *arrays)


def fold_body(s_ref, after, source, away, kept):
    half = source.shape[1] // 2
    sign = (1 - 2 * s_ref[0]).astype(jnp.float32)
    upper = source[:, :half]
    lower = sign * source[:, half:]
    away[...] = upper - lower
    kept[...] = upper + lower


def spectral(planes, into_high, into_low, span_high, span_low):
    turned = []
    for pair in range(0, len(planes), 2):
        cells = jnp.concatenate(planes[pair : pair + 2], axis=1)
        turned.append(times(cells, into_high, into_low).T)
    return times(jnp.concatenate(turned, axis=0), span_high, span_low)


def held_body(s_ref, kept, into_high, into_low, span_high, span_low, out):
    out[...] = spectral(
        [kept[z] for z in range(kept.shape[0])], into_high[...], into_low[...],
        span_high[s_ref[0]], span_low[s_ref[0]],
    ).reshape(out.shape)


def continuants(centre, first, count):
    values = [jnp.ones_like(centre), centre + first]
    for _ in range(1, count):
        values.append(centre * values[-1] - values[-2])
    return values


def pivot_body(s_ref, lam, sigma, out):
    own = (out.shape[0] - 2) // 3
    width = out.shape[1]
    low = s_ref[1].astype(jnp.float32)

    def tile(group, nothing):
        rows = pl.ds(pl.multiple_of(group * 8, 8), 8)
        centre = lam[s_ref[0]] + sigma[rows] - 2.0
        mine = continuants(centre, 1.0 - low, own)
        other = continuants(centre, low, own)
        for i in range(own):
            out[i, rows] = mine[i + 1]
            out[own + i, rows] = other[i + 1]
            out[2 * own + i, rows] = 1.0 / mine[i + 1]
        out[3 * own, rows] = 1.0 / (mine[own] * other[own] - mine[own - 1] * other[own - 1])
        out[3 * own + 1, rows] = 1.0 / other[own]
        return nothing

    lax.fori_loop(0, width // 8, tile, 0)


def arrived_body(
    s_ref, arrived, held, into_high, into_low, span_high, span_low, pivots, edge, basis_t, far,
    planes, edges, carried, opening, sums,
):
    count = held.shape[0]
    own = 2 * count
    width, half = held.shape[1:]
    planes[:count] = held[...]
    planes[count:] = spectral(
        [arrived[z] for z in range(count)], into_high[...], into_low[...],
        span_high[s_ref[0]], span_low[s_ref[0]],
    ).reshape(held.shape)
    sums[...] = jnp.zeros_like(sums)
    code = s_ref[2]
    side = width // 16

    def tile(group, nothing):
        rows = pl.ds(pl.multiple_of(group * 8, 8), 8)
        parity = group // side
        carry = planes[code, rows]
        carries = [carry]
        for i in range(1, own):
            carry = pivots[i - 1, rows] * planes[jnp.bitwise_xor(i, code), rows] - carry
            carries.append(carry)
        carried[rows] = carry
        shared = carry * pivots[3 * own, rows]
        scale = edge[rows]
        value = shared * pivots[2 * own - 1, rows]
        sums[parity, own - 1] += scale * value
        for i in range(own - 2, -1, -1):
            step = value if i == 0 else pivots[i - 1, rows] * value
            value = (carries[i] - step) * pivots[2 * own + i, rows]
            sums[parity, i] += scale * value
        opening[rows] = value + pivots[2 * own - 2, rows] * shared * pivots[3 * own - 1, rows]
        shared = scale * shared
        for i in range(own):
            term = shared if i == 0 else pivots[own + i - 1, rows] * shared
            sums[parity, own + i] += term if (own - i) % 2 == 0 else -term
        return nothing

    lax.fori_loop(0, width // 8, tile, 0)
    total = jnp.sum(sums[...], axis=2)
    modal = lambda v: jnp.dot(
        basis_t[s_ref[1]], v, precision=HIGHEST, preferred_element_type=jnp.float32
    )
    even = modal(total[0])
    odd = modal(total[1])
    edge_low = even + odd
    edge_high = even - odd
    edges[0] = edge_high + far[s_ref[0]] * edge_low
    edges[1] = edge_low + far[s_ref[0]] * edge_high


def powers(s_ref, log_rho):
    rate = log_rho[s_ref[0]]
    return lambda n: jnp.exp(rate * n)


def scalar(value):
    return value.astype(jnp.float32)


def z_body(s_ref, edges, got1, got2, got3, log_rho, carried, four, two, passed, *, width):
    passed[...] = carried[...]
    power = powers(s_ref, log_rho)
    zi = s_ref[5]
    wide = float(width)
    right, left = edges[0], edges[1]
    low_sum = jnp.zeros_like(right)
    high_sum = jnp.zeros_like(right)
    right4 = power(wide * scalar(Z_RING - 1 - zi)) * right
    left4 = power(wide * scalar(zi)) * left
    for d, got in ((1, got1), (2, got2), (3, got3)):
        before = scalar(zi >= d)
        source = jnp.where(zi >= d, zi - d, zi - d + Z_RING)
        low_sum = low_sum + before * power(wide * (d - 1)) * got[0]
        high_sum = high_sum + (1.0 - before) * power(wide * (Z_RING - 1 - d)) * got[1]
        right4 = right4 + power(wide * scalar(Z_RING - 1 - source)) * got[0]
        left4 = left4 + power(wide * scalar(source)) * got[1]
    hop = power(wide)
    per_rho = power(-1.0)
    four[0] = per_rho * low_sum + left + hop * high_sum
    four[1] = per_rho * high_sum + right + hop * low_sum
    four[2] = right4
    four[3] = left4
    two[0] = right4
    two[1] = left4


def y_body(s_ref, four, there, beside1, beside2, log_rho, opening, run8, part, passed, *, width):
    passed[...] = opening[...]
    power = powers(s_ref, log_rho)
    zi = s_ref[5]
    wide = float(width)
    behind = scalar(s_ref[6])
    other0 = beside1[0] + beside2[0]
    other1 = beside1[1] + beside2[1]
    right4 = four[2] + there[2]
    left4 = four[3] + there[3]
    low_sum = behind * power(wide * scalar(zi)) * other0
    high_sum = (1.0 - behind) * power(wide * scalar(Z_RING - 1 - zi)) * other1
    run4 = power(wide * Z_RING)
    is_behind = s_ref[6] == 1
    run8[0] = jnp.where(is_behind, run4 * other0 + right4, run4 * right4 + other0)
    run8[1] = jnp.where(is_behind, other1 + run4 * left4, left4 + run4 * other1)
    hop = power(wide)
    per_rho = power(-1.0)
    part[0] = four[0] + there[0] + per_rho * low_sum + hop * high_sum
    part[1] = four[1] + there[1] + per_rho * high_sum + hop * low_sum


def x_sums(s_ref, run8, part, gots, log_rho, width):
    power = powers(s_ref, log_rho)
    wide = float(width)
    block = Z_RING * Y_PAIR
    right_sum = power(wide * block * (X_RING - 1)) * run8[0]
    left_sum = power(wide * block * (X_RING - 1)) * run8[1]
    for d, got in enumerate(gots, 1):
        right_sum = right_sum + power(wide * block * (d - 1)) * got[0]
        left_sum = left_sum + power(wide * block * (X_RING - 1 - d)) * got[1]
    periodic = 1.0 / (1.0 - power(wide * block * X_RING))
    low_sum = power(wide * scalar(s_ref[7])) * right_sum * periodic
    high_sum = power(wide * scalar(block - 1 - s_ref[7])) * left_sum * periodic
    rho = power(1.0)
    per_rho = power(-1.0)
    hop = power(wide)
    gain = rho / (1.0 - rho * rho)
    into_low = gain * (part[0] + per_rho * low_sum + hop * high_sum)
    into_high = gain * (part[1] + per_rho * high_sum + hop * low_sum)
    return into_low, into_high


def to_cells(values, span_t_high, span_t_low, back_high, back_low):
    lines = times(values, span_t_high, span_t_low)
    size = back_high.shape[0]
    return [
        times(lines[at : at + size].T, back_high, back_low) for at in range(0, lines.shape[0], size)
    ]


def solve_body(
    s_ref, planes, carried, opening, run8, part, got1, got2, got3, log_rho, pivots,
    span_t_high, span_t_low, back_high, back_low, edge, basis,
    wall, away, keep, solved, both, first,
):
    own, width, half = planes.shape
    count = own // 2
    is_low = s_ref[1] == 1
    code = s_ref[2]
    depthwise = lambda v: jnp.dot(
        basis[s_ref[1]], v, precision=HIGHEST, preferred_element_type=jnp.float32
    )
    into_low, into_high = x_sums(s_ref, run8, part, (got1, got2, got3), log_rho, width)
    gain_low = depthwise(into_low)
    gain_high = depthwise(into_high)
    both[0] = gain_low + gain_high
    both[1] = gain_low - gain_high
    first[width:] = jnp.zeros_like(first[width:])
    first[width : width + 1] = jnp.where(is_low, gain_low[own : own + 1], gain_low[:1])
    first[width + 1 : width + 2] = jnp.where(is_low, gain_high[own : own + 1], gain_high[:1])
    side = width // 16

    def tile(group, nothing):
        rows = pl.ds(pl.multiple_of(group * 8, 8), 8)
        parity = group // side
        scale = edge[rows]
        rhs = lambda i: scale * both[parity, i : i + 1]
        mine = lambda i: pivots[i - 1, rows]
        other = lambda i: pivots[own + i - 1, rows]
        carry = planes[code, rows] - rhs(0)
        carries = [carry]
        for i in range(1, own):
            carry = mine(i) * (planes[jnp.bitwise_xor(i, code), rows] - rhs(i)) - carry
            carries.append(carry)
        right = rhs(own)
        total = -right
        direct = -mine(own - 1) * right
        for i in range(1, own):
            right = rhs(own + i)
            total = -other(i) * right - total
            term = right if i == own - 1 else mine(own - 1 - i) * right
            direct = direct - term if i % 2 == 0 else direct + term
        total = total + carried[rows]
        value = (carry * other(own) - mine(own - 1) * total) * pivots[3 * own, rows]
        far_first = opening[rows] + (direct + value) * pivots[3 * own + 1, rows]
        solved[jnp.bitwise_xor(own - 1, code), rows] = value
        for i in range(own - 2, -1, -1):
            step = value if i == 0 else mine(i) * value
            value = (carries[i] - step) * pivots[2 * own + i, rows]
            solved[jnp.bitwise_xor(i, code), rows] = value
        first[rows] = jnp.where(is_low, far_first, value)
        return nothing

    lax.fori_loop(0, width // 8, tile, 0)
    table_high = span_t_high[s_ref[0]]
    table_low = span_t_low[s_ref[0]]
    line = times(first[...], table_high, table_low).T
    main = times(line[:, :width], back_high[:width, :width], back_low[:width, :width])
    wall[...] = jnp.concatenate([main, line[:, width:]], axis=1)
    values = solved[count:].reshape(count * width, half)
    for k, cells in enumerate(to_cells(values, table_high, table_low, back_high[...], back_low[...])):
        away[2 * k] = cells[:, :width]
        away[2 * k + 1] = cells[:, width:]
    keep[...] = solved[:count]


def cells_body(s_ref, keep, span_t_high, span_t_low, back_high, back_low, mine):
    count, width, half = keep.shape
    values = keep[...].reshape(count * width, half)
    pairs = to_cells(
        values, span_t_high[s_ref[0]], span_t_low[s_ref[0]], back_high[...], back_low[...]
    )
    for k, cells in enumerate(pairs):
        mine[2 * k] = cells[:, :width]
        mine[2 * k + 1] = cells[:, width:]


def join_body(s_ref, mine, came, out, held, sems):
    half = mine.shape[1]
    sign = (1 - 2 * s_ref[0]).astype(jnp.float32)
    copies = []
    for z in range(mine.shape[0]):
        ours = mine[z]
        theirs = came[z]
        held[z, :half] = ours + theirs
        held[z, half:] = sign * (ours - theirs)
        copy = pltpu.make_async_copy(held.at[z], out.at[z], sems.at[z])
        copy.start()
        copies.append(copy)
    for copy in copies:
        copy.wait()


def edge_body(s_ref, conductivity, temp, phase, gas, cond, packs, along, packed):
    depth, rows, width = temp.shape
    lane = lax.broadcasted_iota(jnp.int32, (CHUNK, width), 1)
    cold, warm = conductivity[0], conductivity[1]
    packed[...] = jnp.zeros_like(packed)

    def plane(z, nothing):
        for start in range(0, rows, CHUNK):
            at = slice(start, start + CHUNK)
            kept = packed[at]
            value = jnp.where(phase[z, at] == 1, warm, cold)
            cond[z, at] = value
            for k, part in enumerate((temp[z, at], value)):
                spot = 4 * (k * depth + z)
                chosen_lane = (lane >= spot) & (lane < spot + 4)
                kept = jnp.where(chosen_lane, pltpu.roll(part, spot + 2, 1), kept)
                line = 4 * depth * k + z
                if start == 0:
                    along[pl.ds(line + 2 * depth, 1)] = part[:1]
                    along[pl.ds(line + 3 * depth, 1)] = part[1:2]
                if start + CHUNK == rows:
                    along[pl.ds(line, 1)] = part[CHUNK - 2 : CHUNK - 1]
                    along[pl.ds(line + depth, 1)] = part[CHUNK - 1 :]
            packed[at] = kept
        return nothing

    lax.fori_loop(0, depth, plane, 0)
    last = 8 * depth
    turned = packed[...].T
    turned_gas = pltpu.roll(gas[...], 2, 1).T[:8]
    for h, at in pieces(rows):
        packs[h, :last] = turned[:, at]
        packs[h, last:] = turned_gas[:, at]
    along[last : last + 8] = jnp.concatenate(
        [gas[rows - 2 :], gas[:2], jnp.zeros((4, width), jnp.float32)], axis=0
    )


def pieces(length):
    return [(h, slice(h * 128, h * 128 + 128)) for h in range(length // 128)]


def column(ref, depth, kind, k):
    at = pl.ds(4 * depth * kind + k, depth, stride=4)
    return jnp.concatenate([ref[h, at] for h in range(ref.shape[0])], axis=1)


def flat(ref, row):
    return jnp.concatenate([ref[h, row : row + 1] for h in range(ref.shape[0])], axis=1)


def interleave(ref, odd, even):
    depth, length = odd.shape
    for h, at in pieces(length):
        ref[h, pl.ds(1, depth, stride=2)] = odd[:, at]
        ref[h, pl.ds(0, depth, stride=2)] = even[:, at]


def side_columns(s_ref, near, far, depth, kind, k, left):
    even = s_ref[8] == 0
    a, b = (far, near) if left else (near, far)
    return jnp.where(even, column(a, depth, kind, k), column(b, depth, kind, k))


def pass_body(s_ref, value, out):
    out[...] = value[...]


def corner_body(s_ref, along, near_x, far_x, out):
    depth = (along.shape[0] - 8) // 8
    width = along.shape[1]
    out[: along.shape[0]] = along[...]
    lane = lax.broadcasted_iota(jnp.int32, (depth, width), 1)
    block = jnp.zeros((depth, width), jnp.float32)
    rows = near_x.shape[0] * near_x.shape[2]
    spot = 0
    for y in (rows - 1, 0):
        for kind in range(2):
            for k, left in ((1, True), (2, False)):
                value = side_columns(s_ref, near_x, far_x, depth, kind, k, left)
                block = jnp.where(lane == spot, value[:, y : y + 1], block)
                spot += 1
    out[along.shape[0] :] = block


def settle(s_ref, lines, near, far):
    even = s_ref[0] == 0
    lines[0] = jnp.where(even, far[...], near[...])
    lines[1] = jnp.where(even, near[...], far[...])


def to_columns(packed, values):
    for h, at in pieces(packed.shape[1]):
        packed[: values.shape[1], at] = values[h]
    return packed[...].T


def rim(temp, cond, outer, inner, low, high, gas):
    depth, length = temp.shape
    row = lax.broadcasted_iota(jnp.int32, (depth, length), 0)
    lane = lax.broadcasted_iota(jnp.int32, (depth, length), 1)

    def around(value, at_low, at_high):
        return (
            jnp.where(lane == 0, at_low, pltpu.roll(value, 1, 1)),
            jnp.where(lane == length - 1, at_high, pltpu.roll(value, length - 1, 1)),
            jnp.where(row == 0, value, pltpu.roll(value, 1, 0)),
            jnp.where(row == depth - 1, value, pltpu.roll(value, depth - 1, 0)),
        )

    temps = (outer[0], inner[0]) + around(temp, low[0], high[0])
    conds = (outer[1], inner[1]) + around(cond, low[1], high[1])
    total = jnp.zeros_like(temp)
    for side_temp, side_cond in zip(temps, conds):
        total = total + (cond + side_cond) * (side_temp - temp)
    surface = jnp.where(row == 0, (STEP_RATE * HEAT_TRANSFER) * (gas - temp), 0.0)
    return temp + (0.5 * STEP_RATE) * total + surface


def step_planes(temp, cond, up, down, cond_up, cond_down, inflow, emit):
    depth, rows, width = temp.shape
    lane = lax.broadcasted_iota(jnp.int32, (CHUNK, width), 1)
    end = width - 1

    def shifted(ref, z, start, above, below):
        if start == 0:
            upper = jnp.concatenate([above[pl.ds(z, 1)], ref[z, : CHUNK - 1]], axis=0)
        else:
            upper = ref[z, start - 1 : start + CHUNK - 1]
        if start + CHUNK == rows:
            lower = jnp.concatenate([ref[z, start + 1 :], below[pl.ds(z, 1)]], axis=0)
        else:
            lower = ref[z, start + 1 : start + CHUNK + 1]
        return upper, lower

    def plane(z, first):
        before = jnp.maximum(z - 1, 0)
        after = jnp.minimum(z + 1, depth - 1)
        for start in range(0, rows, CHUNK):
            at = slice(start, start + CHUNK)
            here = temp[z, at]
            own = cond[z, at]
            pairs = []
            total = None
            sides = list(zip(shifted(temp, z, start, up, down), shifted(cond, z, start, cond_up, cond_down)))
            sides += [(temp[before, at], cond[before, at]), (temp[after, at], cond[after, at])]
            for side_temp, side_cond in sides:
                pair = own + side_cond
                pairs.append(pair)
                term = pair * (side_temp - here)
                total = term if total is None else total + term
            pair = own + pltpu.roll(own, end, 1)
            pairs.append(pair)
            flow = jnp.where(lane == end, 0.0, pair * (pltpu.roll(here, end, 1) - here))
            total = total + (flow - pltpu.roll(flow, 1, 1))
            spot = width - (2 * z + 1)
            entering = pltpu.roll(inflow[at], spot, 1)
            total = total + jnp.where((lane == 0) | (lane == end), entering, 0.0)
            emit(z, start, first, here + (0.5 * STEP_RATE) * total, pairs)

    plane(0, True)

    def later(z, nothing):
        plane(z, False)
        return nothing

    lax.fori_loop(1, depth, later, 0)


def first_body(
    s_ref, temp, cond, gas, packs, along, near_x, far_x, near_y, far_y,
    out, base_flow, face, base_lines, cond_lines, packed, flow, inflow, lines,
):
    depth, rows, width = temp.shape
    end = width - 1
    settle(s_ref, lines, near_y, far_y)
    last = 8 * depth
    own = lambda k: tuple(column(packs, depth, kind, k) for kind in range(2))
    left = lambda k: tuple(side_columns(s_ref, near_x, far_x, depth, kind, k, True) for kind in range(2))
    right = lambda k: tuple(side_columns(s_ref, near_x, far_x, depth, kind, k, False) for kind in range(2))
    line = lambda ref, k: tuple(
        ref[4 * depth * kind + depth * k : 4 * depth * kind + depth * (k + 1)] for kind in range(2)
    )
    above = lambda k: line(lines.at[0], k)
    below = lambda k: line(lines.at[1], k)
    corner = lambda which, spot: tuple(
        lines[which, last + 8 :][:, at : at + 1] for at in (spot, spot + 2)
    )
    even = s_ref[8] == 0
    gas_left = jnp.where(even, flat(far_x, last + 1), flat(near_x, last + 1))
    gas_right = jnp.where(even, flat(near_x, last + 2), flat(far_x, last + 2))
    at_lane = lambda pair, lane: tuple(v[:, lane : lane + 1] for v in pair)
    up_line, down_line = above(1), below(2)
    out_left = rim(*left(1), left(0), own(2), corner(0, 0), corner(1, 4), gas_left)
    out_right = rim(*right(2), right(3), own(1), corner(0, 1), corner(1, 5), gas_right)
    in_left = rim(
        *own(2), left(1), own(3), at_lane(up_line, 0), at_lane(down_line, 0), flat(packs, last + 2)
    )
    in_right = rim(
        *own(1), right(2), own(0), at_lane(up_line, end), at_lane(down_line, end),
        flat(packs, last + 1),
    )
    base_lines[0] = rim(
        *up_line, above(0), line(along, 2), corner(0, 0), corner(0, 1), lines[0, last + 1 : last + 2]
    )
    base_lines[1] = rim(
        *down_line, below(3), line(along, 1), corner(1, 4), corner(1, 5), lines[1, last + 2 : last + 3]
    )
    cond_lines[0] = up_line[1]
    cond_lines[1] = down_line[1]
    left_pair = own(2)[1] + left(1)[1]
    right_pair = own(1)[1] + right(2)[1]
    interleave(face, left_pair, right_pair)
    interleave(flow, left_pair * (left(1)[0] - own(2)[0]), right_pair * (right(2)[0] - own(1)[0]))
    interleave(base_flow, left_pair * (out_left - in_left), right_pair * (out_right - in_right))
    packed[...] = jnp.zeros_like(packed)
    inflow[...] = to_columns(packed, flow)

    def emit(z, start, first, value, pairs):
        at = slice(start, start + CHUNK)
        if first:
            value = value + (STEP_RATE * HEAT_TRANSFER) * (gas[at] - temp[0, at])
        out[z, at] = value

    span = lambda which, kind, k: lines.at[
        which, 4 * depth * kind + depth * k : 4 * depth * kind + depth * (k + 1)
    ]
    step_planes(
        temp, cond, span(0, 0, 1), span(1, 0, 2), span(0, 1, 1), span(1, 1, 2), inflow, emit
    )


def second_body(
    s_ref, base, cond, temp, gas, base_flow, face_rows, base_lines, cond_lines,
    out, top, weights, held, sems, packed, inflow, face,
):
    depth, rows, width = base.shape
    lane = lax.broadcasted_iota(jnp.int32, (CHUNK, width), 1)
    end = width - 1
    packed[...] = jnp.zeros_like(packed)
    inflow[...] = to_columns(packed, base_flow)
    face[...] = to_columns(packed, face_rows)

    def emit(z, start, first, value, pairs):
        at = slice(start, start + CHUNK)
        if first:
            value = value + (STEP_RATE * HEAT_TRANSFER) * (gas[at] - temp[0, at])
            edge = pltpu.roll(face[at], end, 1)
            across = pairs[4]
            left = jnp.where(lane == 0, edge, pltpu.roll(across, 1, 1))
            right = jnp.where(lane == end, edge, across)
            for k, pair in enumerate((pairs[0], pairs[1], left, right, pairs[3])):
                weights[k, at] = (0.5 * STEP_RATE) * pair
        held[z, at] = value
        if not first and start + CHUNK == rows:

            @pl.when(z >= 2)
            def _():
                pltpu.make_async_copy(held.at[z], out.at[z], sems.at[z]).start()

    step_planes(
        base, cond, base_lines.at[0], base_lines.at[1], cond_lines.at[0], cond_lines.at[1],
        inflow, emit,
    )
    top[...] = held[:2]
    for z in range(2, depth):
        pltpu.make_async_copy(held.at[z], out.at[z], sems.at[z]).wait()


def faces(value, row, lane, up, down, left, right):
    rows, width = value.shape
    return (
        jnp.where(row == 0, up, pltpu.roll(value, 1, 0)),
        jnp.where(row == rows - 1, down, pltpu.roll(value, rows - 1, 0)),
        jnp.where(lane == 0, left, pltpu.roll(value, 1, 1)),
        jnp.where(lane == width - 1, right, pltpu.roll(value, width - 1, 1)),
    )


def wall_body(s_ref, ours, theirs, weights, base, filled, out, held, sem):
    half = ours.shape[0]
    rows, width = weights.shape[1:]
    sign = (1 - 2 * s_ref[0]).astype(jnp.float32)
    bottom = (1 - 2 * s_ref[3]).astype(jnp.float32)
    second = s_ref[4] == 1
    factor = STEP_RATE * HEAT_TRANSFER * PRESSURE_WORK

    def lines(start, count, minus):
        our_sign = jnp.where(s_ref[0] == 0, 1.0, minus) * factor
        their_sign = jnp.where(s_ref[0] == 0, minus, 1.0) * factor
        at = pl.ds(start, count)
        return our_sign * ours[at] + their_sign * theirs[at]

    begin = pl.multiple_of(s_ref[4] * rows, rows)
    middle = lines(begin, rows, bottom)
    above = lines(jnp.where(second, rows - 1, half - 1), 1, jnp.where(second, bottom, -bottom))
    below = lines(jnp.where(second, 0, rows), 1, jnp.where(second, -bottom, bottom))
    share = middle[:, :width]
    row = lax.broadcasted_iota(jnp.int32, (rows, width), 0)
    lane = lax.broadcasted_iota(jnp.int32, (rows, width), 1)
    around = faces(
        share, row, lane, above[:, :width], below[:, :width],
        middle[:, width : width + 1], middle[:, width + 1 : width + 2],
    )
    added = 2.0 * share
    for k in range(4):
        added = added + weights[k] * (around[k] - share)
    down = weights[4] * share
    held[0] = base[0] + added - down
    held[1] = base[1] + down
    copy = pltpu.make_async_copy(held, out.at[:2], sem)
    copy.start()
    copy.wait()


def mover(groups, pencils):
    def move(value, target):
        pairs = []
        for g in range(groups):
            for p in range(pencils):
                to = target(g, p)
                pairs.append((g * pencils + p, to[0] * pencils + to[1]))
        return lax.ppermute(value, ("grp", "pen"), pairs)

    return move


def per_device(pressure_source, solid_temp, gas_wall_temp, phase_map, phase_conductivity):
    groups = lax.axis_size("grp")
    pencils = lax.axis_size("pen")
    group_idx = lax.axis_index("grp")
    pencil_idx = lax.axis_index("pen")
    depth_loc, span_len, width = pressure_source.shape
    depth = depth_loc * groups
    half = span_len // 2
    own = depth // 2
    core = group_idx % 2
    low = group_idx // 2
    zi = pencil_idx % Z_RING
    yl = pencil_idx // Z_RING % Y_PAIR
    place = pencil_idx % (Z_RING * Y_PAIR)
    move = mover(groups, pencils)
    tab = make_tables(span_len, width, depth)
    const = {k: tuple(map(jnp.asarray, v)) if isinstance(v, tuple) else jnp.asarray(v) for k, v in tab.items()}
    code = jnp.where(low == 0, core * 4, 7 - 4 * core)
    scalars = jnp.stack([core, low, code, low, core, zi, yl, place, pencil_idx % 2]).astype(jnp.int32)
    span = list(const["span"])
    into = list(const["into"])
    back = list(const["back"])
    span_t = list(const["span_t"])
    tile_rows = span_len // groups
    flip = lambda mask: lambda g, p: (g ^ mask, p)
    near_pair = lambda g, p: (g, p ^ 1)
    far_pair = lambda g, p: (g, (p + 1 if p % 2 else p - 1) % pencils)

    other_core = lambda g, p: (g ^ 1, p)
    other_half = lambda g, p: (g ^ 2, p)
    halves_of = tile_rows // 128
    column_scratch = pltpu.VMEM((tile_rows, width), jnp.float32)
    row_scratch = pltpu.VMEM((width, tile_rows), jnp.float32)
    (pivots,) = run(
        pivot_body, 1.2, scalars, [], [const["lam"], const["sigma"]], [(3 * own + 2, width, half)]
    )
    cond, packs, along = run(
        edge_body, 2.8, scalars, [pivots], [solid_temp, phase_map, gas_wall_temp],
        [(depth, tile_rows, width), (halves_of, 8 * depth + 8, 128), (8 * depth + 8, width)],
        scratch=[column_scratch], small=[phase_conductivity],
    )
    near_x = [move(packs, near_pair), move(packs, far_pair)]
    folded = jax.ShapeDtypeStruct((depth_loc, half, width), jnp.float32)
    away, kept = run_blocks(
        fold_body, 0.8, scalars, [along, pressure_source], [ORDER, plane_of(pressure_source)],
        [folded.shape, folded.shape], [plane_of(folded), plane_of(folded)], depth_loc,
    )
    arrived = move(away, other_core)
    (held,) = run(
        held_body, 2.1, scalars, [], [kept, *into, *span], [(depth_loc, width, half)]
    )
    (lines,) = run(
        corner_body, 0.6, scalars, [held], [along, *near_x], [(9 * depth + 8, width)]
    )
    near_y = [move(lines, flip(1)), move(lines, flip(3))]
    planes, edges, carried, opening = run(
        arrived_body, 3.4, scalars, [lines],
        [arrived, held, *into, *span, pivots, const["edge"], const["basis_t"], const["far"]],
        [(own, width, half), (2, depth, half), (width, half), (width, half)],
        scratch=[pltpu.VMEM((2, depth, 8, half), jnp.float32)],
    )
    z_got = [
        move(edges, lambda g, p, d=d: (g, p // Z_RING * Z_RING + (p + d) % Z_RING))
        for d in range(1, Z_RING)
    ]
    log_rho = const["log_rho"]
    pair_shape = edges.shape
    four, two, carried = run(
        functools.partial(z_body, width=width), 0.6, scalars, near_y,
        [edges, *z_got, log_rho, carried], [(4,) + pair_shape[1:], pair_shape, carried.shape],
    )
    carried_there = move(carried, other_half)
    there = move(four, other_half)
    beside1 = move(two, lambda g, p: (g, p ^ Z_RING))
    beside2 = move(two, lambda g, p: (g ^ 2, p ^ Z_RING))
    base, base_flow, face, base_lines, cond_lines = run(
        first_body, 6.6, scalars, [two],
        [solid_temp, cond, gas_wall_temp, packs, along, *near_x, *near_y],
        [(depth, tile_rows, width), (halves_of, 2 * depth, 128), (halves_of, 2 * depth, 128),
         (2, depth, width), (2, depth, width)],
        scratch=[
            row_scratch, pltpu.VMEM((halves_of, 2 * depth, 128), jnp.float32), column_scratch,
            pltpu.VMEM((2, 9 * depth + 8, width), jnp.float32),
        ],
    )
    run8, part, opening = run(
        functools.partial(y_body, width=width), 0.6, scalars, [base, carried_there],
        [four, there, beside1, beside2, log_rho, opening], [pair_shape, pair_shape, opening.shape],
    )
    block = Z_RING * Y_PAIR
    opening_there = move(opening, other_half)
    x_got = [move(run8, lambda g, p, d=d: (g, (p + block * d) % pencils)) for d in range(1, X_RING)]
    final, top, weights = run(
        second_body, 6.5, scalars, [run8],
        [base, cond, solid_temp, gas_wall_temp, base_flow, face, base_lines, cond_lines],
        [solid_temp.shape, (2, tile_rows, width), (5, tile_rows, width)],
        scratch=[
            pltpu.VMEM((depth, tile_rows, width), jnp.float32), pltpu.SemaphoreType.DMA((depth,)),
            row_scratch, column_scratch, column_scratch,
        ],
        out_specs=[ORDER, FAST, FAST],
    )
    wall, away, keep = run(
        solve_body, 6.9, scalars, [weights],
        [planes, carried_there, opening_there, run8, part, *x_got, log_rho, pivots, *span_t, *back,
         const["edge"], const["basis"]],
        [(half, 2 * width), (depth_loc, half, width), (depth_loc, width, half)],
        scratch=[
            pltpu.VMEM((own, width, half), jnp.float32),
            pltpu.VMEM((2, depth, half), jnp.float32),
            pltpu.VMEM((2 * width, half), jnp.float32),
        ],
    )
    wall_came = move(wall, other_core)
    came = move(away, other_core)
    (mine,) = run(cells_body, 2.2, scalars, [], [keep, *span_t, *back], [(depth_loc, half, width)])
    (pressure,) = run(
        join_body, 1.9, scalars, [], [mine, came], [pressure_source.shape], out_specs=[ORDER],
        scratch=[
            pltpu.VMEM(pressure_source.shape, jnp.float32), pltpu.SemaphoreType.DMA((depth_loc,))
        ],
    )
    (final,) = run(
        wall_body, 1.5, scalars, [], [wall, wall_came, weights, top, (final, ORDER)], [final.shape],
        scratch=[pltpu.VMEM(top.shape, jnp.float32), pltpu.SemaphoreType.DMA],
        out_specs=[ORDER], aliases={5: 0},
    )
    return (pressure, final)


def solution(mesh):
    in_specs = (
        P("grp", None, "pen"),
        P(None, "grp", "pen"),
        P("grp", "pen"),
        P(None, "grp", "pen"),
        P(),
    )
    out_specs = (P("grp", None, "pen"), P(None, "grp", "pen"))
    return jax.shard_map(
        per_device, mesh=mesh, in_specs=in_specs, out_specs=out_specs, check_vma=False
    )
```

```python
import functools
import math

import jax
import jax.numpy as jnp
import numpy as np
from jax import lax
from jax.experimental import pallas as pl
from jax.experimental.pallas import tpu as pltpu
from jax.sharding import PartitionSpec as P

HIGHEST = lax.Precision.HIGHEST
HEAT_TRANSFER = 1.0
PRESSURE_WORK = 0.5
STEP_RATE = 0.12
Z_RING, Y_PAIR, X_RING = 4, 2, 4
VMEM_LIMIT = 18 * 1024 * 1024
BLOCK_LIMIT = 16 * 1024 * 1024
LANES = 512
CHUNK = 32
COST_SCALE = 0.1


def halves(value):
    high = np.asarray(value, np.float32).astype(jnp.bfloat16)
    low = (np.asarray(value, np.float64) - high.astype(np.float64)).astype(jnp.bfloat16)
    return high, low


def make_tables(span_len, width, depth):
    half = span_len // 2
    waves = np.stack([2 * np.arange(half), 2 * np.arange(half) + 1]).astype(np.float64)
    rows = np.arange(half)
    angle = 2 * np.pi * ((rows[None, :, None] * waves[:, None, :]) % span_len) / span_len
    span = np.cos(angle) + np.sin(angle)
    lam = -4 * np.sin(np.pi * waves / span_len) ** 2
    order = np.concatenate([np.arange(0, width, 2), np.arange(1, width, 2)]) + 1.0
    cells = np.arange(width) + 1.0
    sine = np.sqrt(2 / (width + 1)) * np.sin(np.pi * cells[:, None] * order[None, :] / (width + 1))
    sigma = -4 * np.sin(np.pi * order / (2 * (width + 1))) ** 2
    modes = np.arange(depth)
    theta = np.pi * (2 * modes + 1) / (2 * depth + 1)
    basis = np.cos(theta[None, :] * (np.arange(depth)[:, None] + 0.5)) / np.sqrt((2 * depth + 1) / 4)
    mu = -4 * np.sin(theta / 2) ** 2
    stretch = -(mu[None, :, None] + lam[:, None, :])
    log_rho = -2 * np.arcsinh(np.sqrt(stretch) / 2)
    down = np.arange(depth // 2)
    up = depth - 1 - down
    ordered = np.stack([basis[np.concatenate([down, up])], basis[np.concatenate([up, down])]])
    pair = np.kron(np.eye(2), sine)
    f32 = lambda v: np.asarray(v, np.float32)
    lanes = min(LANES, half)
    return {
        "span": halves(span),
        "span_t": halves(np.swapaxes(span, 1, 2)),
        "into": halves(pair / span_len),
        "back": halves(pair.T),
        "lam": f32(lam)[:, None, :],
        "sigma": f32(np.repeat(sigma[:, None], lanes, 1)),
        "edge": f32(np.repeat(sine[0][:, None], lanes, 1)),
        "basis": f32(ordered),
        "basis_t": f32(np.swapaxes(ordered, 1, 2)),
        "log_rho": f32(log_rho),
        "far": f32(np.exp(log_rho * (width + 1))),
    }


def product(first, second):
    return jnp.dot(first, second, preferred_element_type=jnp.float32)


def split(value):
    high = value.astype(jnp.bfloat16)
    return high, (value - high.astype(jnp.float32)).astype(jnp.bfloat16)


def times(value, high, low):
    value_high, value_low = split(value)
    return product(value_high, high) + (product(value_high, low) + product(value_low, high))


def times_turned(high, low, value):
    value_high, value_low = split(value)
    turned = lambda a, b: lax.dot_general(
        a, b, (((1,), (1,)), ((), ())), preferred_element_type=jnp.float32
    )
    return turned(high, value_high) + (turned(low, value_high) + turned(high, value_low))


ORDER = pl.BlockSpec(memory_space=pl.ANY)
SCALARS = pl.BlockSpec(memory_space=pltpu.SMEM)
FAST = pl.BlockSpec(memory_space=pltpu.VMEM)


def plane_of(array):
    rest = array.shape[1:]
    return pl.BlockSpec((1,) + rest, lambda i, s: (i,) + (0,) * len(rest))


def cost(time_us):
    return pl.CostEstimate(flops=1, bytes_accessed=int(time_us * 3.69e6 * COST_SCALE), transcendentals=0)


def run(body, time_us, scalars, ordered, arrays, outs, scratch=(), small=(), out_specs=None, aliases=None):
    outs = [jax.ShapeDtypeStruct(shape, jnp.float32) for shape in outs]
    skip = len(ordered)
    count = len(small)
    kinds = [FAST if spec is None else spec for spec in (a[1] if type(a) is tuple else None for a in arrays)]
    arrays = [a[0] if type(a) is tuple else a for a in arrays]
    specs = [SCALARS] + [SCALARS] * count + [ORDER] * skip + kinds

    def inner(s_ref, *refs):
        body(s_ref, *refs[:count], *refs[count + skip :])

    return pl.pallas_call(
        inner,
        out_shape=outs,
        in_specs=specs,
        out_specs=out_specs or [FAST] * len(outs),
        scratch_shapes=list(scratch),
        input_output_aliases=aliases or {},
        compiler_params=pltpu.CompilerParams(vmem_limit_bytes=VMEM_LIMIT),
        cost_estimate=cost(time_us),
    )(scalars, *small, *ordered, *arrays)


def run_blocks(body, time_us, scalars, arrays, specs, outs, out_specs, steps):
    return pl.pallas_call(
        body,
        out_shape=[jax.ShapeDtypeStruct(out, jnp.float32) for out in outs],
        grid_spec=pltpu.PrefetchScalarGridSpec(
            num_scalar_prefetch=1, grid=(steps,), in_specs=specs, out_specs=out_specs
        ),
        compiler_params=pltpu.CompilerParams(vmem_limit_bytes=BLOCK_LIMIT),
        cost_estimate=cost(time_us),
    )(scalars, *arrays)


def fold_body(s_ref, after, source, away, kept):
    half = source.shape[1] // 2
    sign = (1 - 2 * s_ref[0]).astype(jnp.float32)
    upper = source[:, :half]
    lower = sign * source[:, half:]
    away[...] = upper - lower
    kept[...] = upper + lower


def spectral(planes, into_high, into_low, span_high, span_low):
    turned = []
    for pair in range(0, len(planes), 2):
        cells = jnp.concatenate(planes[pair : pair + 2], axis=1)
        turned.append(times(cells, into_high, into_low).T)
    return times(jnp.concatenate(turned, axis=0), span_high, span_low)


def held_body(s_ref, kept, into_high, into_low, span_high, span_low, out):
    out[...] = spectral(
        [kept[z] for z in range(kept.shape[0])], into_high[...], into_low[...],
        span_high[s_ref[0]], span_low[s_ref[0]],
    ).reshape(out.shape)


def continuants(centre, first, count):
    values = [jnp.ones_like(centre), centre + first]
    for _ in range(1, count):
        values.append(centre * values[-1] - values[-2])
    return values


def pivot_body(s_ref, lam, sigma, out):
    own = (out.shape[0] - 2) // 3
    width = out.shape[1]
    low = s_ref[1].astype(jnp.float32)

    def tile(group, nothing):
        rows = pl.ds(pl.multiple_of(group * 8, 8), 8)
        centre = lam[s_ref[0]] + sigma[rows] - 2.0
        mine = continuants(centre, 1.0 - low, own)
        other = continuants(centre, low, own)
        for i in range(own):
            out[i, rows] = mine[i + 1]
            out[own + i, rows] = other[i + 1]
            out[2 * own + i, rows] = 1.0 / mine[i + 1]
        out[3 * own, rows] = 1.0 / (mine[own] * other[own] - mine[own - 1] * other[own - 1])
        out[3 * own + 1, rows] = 1.0 / other[own]
        return nothing

    lax.fori_loop(0, width // 8, tile, 0)


def arrived_body(
    s_ref, arrived, held, into_high, into_low, span_high, span_low, pivots, edge, basis_t, far, packs,
    planes, edges, carried, opening, mixed, sums,
):
    count = held.shape[0]
    own = 2 * count
    width, half = held.shape[1:]
    planes[:count] = held[...]
    planes[count:] = spectral(
        [arrived[z] for z in range(count)], into_high[...], into_low[...],
        span_high[s_ref[0]], span_low[s_ref[0]],
    ).reshape(held.shape)
    sums[...] = jnp.zeros_like(sums)
    code = s_ref[2]
    side = width // 16

    def tile(group, nothing):
        rows = pl.ds(pl.multiple_of(group * 8, 8), 8)
        parity = group // side
        carry = planes[code, rows]
        carries = [carry]
        for i in range(1, own):
            carry = pivots[i - 1, rows] * planes[jnp.bitwise_xor(i, code), rows] - carry
            carries.append(carry)
        carried[rows] = carry
        shared = carry * pivots[3 * own, rows]
        scale = edge[rows]
        value = shared * pivots[2 * own - 1, rows]
        sums[parity, own - 1] += scale * value
        for i in range(own - 2, -1, -1):
            step = value if i == 0 else pivots[i - 1, rows] * value
            value = (carries[i] - step) * pivots[2 * own + i, rows]
            sums[parity, i] += scale * value
        opening[rows] = value + pivots[2 * own - 2, rows] * shared * pivots[3 * own - 1, rows]
        shared = scale * shared
        for i in range(own):
            term = shared if i == 0 else pivots[own + i - 1, rows] * shared
            sums[parity, own + i] += term if (own - i) % 2 == 0 else -term
        return nothing

    lax.fori_loop(0, width // 8, tile, 0)
    total = jnp.sum(sums[...], axis=2)
    modal = lambda v: jnp.dot(
        basis_t[s_ref[1]], v, precision=HIGHEST, preferred_element_type=jnp.float32
    )
    even = modal(total[0])
    odd = modal(total[1])
    edge_low = even + odd
    edge_high = even - odd
    right = edge_high + far[s_ref[0]] * edge_low
    left = edge_low + far[s_ref[0]] * edge_high
    edges[0] = right
    edges[1] = left
    at = 0
    for value in (right, left):
        for _, lanes in pieces(half):
            mixed[at : at + value.shape[0]] = value[:, lanes]
            at += value.shape[0]
    mixed[at:] = packs[...]


def powers(s_ref, log_rho):
    rate = log_rho[s_ref[0]]
    return lambda n: jnp.exp(rate * n)


def scalar(value):
    return value.astype(jnp.float32)


def z_body(s_ref, edges, mixed, got2, got3, log_rho, four, two, *, width):
    power = powers(s_ref, log_rho)
    zi = s_ref[5]
    wide = float(width)
    right, left = edges[0], edges[1]
    low_sum = jnp.zeros_like(right)
    high_sum = jnp.zeros_like(right)
    right4 = power(wide * scalar(Z_RING - 1 - zi)) * right
    left4 = power(wide * scalar(zi)) * left
    size = right.shape[0]
    lanes = mixed.shape[1]
    pieces_of = right.shape[1] // lanes
    first_right, first_left = (
        jnp.concatenate(
            [mixed[(k * pieces_of + c) * size : (k * pieces_of + c + 1) * size] for c in range(pieces_of)],
            axis=1,
        )
        for k in range(2)
    )
    for d, got_right, got_left in (
        (1, first_right, first_left), (2, got2[0], got2[1]), (3, got3[0], got3[1])
    ):
        source = jnp.bitwise_xor(zi, d)
        before = scalar(source < zi)
        gap = jnp.maximum(zi - source, source - zi) - 1
        step = power(wide * scalar(gap))
        low_sum = low_sum + before * step * got_right
        high_sum = high_sum + (1.0 - before) * step * got_left
        right4 = right4 + power(wide * scalar(Z_RING - 1 - source)) * got_right
        left4 = left4 + power(wide * scalar(source)) * got_left
    hop = power(wide)
    per_rho = power(-1.0)
    four[0] = per_rho * low_sum + left + hop * high_sum
    four[1] = per_rho * high_sum + right + hop * low_sum
    four[2] = right4
    four[3] = left4
    two[0] = right4
    two[1] = left4


def y_body(s_ref, four, there, beside1, beside2, log_rho, opening, run8, part, passed, *, width):
    passed[...] = opening[...]
    power = powers(s_ref, log_rho)
    zi = s_ref[5]
    wide = float(width)
    behind = scalar(s_ref[6])
    other0 = beside1[0] + beside2[0]
    other1 = beside1[1] + beside2[1]
    right4 = four[2] + there[2]
    left4 = four[3] + there[3]
    low_sum = behind * power(wide * scalar(zi)) * other0
    high_sum = (1.0 - behind) * power(wide * scalar(Z_RING - 1 - zi)) * other1
    run4 = power(wide * Z_RING)
    is_behind = s_ref[6] == 1
    run8[0] = jnp.where(is_behind, run4 * other0 + right4, run4 * right4 + other0)
    run8[1] = jnp.where(is_behind, other1 + run4 * left4, left4 + run4 * other1)
    hop = power(wide)
    per_rho = power(-1.0)
    part[0] = four[0] + there[0] + per_rho * low_sum + hop * high_sum
    part[1] = four[1] + there[1] + per_rho * high_sum + hop * low_sum


def x_sums(s_ref, run8, part, gots, log_rho, width):
    power = powers(s_ref, log_rho)
    wide = float(width)
    block = Z_RING * Y_PAIR
    right_sum = power(wide * block * (X_RING - 1)) * run8[0]
    left_sum = power(wide * block * (X_RING - 1)) * run8[1]
    for d, got in enumerate(gots, 1):
        right_sum = right_sum + power(wide * block * (d - 1)) * got[0]
        left_sum = left_sum + power(wide * block * (X_RING - 1 - d)) * got[1]
    periodic = 1.0 / (1.0 - power(wide * block * X_RING))
    low_sum = power(wide * scalar(s_ref[7])) * right_sum * periodic
    high_sum = power(wide * scalar(block - 1 - s_ref[7])) * left_sum * periodic
    rho = power(1.0)
    per_rho = power(-1.0)
    hop = power(wide)
    gain = rho / (1.0 - rho * rho)
    into_low = gain * (part[0] + per_rho * low_sum + hop * high_sum)
    into_high = gain * (part[1] + per_rho * high_sum + hop * low_sum)
    return into_low, into_high


def to_cells(values, span_t_high, span_t_low, back_high, back_low):
    lines = times(values, span_t_high, span_t_low)
    size = back_high.shape[0]
    return [
        times(lines[at : at + size].T, back_high, back_low) for at in range(0, lines.shape[0], size)
    ]


def solve_body(
    s_ref, planes, carried, opening, run8, part, got1, got2, got3, log_rho, pivots,
    span_t_high, span_t_low, back_high, back_low, edge, basis,
    wall, away, keep, solved, both, first,
):
    own, width, half = planes.shape
    count = own // 2
    is_low = s_ref[1] == 1
    code = s_ref[2]
    depthwise = lambda v: jnp.dot(
        basis[s_ref[1]], v, precision=HIGHEST, preferred_element_type=jnp.float32
    )
    into_low, into_high = x_sums(s_ref, run8, part, (got1, got2, got3), log_rho, width)
    gain_low = depthwise(into_low)
    gain_high = depthwise(into_high)
    both[0] = gain_low + gain_high
    both[1] = gain_low - gain_high
    first[width:] = jnp.zeros_like(first[width:])
    first[width : width + 1] = jnp.where(is_low, gain_low[own : own + 1], gain_low[:1])
    first[width + 1 : width + 2] = jnp.where(is_low, gain_high[own : own + 1], gain_high[:1])
    side = width // 16

    def tile(group, nothing):
        rows = pl.ds(pl.multiple_of(group * 8, 8), 8)
        parity = group // side
        scale = edge[rows]
        rhs = lambda i: scale * both[parity, i : i + 1]
        mine = lambda i: pivots[i - 1, rows]
        other = lambda i: pivots[own + i - 1, rows]
        carry = planes[code, rows] - rhs(0)
        carries = [carry]
        for i in range(1, own):
            carry = mine(i) * (planes[jnp.bitwise_xor(i, code), rows] - rhs(i)) - carry
            carries.append(carry)
        right = rhs(own)
        total = -right
        direct = -mine(own - 1) * right
        for i in range(1, own):
            right = rhs(own + i)
            total = -other(i) * right - total
            term = right if i == own - 1 else mine(own - 1 - i) * right
            direct = direct - term if i % 2 == 0 else direct + term
        total = total + carried[rows]
        value = (carry * other(own) - mine(own - 1) * total) * pivots[3 * own, rows]
        far_first = opening[rows] + (direct + value) * pivots[3 * own + 1, rows]
        solved[jnp.bitwise_xor(own - 1, code), rows] = value
        for i in range(own - 2, -1, -1):
            step = value if i == 0 else mine(i) * value
            value = (carries[i] - step) * pivots[2 * own + i, rows]
            solved[jnp.bitwise_xor(i, code), rows] = value
        first[rows] = jnp.where(is_low, far_first, value)
        return nothing

    lax.fori_loop(0, width // 8, tile, 0)
    table_high = span_t_high[s_ref[0]]
    table_low = span_t_low[s_ref[0]]
    line = times(first[...], table_high, table_low).T
    main = times(line[:, :width], back_high[:width, :width], back_low[:width, :width])
    wall[...] = jnp.concatenate([main, line[:, width:]], axis=1)
    values = solved[count:].reshape(count * width, half)
    for k, cells in enumerate(to_cells(values, table_high, table_low, back_high[...], back_low[...])):
        away[2 * k] = cells[:, :width]
        away[2 * k + 1] = cells[:, width:]
    keep[...] = solved[:count]


def cells_body(s_ref, keep, span_t_high, span_t_low, back_high, back_low, mine):
    count, width, half = keep.shape
    values = keep[...].reshape(count * width, half)
    pairs = to_cells(
        values, span_t_high[s_ref[0]], span_t_low[s_ref[0]], back_high[...], back_low[...]
    )
    for k, cells in enumerate(pairs):
        mine[2 * k] = cells[:, :width]
        mine[2 * k + 1] = cells[:, width:]


def join_planes(s_ref, mine, came, out, held, sems):
    half = mine.shape[1]
    sign = (1 - 2 * s_ref[0]).astype(jnp.float32)
    copies = []
    for z in range(mine.shape[0]):
        ours = mine[z]
        theirs = came[z]
        held[z, :half] = ours + theirs
        held[z, half:] = sign * (ours - theirs)
        copy = pltpu.make_async_copy(held.at[z], out.at[z], sems.at[z])
        copy.start()
        copies.append(copy)
    return copies


def edge_body(s_ref, conductivity, temp, phase, gas, cond, packs, along, packed):
    depth, rows, width = temp.shape
    lane = lax.broadcasted_iota(jnp.int32, (CHUNK, width), 1)
    cold, warm = conductivity[0], conductivity[1]
    packed[...] = jnp.zeros_like(packed)

    def plane(z, nothing):
        for start in range(0, rows, CHUNK):
            at = slice(start, start + CHUNK)
            kept = packed[at]
            value = jnp.where(phase[z, at] == 1, warm, cold)
            cond[z, at] = value
            for k, part in enumerate((temp[z, at], value)):
                spot = 4 * (k * depth + z)
                chosen_lane = (lane >= spot) & (lane < spot + 4)
                kept = jnp.where(chosen_lane, pltpu.roll(part, spot + 2, 1), kept)
                line = 4 * depth * k + z
                if start == 0:
                    along[pl.ds(line + 2 * depth, 1)] = part[:1]
                    along[pl.ds(line + 3 * depth, 1)] = part[1:2]
                if start + CHUNK == rows:
                    along[pl.ds(line, 1)] = part[CHUNK - 2 : CHUNK - 1]
                    along[pl.ds(line + depth, 1)] = part[CHUNK - 1 :]
            packed[at] = kept
        return nothing

    lax.fori_loop(0, depth, plane, 0)
    last = 8 * depth
    turned = packed[...].T
    turned_gas = pltpu.roll(gas[...], 2, 1).T[:8]
    for h, at in pieces(rows):
        base = h * (last + 8)
        packs[base : base + last] = turned[:, at]
        packs[base + last : base + last + 8] = turned_gas[:, at]
    along[last : last + 8] = jnp.concatenate(
        [gas[rows - 2 :], gas[:2], jnp.zeros((4, width), jnp.float32)], axis=0
    )


def pieces(length):
    return [(h, slice(h * 128, h * 128 + 128)) for h in range(length // 128)]


def column(source, depth, kind, k):
    ref, base, size = source
    at = lambda h: pl.ds(base + h * size + 4 * depth * kind + k, depth, stride=4)
    return jnp.concatenate([ref[at(h)] for h in range((ref.shape[0] - base) // size)], axis=1)


def flat(source, row):
    ref, base, size = source
    at = lambda h: base + h * size + row
    count = (ref.shape[0] - base) // size
    return jnp.concatenate([ref[at(h) : at(h) + 1] for h in range(count)], axis=1)


def sources(packs, mixed, far_x, depth):
    size = 8 * depth + 8
    return (packs, 0, size), (mixed, mixed.shape[0] - packs.shape[0], size), (far_x, 0, size)


def interleave(ref, odd, even):
    depth, length = odd.shape
    for h, at in pieces(length):
        ref[h, pl.ds(1, depth, stride=2)] = odd[:, at]
        ref[h, pl.ds(0, depth, stride=2)] = even[:, at]


def side_columns(s_ref, near, far, depth, kind, k, left):
    even = s_ref[8] == 0
    a, b = (far, near) if left else (near, far)
    return jnp.where(even, column(a, depth, kind, k), column(b, depth, kind, k))


def corner_body(s_ref, along, packs, mixed, far, out):
    depth = (along.shape[0] - 8) // 8
    width = along.shape[1]
    _, near_x, far_x = sources(packs, mixed, far, depth)
    out[: along.shape[0]] = along[...]
    lane = lax.broadcasted_iota(jnp.int32, (depth, width), 1)
    block = jnp.zeros((depth, width), jnp.float32)
    rows = packs.shape[0] // (8 * depth + 8) * 128
    spot = 0
    for y in (rows - 1, 0):
        for kind in range(2):
            for k, left in ((1, True), (2, False)):
                value = side_columns(s_ref, near_x, far_x, depth, kind, k, left)
                block = jnp.where(lane == spot, value[:, y : y + 1], block)
                spot += 1
    out[along.shape[0] :] = block


def settle(s_ref, lines, near, far):
    even = s_ref[0] == 0
    lines[0] = jnp.where(even, far[...], near[...])
    lines[1] = jnp.where(even, near[...], far[...])


def to_columns(packed, values):
    for h, at in pieces(packed.shape[1]):
        packed[: values.shape[1], at] = values[h]
    return packed[...].T


def rim(temp, cond, outer, inner, low, high, gas):
    depth, length = temp.shape
    row = lax.broadcasted_iota(jnp.int32, (depth, length), 0)
    lane = lax.broadcasted_iota(jnp.int32, (depth, length), 1)

    def around(value, at_low, at_high):
        return (
            jnp.where(lane == 0, at_low, pltpu.roll(value, 1, 1)),
            jnp.where(lane == length - 1, at_high, pltpu.roll(value, length - 1, 1)),
            jnp.where(row == 0, value, pltpu.roll(value, 1, 0)),
            jnp.where(row == depth - 1, value, pltpu.roll(value, depth - 1, 0)),
        )

    temps = (outer[0], inner[0]) + around(temp, low[0], high[0])
    conds = (outer[1], inner[1]) + around(cond, low[1], high[1])
    total = jnp.zeros_like(temp)
    for side_temp, side_cond in zip(temps, conds):
        total = total + (cond + side_cond) * (side_temp - temp)
    surface = jnp.where(row == 0, (STEP_RATE * HEAT_TRANSFER) * (gas - temp), 0.0)
    return temp + (0.5 * STEP_RATE) * total + surface


def entering(inflow, z, at, lane):
    width = lane.shape[1]
    moved = pltpu.roll(inflow[at], width - (2 * z + 1), 1)
    return jnp.where((lane == 0) | (lane == width - 1), moved, 0.0)


def step_planes(temp, cond, up, down, cond_up, cond_down, inflow, emit, starts):
    depth, rows, width = temp.shape
    lane = lax.broadcasted_iota(jnp.int32, (CHUNK, width), 1)
    end = width - 1

    def shifted(ref, z, start, above, below):
        if start == 0:
            upper = jnp.concatenate([above[pl.ds(z, 1)], ref[z, : CHUNK - 1]], axis=0)
        else:
            upper = ref[z, start - 1 : start + CHUNK - 1]
        if start + CHUNK == rows:
            lower = jnp.concatenate([ref[z, start + 1 :], below[pl.ds(z, 1)]], axis=0)
        else:
            lower = ref[z, start + 1 : start + CHUNK + 1]
        return upper, lower

    def plane(z, first):
        before = jnp.maximum(z - 1, 0)
        after = jnp.minimum(z + 1, depth - 1)
        for start in starts:
            at = slice(start, start + CHUNK)
            here = temp[z, at]
            own = cond[z, at]
            pairs = []
            total = None
            sides = list(zip(shifted(temp, z, start, up, down), shifted(cond, z, start, cond_up, cond_down)))
            sides += [(temp[before, at], cond[before, at]), (temp[after, at], cond[after, at])]
            for side_temp, side_cond in sides:
                pair = own + side_cond
                pairs.append(pair)
                term = pair * (side_temp - here)
                total = term if total is None else total + term
            pair = own + pltpu.roll(own, end, 1)
            pairs.append(pair)
            flow = jnp.where(lane == end, 0.0, pair * (pltpu.roll(here, end, 1) - here))
            total = total + (flow - pltpu.roll(flow, 1, 1))
            if inflow is not None:
                total = total + entering(inflow, z, at, lane)
            emit(z, start, first, here + (0.5 * STEP_RATE) * total, pairs)

    plane(0, True)

    def later(z, nothing):
        plane(z, False)
        return nothing

    lax.fori_loop(1, depth, later, 0)


def inflow_rows(s_ref, packs, near_x, far_x, flow, depth):
    own = lambda kind, k: column(packs, depth, kind, k)
    side = lambda kind, k, left: side_columns(s_ref, near_x, far_x, depth, kind, k, left)
    left_pair = own(1, 2) + side(1, 1, True)
    right_pair = own(1, 1) + side(1, 2, False)
    interleave(
        flow,
        left_pair * (side(0, 1, True) - own(0, 2)),
        right_pair * (side(0, 2, False) - own(0, 1)),
    )
    return left_pair, right_pair


def base_emit(temp, gas, out):
    def emit(z, start, first, value, pairs):
        at = slice(start, start + CHUNK)
        if first:
            value = value + (STEP_RATE * HEAT_TRANSFER) * (gas[at] - temp[0, at])
        out[z, at] = value

    return emit


def inner_body(s_ref, temp, cond, gas, out):
    rows = temp.shape[1]
    step_planes(
        temp, cond, None, None, None, None, None, base_emit(temp, gas, out),
        range(CHUNK, rows - CHUNK, CHUNK),
    )


def tile_rims(mine, near_x, far_x, along, lines, depth, width, side):
    last = 8 * depth
    own = lambda k: tuple(column(mine, depth, kind, k) for kind in range(2))
    left = lambda k: tuple(side(depth, kind, k, True) for kind in range(2))
    right = lambda k: tuple(side(depth, kind, k, False) for kind in range(2))
    zero = jnp.zeros((depth, 1), jnp.float32)
    if lines is None:
        corner = lambda which, spot: (zero, zero)
        at_lane = lambda pair, lane: (zero, zero)
        up_line = down_line = None
    else:
        line = lambda ref, k: tuple(
            ref[4 * depth * kind + depth * k : 4 * depth * kind + depth * (k + 1)] for kind in range(2)
        )
        corner = lambda which, spot: tuple(
            lines[which, last + 8 :][:, at : at + 1] for at in (spot, spot + 2)
        )
        at_lane = lambda pair, lane: tuple(v[:, lane : lane + 1] for v in pair)
        up_line, down_line = line(lines.at[0], 1), line(lines.at[1], 2)
    gas_left, gas_right = side.gas
    out_left = rim(*left(1), left(0), own(2), corner(0, 0), corner(1, 4), gas_left)
    out_right = rim(*right(2), right(3), own(1), corner(0, 1), corner(1, 5), gas_right)
    in_left = rim(
        *own(2), left(1), own(3), at_lane(up_line, 0), at_lane(down_line, 0), flat(mine, last + 2)
    )
    in_right = rim(
        *own(1), right(2), own(0), at_lane(up_line, width - 1), at_lane(down_line, width - 1),
        flat(mine, last + 1),
    )
    if lines is None:
        return out_left - in_left, out_right - in_right, None, None
    upper = rim(
        *up_line, line(lines.at[0], 0), line(along, 2), corner(0, 0), corner(0, 1),
        lines[0, last + 1 : last + 2],
    )
    lower = rim(
        *down_line, line(lines.at[1], 3), line(along, 1), corner(1, 4), corner(1, 5),
        lines[1, last + 2 : last + 3],
    )
    return out_left - in_left, out_right - in_right, upper, lower


class Sides:
    def __init__(self, s_ref, near_x, far_x, depth):
        self.s_ref, self.near_x, self.far_x = s_ref, near_x, far_x
        last = 8 * depth
        even = s_ref[8] == 0
        self.gas = (
            jnp.where(even, flat(far_x, last + 1), flat(near_x, last + 1)),
            jnp.where(even, flat(near_x, last + 2), flat(far_x, last + 2)),
        )

    def __call__(self, depth, kind, k, left):
        return side_columns(self.s_ref, self.near_x, self.far_x, depth, kind, k, left)


def final_emit(temp, gas, face, held, weights, done):
    rows, width = held.shape[1:]
    lane = lax.broadcasted_iota(jnp.int32, (CHUNK, width), 1)
    end = width - 1

    def emit(z, start, first, value, pairs):
        at = slice(start, start + CHUNK)
        if first:
            value = value + (STEP_RATE * HEAT_TRANSFER) * (gas[at] - temp[0, at])
            edge = pltpu.roll(face[at], end, 1)
            across = pairs[4]
            left = jnp.where(lane == 0, edge, pltpu.roll(across, 1, 1))
            right = jnp.where(lane == end, edge, across)
            for k, pair in enumerate((pairs[0], pairs[1], left, right, pairs[3])):
                weights[k, at] = (0.5 * STEP_RATE) * pair
        held[z, at] = value
        done(z, start, first)

    return emit


def middle_body(
    s_ref, base_in, temp, cond, gas, packs, mixed, far, base, held, weights,
    packed, flow, inflow, face,
):
    depth, rows, width = temp.shape
    lane = lax.broadcasted_iota(jnp.int32, (CHUNK, width), 1)
    mine, near_x, far_x = sources(packs, mixed, far, depth)
    left_pair, right_pair = inflow_rows(s_ref, mine, near_x, far_x, flow, depth)
    packed[...] = jnp.zeros_like(packed)
    inflow[...] = to_columns(packed, flow)

    def mend(z, nothing):
        for start in range(CHUNK, rows - CHUNK, CHUNK):
            at = slice(start, start + CHUNK)
            base[z, at] = base_in[z, at] + (0.5 * STEP_RATE) * entering(inflow, z, at, lane)
        return nothing

    lax.fori_loop(0, depth, mend, 0)
    side = Sides(s_ref, near_x, far_x, depth)
    left_step, right_step, _, _ = tile_rims(mine, near_x, far_x, None, None, depth, width, side)
    interleave(flow, left_pair * left_step, right_pair * right_step)
    inflow[...] = to_columns(packed, flow)
    interleave(flow, left_pair, right_pair)
    face[...] = to_columns(packed, flow)
    step_planes(
        base, cond, None, None, None, None, inflow,
        final_emit(temp, gas, face, held, weights, lambda z, start, first: None),
        range(2 * CHUNK, rows - 2 * CHUNK, CHUNK),
    )


def outer_body(
    s_ref, base_in, held_in, weights_in, temp, cond, gas, packs, along, mixed, far, near_y, far_y,
    base, held, weights, out, top, sems, packed, flow, inflow, face, lines, base_lines,
):
    depth, rows, width = temp.shape
    settle(s_ref, lines, near_y, far_y)
    mine, near_x, far_x = sources(packs, mixed, far, depth)
    left_pair, right_pair = inflow_rows(s_ref, mine, near_x, far_x, flow, depth)
    packed[...] = jnp.zeros_like(packed)
    inflow[...] = to_columns(packed, flow)
    side = Sides(s_ref, near_x, far_x, depth)
    left_step, right_step, base_lines[0], base_lines[1] = tile_rims(
        mine, near_x, far_x, along, lines, depth, width, side
    )
    span = lambda which, kind, k: lines.at[
        which, 4 * depth * kind + depth * k : 4 * depth * kind + depth * (k + 1)
    ]
    cond_up, cond_down = span(0, 1, 1), span(1, 1, 2)
    step_planes(
        temp, cond, span(0, 0, 1), span(1, 0, 2), cond_up, cond_down, inflow,
        base_emit(temp, gas, base), (0, rows - CHUNK),
    )
    interleave(flow, left_pair * left_step, right_pair * right_step)
    inflow[...] = to_columns(packed, flow)
    interleave(flow, left_pair, right_pair)
    face[...] = to_columns(packed, flow)

    def done(z, start, first):
        if not first and start + CHUNK == rows:

            @pl.when(z >= 2)
            def _():
                pltpu.make_async_copy(held.at[z], out.at[z], sems.at[z]).start()

    step_planes(
        base, cond, base_lines.at[0], base_lines.at[1], cond_up, cond_down, inflow,
        final_emit(temp, gas, face, held, weights, done),
        (0, CHUNK, rows - 2 * CHUNK, rows - CHUNK),
    )
    top[...] = held[:2]
    for z in range(2, depth):
        pltpu.make_async_copy(held.at[z], out.at[z], sems.at[z]).wait()


def faces(value, row, lane, up, down, left, right):
    rows, width = value.shape
    return (
        jnp.where(row == 0, up, pltpu.roll(value, 1, 0)),
        jnp.where(row == rows - 1, down, pltpu.roll(value, rows - 1, 0)),
        jnp.where(lane == 0, left, pltpu.roll(value, 1, 1)),
        jnp.where(lane == width - 1, right, pltpu.roll(value, width - 1, 1)),
    )


def finish_body(
    s_ref, ours, theirs, weights, base, mine, came, filled, pressure, out, held, sem, joined, sems
):
    half = ours.shape[0]
    rows, width = weights.shape[1:]
    sign = (1 - 2 * s_ref[0]).astype(jnp.float32)
    bottom = (1 - 2 * s_ref[3]).astype(jnp.float32)
    second = s_ref[4] == 1
    factor = STEP_RATE * HEAT_TRANSFER * PRESSURE_WORK

    def lines(start, count, minus):
        our_sign = jnp.where(s_ref[0] == 0, 1.0, minus) * factor
        their_sign = jnp.where(s_ref[0] == 0, minus, 1.0) * factor
        at = pl.ds(start, count)
        return our_sign * ours[at] + their_sign * theirs[at]

    begin = pl.multiple_of(s_ref[4] * rows, rows)
    middle = lines(begin, rows, bottom)
    above = lines(jnp.where(second, rows - 1, half - 1), 1, jnp.where(second, bottom, -bottom))
    below = lines(jnp.where(second, 0, rows), 1, jnp.where(second, -bottom, bottom))
    share = middle[:, :width]
    row = lax.broadcasted_iota(jnp.int32, (rows, width), 0)
    lane = lax.broadcasted_iota(jnp.int32, (rows, width), 1)
    around = faces(
        share, row, lane, above[:, :width], below[:, :width],
        middle[:, width : width + 1], middle[:, width + 1 : width + 2],
    )
    added = 2.0 * share
    for k in range(4):
        added = added + weights[k] * (around[k] - share)
    down = weights[4] * share
    held[0] = base[0] + added - down
    held[1] = base[1] + down
    copy = pltpu.make_async_copy(held, out.at[:2], sem)
    copy.start()
    for other in join_planes(s_ref, mine, came, pressure, joined, sems):
        other.wait()
    copy.wait()


def mover(groups, pencils):
    def move(value, target):
        pairs = []
        for g in range(groups):
            for p in range(pencils):
                to = target(g, p)
                pairs.append((g * pencils + p, to[0] * pencils + to[1]))
        return lax.ppermute(value, ("grp", "pen"), pairs)

    return move


def per_device(pressure_source, solid_temp, gas_wall_temp, phase_map, phase_conductivity):
    groups = lax.axis_size("grp")
    pencils = lax.axis_size("pen")
    group_idx = lax.axis_index("grp")
    pencil_idx = lax.axis_index("pen")
    depth_loc, span_len, width = pressure_source.shape
    depth = depth_loc * groups
    half = span_len // 2
    own = depth // 2
    core = group_idx % 2
    low = group_idx // 2
    zi = pencil_idx % Z_RING
    yl = pencil_idx // Z_RING % Y_PAIR
    place = pencil_idx % (Z_RING * Y_PAIR)
    move = mover(groups, pencils)
    tab = make_tables(span_len, width, depth)
    const = {k: tuple(map(jnp.asarray, v)) if isinstance(v, tuple) else jnp.asarray(v) for k, v in tab.items()}
    code = jnp.where(low == 0, core * 4, 7 - 4 * core)
    scalars = jnp.stack([core, low, code, low, core, zi, yl, place, pencil_idx % 2]).astype(jnp.int32)
    span = list(const["span"])
    into = list(const["into"])
    back = list(const["back"])
    span_t = list(const["span_t"])
    tile_rows = span_len // groups
    flip = lambda mask: lambda g, p: (g ^ mask, p)
    near_pair = lambda g, p: (g, p ^ 1)
    far_pair = lambda g, p: (g, (p + 1 if p % 2 else p - 1) % pencils)

    other_core = lambda g, p: (g ^ 1, p)
    other_half = lambda g, p: (g ^ 2, p)
    halves_of = tile_rows // 128
    column_scratch = pltpu.VMEM((tile_rows, width), jnp.float32)
    row_scratch = pltpu.VMEM((width, tile_rows), jnp.float32)
    (pivots,) = run(
        pivot_body, 1.2, scalars, [], [const["lam"], const["sigma"]], [(3 * own + 2, width, half)]
    )
    folded = jax.ShapeDtypeStruct((depth_loc, half, width), jnp.float32)
    away, kept = run_blocks(
        fold_body, 0.8, scalars, [pivots, pressure_source], [ORDER, plane_of(pressure_source)],
        [folded.shape, folded.shape], [plane_of(folded), plane_of(folded)], depth_loc,
    )
    arrived = move(away, other_core)
    (held,) = run(
        held_body, 2.1, scalars, [], [kept, *into, *span], [(depth_loc, width, half)]
    )
    cond, packs, along = run(
        edge_body, 2.8, scalars, [held], [solid_temp, phase_map, gas_wall_temp],
        [(depth, tile_rows, width), (halves_of * (8 * depth + 8), 128), (8 * depth + 8, width)],
        scratch=[column_scratch], small=[phase_conductivity],
    )
    planes, edges, carried, opening, mixed = run(
        arrived_body, 3.4, scalars, [],
        [arrived, held, *into, *span, pivots, const["edge"], const["basis_t"], const["far"],
         packs],
        [(own, width, half), (2, depth, half), (width, half), (width, half),
         (2 * depth * half // 128 + packs.shape[0], 128)],
        scratch=[pltpu.VMEM((2, depth, 8, half), jnp.float32)],
    )
    mixed = move(mixed, near_pair)
    z_got = [move(edges, lambda g, p, d=d: (g, p ^ d)) for d in range(2, Z_RING)]
    far_x = move(packs, far_pair)
    carried_there = move(carried, other_half)
    log_rho = const["log_rho"]
    pair_shape = edges.shape
    (base,) = run(
        inner_body, 4.5, scalars, [edges], [solid_temp, cond, gas_wall_temp],
        [(depth, tile_rows, width)],
    )
    four, two = run(
        functools.partial(z_body, width=width), 0.6, scalars, [far_x, carried_there, base],
        [edges, mixed, *z_got, log_rho], [(4,) + pair_shape[1:], pair_shape],
    )
    there = move(four, other_half)
    beside1 = move(two, lambda g, p: (g, p ^ Z_RING))
    beside2 = move(two, lambda g, p: (g ^ 2, p ^ Z_RING))
    (lines,) = run(
        corner_body, 0.6, scalars, [two], [along, packs, mixed, far_x], [(9 * depth + 8, width)]
    )
    near_y = [move(lines, flip(1)), move(lines, flip(3))]
    flow_scratch = pltpu.VMEM((halves_of, 2 * depth, 128), jnp.float32)
    tile = (depth, tile_rows, width)
    base, begun, weights = run(
        middle_body, 4.5, scalars, [lines],
        [base, solid_temp, cond, gas_wall_temp, packs, mixed, far_x],
        [tile, tile, (5, tile_rows, width)],
        scratch=[row_scratch, flow_scratch, column_scratch, column_scratch],
        aliases={2: 0},
    )
    run8, part, opening = run(
        functools.partial(y_body, width=width), 0.6, scalars, [base, *near_y],
        [four, there, beside1, beside2, log_rho, opening], [pair_shape, pair_shape, opening.shape],
    )
    block = Z_RING * Y_PAIR
    opening_there = move(opening, other_half)
    x_got = [move(run8, lambda g, p, d=d: (g, (p + block * d) % pencils)) for d in range(1, X_RING)]
    _, _, weights, final, top = run(
        outer_body, 5.5, scalars, [run8],
        [base, begun, weights, solid_temp, cond, gas_wall_temp, packs, along, mixed, far_x, *near_y],
        [tile, tile, (5, tile_rows, width), solid_temp.shape, (2, tile_rows, width)],
        scratch=[
            pltpu.SemaphoreType.DMA((depth,)),
            row_scratch, flow_scratch, column_scratch, column_scratch,
            pltpu.VMEM((2, 9 * depth + 8, width), jnp.float32),
            pltpu.VMEM((2, depth, width), jnp.float32),
        ],
        out_specs=[FAST, FAST, FAST, ORDER, FAST], aliases={2: 0, 3: 1, 4: 2},
    )
    wall, away, keep = run(
        solve_body, 6.9, scalars, [weights],
        [planes, carried_there, opening_there, run8, part, *x_got, log_rho, pivots, *span_t, *back,
         const["edge"], const["basis"]],
        [(half, 2 * width), (depth_loc, half, width), (depth_loc, width, half)],
        scratch=[
            pltpu.VMEM((own, width, half), jnp.float32),
            pltpu.VMEM((2, depth, half), jnp.float32),
            pltpu.VMEM((2 * width, half), jnp.float32),
        ],
    )
    wall_came = move(wall, other_core)
    came = move(away, other_core)
    (mine,) = run(cells_body, 2.2, scalars, [], [keep, *span_t, *back], [(depth_loc, half, width)])
    pressure, final = run(
        finish_body, 2.5, scalars, [], [wall, wall_came, weights, top, mine, came, (final, ORDER)],
        [pressure_source.shape, final.shape],
        scratch=[
            pltpu.VMEM(top.shape, jnp.float32), pltpu.SemaphoreType.DMA,
            pltpu.VMEM(pressure_source.shape, jnp.float32), pltpu.SemaphoreType.DMA((depth_loc,)),
        ],
        out_specs=[ORDER, ORDER], aliases={7: 1},
    )
    return (pressure, final)


def solution(mesh):
    in_specs = (
        P("grp", None, "pen"),
        P(None, "grp", "pen"),
        P("grp", "pen"),
        P(None, "grp", "pen"),
        P(),
    )
    out_specs = (P("grp", None, "pen"), P(None, "grp", "pen"))
    return jax.shard_map(
        per_device, mesh=mesh, in_specs=in_specs, out_specs=out_specs, check_vma=False
    )
```

```python
import functools
import math

import jax
import jax.numpy as jnp
import numpy as np
from jax import lax
from jax.experimental import pallas as pl
from jax.experimental.pallas import tpu as pltpu
from jax.sharding import PartitionSpec as P

HIGHEST = lax.Precision.HIGHEST
HEAT_TRANSFER = 1.0
PRESSURE_WORK = 0.5
STEP_RATE = 0.12
Z_RING, Y_PAIR, X_RING = 4, 2, 4
VMEM_LIMIT = 18 * 1024 * 1024
BLOCK_LIMIT = 16 * 1024 * 1024
LANES = 128
CHUNK = 32
RIM = 32
MIDDLE = 64
COST_SCALE = 0.1


def halves(value):
    high = np.asarray(value, np.float32).astype(jnp.bfloat16)
    low = (np.asarray(value, np.float64) - high.astype(np.float64)).astype(jnp.bfloat16)
    return high, low


def make_tables(span_len, width, depth):
    half = span_len // 2
    waves = np.stack([2 * np.arange(half), 2 * np.arange(half) + 1]).astype(np.float64)
    rows = np.arange(half)
    angle = 2 * np.pi * ((rows[None, :, None] * waves[:, None, :]) % span_len) / span_len
    span = np.cos(angle) + np.sin(angle)
    lam = -4 * np.sin(np.pi * waves / span_len) ** 2
    order = np.concatenate([np.arange(0, width, 2), np.arange(1, width, 2)]) + 1.0
    cells = np.arange(width) + 1.0
    sine = np.sqrt(2 / (width + 1)) * np.sin(np.pi * cells[:, None] * order[None, :] / (width + 1))
    sigma = -4 * np.sin(np.pi * order / (2 * (width + 1))) ** 2
    modes = np.arange(depth)
    theta = np.pi * (2 * modes + 1) / (2 * depth + 1)
    basis = np.cos(theta[None, :] * (np.arange(depth)[:, None] + 0.5)) / np.sqrt((2 * depth + 1) / 4)
    mu = -4 * np.sin(theta / 2) ** 2
    stretch = -(mu[None, :, None] + lam[:, None, :])
    log_rho = -2 * np.arcsinh(np.sqrt(stretch) / 2)
    down = np.arange(depth // 2)
    up = depth - 1 - down
    ordered = np.stack([basis[np.concatenate([down, up])], basis[np.concatenate([up, down])]])
    pair = np.kron(np.eye(2), sine)
    f32 = lambda v: np.asarray(v, np.float32)
    lanes = min(LANES, half)
    return {
        "span": halves(span),
        "span_t": halves(np.swapaxes(span, 1, 2)),
        "into": halves(pair / span_len),
        "back": halves(pair.T),
        "lam": f32(lam)[:, None, :],
        "sigma": f32(np.repeat(sigma[:, None], lanes, 1)),
        "edge": f32(np.repeat(sine[0][:, None], lanes, 1)),
        "basis": f32(ordered),
        "basis_t": f32(np.swapaxes(ordered, 1, 2)),
        "log_rho": f32(log_rho),
        "far": f32(np.exp(log_rho * (width + 1))),
    }


def product(first, second):
    return jnp.dot(first, second, preferred_element_type=jnp.float32)


def split(value):
    high = value.astype(jnp.bfloat16)
    return high, (value - high.astype(jnp.float32)).astype(jnp.bfloat16)


def times(value, high, low):
    value_high, value_low = split(value)
    return product(value_high, high) + (product(value_high, low) + product(value_low, high))


def times_turned(high, low, value):
    value_high, value_low = split(value)
    turned = lambda a, b: lax.dot_general(
        a, b, (((1,), (1,)), ((), ())), preferred_element_type=jnp.float32
    )
    return turned(high, value_high) + (turned(low, value_high) + turned(high, value_low))


ORDER = pl.BlockSpec(memory_space=pl.ANY)
SCALARS = pl.BlockSpec(memory_space=pltpu.SMEM)
FAST = pl.BlockSpec(memory_space=pltpu.VMEM)


def plane_of(array):
    rest = array.shape[1:]
    return pl.BlockSpec((1,) + rest, lambda i, s: (i,) + (0,) * len(rest))


def cost(time_us):
    return pl.CostEstimate(flops=1, bytes_accessed=int(time_us * 3.69e6 * COST_SCALE), transcendentals=0)


def run(body, time_us, scalars, ordered, arrays, outs, scratch=(), small=(), out_specs=None, aliases=None):
    outs = [jax.ShapeDtypeStruct(shape, jnp.float32) for shape in outs]
    skip = len(ordered)
    count = len(small)
    kinds = [FAST if spec is None else spec for spec in (a[1] if type(a) is tuple else None for a in arrays)]
    arrays = [a[0] if type(a) is tuple else a for a in arrays]
    specs = [SCALARS] + [SCALARS] * count + [ORDER] * skip + kinds

    def inner(s_ref, *refs):
        body(s_ref, *refs[:count], *refs[count + skip :])

    return pl.pallas_call(
        inner,
        out_shape=outs,
        in_specs=specs,
        out_specs=out_specs or [FAST] * len(outs),
        scratch_shapes=list(scratch),
        input_output_aliases=aliases or {},
        compiler_params=pltpu.CompilerParams(vmem_limit_bytes=VMEM_LIMIT),
        cost_estimate=cost(time_us),
    )(scalars, *small, *ordered, *arrays)


def run_blocks(body, time_us, scalars, arrays, specs, outs, out_specs, steps):
    return pl.pallas_call(
        body,
        out_shape=[jax.ShapeDtypeStruct(out, jnp.float32) for out in outs],
        grid_spec=pltpu.PrefetchScalarGridSpec(
            num_scalar_prefetch=1, grid=(steps,), in_specs=specs, out_specs=out_specs
        ),
        compiler_params=pltpu.CompilerParams(vmem_limit_bytes=BLOCK_LIMIT),
        cost_estimate=cost(time_us),
    )(scalars, *arrays)


def fold_body(s_ref, after, source, away, kept):
    half = source.shape[1] // 2
    sign = (1 - 2 * s_ref[0]).astype(jnp.float32)
    upper = source[:, :half]
    lower = sign * source[:, half:]
    away[...] = upper - lower
    kept[...] = upper + lower


def spectral(planes, into_high, into_low, span_high, span_low):
    turned = []
    for pair in range(0, len(planes), 2):
        cells = jnp.concatenate(planes[pair : pair + 2], axis=1)
        turned.append(times(cells, into_high, into_low).T)
    return times(jnp.concatenate(turned, axis=0), span_high, span_low)


def held_body(s_ref, kept, into_high, into_low, span_high, span_low, out):
    out[...] = spectral(
        [kept[z] for z in range(kept.shape[0])], into_high[...], into_low[...],
        span_high[s_ref[0]], span_low[s_ref[0]],
    ).reshape(out.shape)


def across(value, length):
    return jnp.concatenate([value] * (length // value.shape[1]), axis=1)


def continuants(centre, first, count):
    values = [jnp.ones_like(centre), centre + first]
    for _ in range(1, count):
        values.append(centre * values[-1] - values[-2])
    return values


def pivot_body(s_ref, lam, sigma, out):
    own = (out.shape[0] - 2) // 3
    width = out.shape[1]
    low = s_ref[1].astype(jnp.float32)

    def tile(group, nothing):
        rows = pl.ds(pl.multiple_of(group * 8, 8), 8)
        centre = lam[s_ref[0]] + across(sigma[rows], out.shape[2]) - 2.0
        mine = continuants(centre, 1.0 - low, own)
        other = continuants(centre, low, own)
        for i in range(own):
            out[i, rows] = mine[i + 1]
            out[own + i, rows] = other[i + 1]
            out[2 * own + i, rows] = 1.0 / mine[i + 1]
        out[3 * own, rows] = 1.0 / (mine[own] * other[own] - mine[own - 1] * other[own - 1])
        out[3 * own + 1, rows] = 1.0 / other[own]
        return nothing

    lax.fori_loop(0, width // 8, tile, 0)


def arrived_body(
    s_ref, arrived, held, into_high, into_low, span_high, span_low, pivots, edge, basis_t, far, packs,
    planes, edges, carried, opening, mixed, sums,
):
    count = held.shape[0]
    own = 2 * count
    width, half = held.shape[1:]
    planes[:count] = held[...]
    planes[count:] = spectral(
        [arrived[z] for z in range(count)], into_high[...], into_low[...],
        span_high[s_ref[0]], span_low[s_ref[0]],
    ).reshape(held.shape)
    sums[...] = jnp.zeros_like(sums)
    code = s_ref[2]
    side = width // 16

    def tile(group, nothing):
        rows = pl.ds(pl.multiple_of(group * 8, 8), 8)
        parity = group // side
        carry = planes[code, rows]
        carries = [carry]
        for i in range(1, own):
            carry = pivots[i - 1, rows] * planes[jnp.bitwise_xor(i, code), rows] - carry
            carries.append(carry)
        carried[rows] = carry
        shared = carry * pivots[3 * own, rows]
        scale = across(edge[rows], half)
        value = shared * pivots[2 * own - 1, rows]
        sums[parity, own - 1] += scale * value
        for i in range(own - 2, -1, -1):
            step = value if i == 0 else pivots[i - 1, rows] * value
            value = (carries[i] - step) * pivots[2 * own + i, rows]
            sums[parity, i] += scale * value
        opening[rows] = value + pivots[2 * own - 2, rows] * shared * pivots[3 * own - 1, rows]
        shared = scale * shared
        for i in range(own):
            term = shared if i == 0 else pivots[own + i - 1, rows] * shared
            sums[parity, own + i] += term if (own - i) % 2 == 0 else -term
        return nothing

    lax.fori_loop(0, width // 8, tile, 0)
    total = jnp.sum(sums[...], axis=2)
    modal = lambda v: jnp.dot(
        basis_t[s_ref[1]], v, precision=HIGHEST, preferred_element_type=jnp.float32
    )
    even = modal(total[0])
    odd = modal(total[1])
    edge_low = even + odd
    edge_high = even - odd
    right = edge_high + far[s_ref[0]] * edge_low
    left = edge_low + far[s_ref[0]] * edge_high
    edges[0] = right
    edges[1] = left
    at = 0
    for value in (right, left):
        for _, lanes in pieces(half):
            mixed[at : at + value.shape[0]] = value[:, lanes]
            at += value.shape[0]
    mixed[at:] = packs[...]


def powers(s_ref, log_rho):
    rate = log_rho[s_ref[0]]
    return lambda n: jnp.exp(rate * n)


def scalar(value):
    return value.astype(jnp.float32)


def z_body(s_ref, edges, mixed, got2, got3, log_rho, four, two, *, width):
    power = powers(s_ref, log_rho)
    zi = s_ref[5]
    wide = float(width)
    right, left = edges[0], edges[1]
    low_sum = jnp.zeros_like(right)
    high_sum = jnp.zeros_like(right)
    right4 = power(wide * scalar(Z_RING - 1 - zi)) * right
    left4 = power(wide * scalar(zi)) * left
    size = right.shape[0]
    lanes = mixed.shape[1]
    pieces_of = right.shape[1] // lanes
    first_right, first_left = (
        jnp.concatenate(
            [mixed[(k * pieces_of + c) * size : (k * pieces_of + c + 1) * size] for c in range(pieces_of)],
            axis=1,
        )
        for k in range(2)
    )
    for d, got_right, got_left in (
        (1, first_right, first_left), (2, got2[0], got2[1]), (3, got3[0], got3[1])
    ):
        source = jnp.bitwise_xor(zi, d)
        before = scalar(source < zi)
        gap = jnp.maximum(zi - source, source - zi) - 1
        step = power(wide * scalar(gap))
        low_sum = low_sum + before * step * got_right
        high_sum = high_sum + (1.0 - before) * step * got_left
        right4 = right4 + power(wide * scalar(Z_RING - 1 - source)) * got_right
        left4 = left4 + power(wide * scalar(source)) * got_left
    hop = power(wide)
    per_rho = power(-1.0)
    four[0] = per_rho * low_sum + left + hop * high_sum
    four[1] = per_rho * high_sum + right + hop * low_sum
    four[2] = right4
    four[3] = left4
    two[0] = right4
    two[1] = left4


def y_body(s_ref, four, there, beside1, beside2, log_rho, opening, run8, part, passed, *, width):
    passed[...] = opening[...]
    power = powers(s_ref, log_rho)
    zi = s_ref[5]
    wide = float(width)
    behind = scalar(s_ref[6])
    other0 = beside1[0] + beside2[0]
    other1 = beside1[1] + beside2[1]
    right4 = four[2] + there[2]
    left4 = four[3] + there[3]
    low_sum = behind * power(wide * scalar(zi)) * other0
    high_sum = (1.0 - behind) * power(wide * scalar(Z_RING - 1 - zi)) * other1
    run4 = power(wide * Z_RING)
    is_behind = s_ref[6] == 1
    run8[0] = jnp.where(is_behind, run4 * other0 + right4, run4 * right4 + other0)
    run8[1] = jnp.where(is_behind, other1 + run4 * left4, left4 + run4 * other1)
    hop = power(wide)
    per_rho = power(-1.0)
    part[0] = four[0] + there[0] + per_rho * low_sum + hop * high_sum
    part[1] = four[1] + there[1] + per_rho * high_sum + hop * low_sum


def x_sums(s_ref, run8, part, gots, log_rho, width):
    power = powers(s_ref, log_rho)
    wide = float(width)
    block = Z_RING * Y_PAIR
    right_sum = power(wide * block * (X_RING - 1)) * run8[0]
    left_sum = power(wide * block * (X_RING - 1)) * run8[1]
    for d, got in enumerate(gots, 1):
        right_sum = right_sum + power(wide * block * (d - 1)) * got[0]
        left_sum = left_sum + power(wide * block * (X_RING - 1 - d)) * got[1]
    periodic = 1.0 / (1.0 - power(wide * block * X_RING))
    low_sum = power(wide * scalar(s_ref[7])) * right_sum * periodic
    high_sum = power(wide * scalar(block - 1 - s_ref[7])) * left_sum * periodic
    rho = power(1.0)
    per_rho = power(-1.0)
    hop = power(wide)
    gain = rho / (1.0 - rho * rho)
    into_low = gain * (part[0] + per_rho * low_sum + hop * high_sum)
    into_high = gain * (part[1] + per_rho * high_sum + hop * low_sum)
    return into_low, into_high


def to_cells(values, span_t_high, span_t_low, back_high, back_low):
    lines = times(values, span_t_high, span_t_low)
    size = back_high.shape[0]
    return [
        times(lines[at : at + size].T, back_high, back_low) for at in range(0, lines.shape[0], size)
    ]


def solve_body(
    s_ref, planes, carried, opening, run8, part, got1, got2, got3, log_rho, pivots,
    span_t_high, span_t_low, back_high, back_low, edge, basis,
    wall, away, keep, solved, both, first,
):
    own, width, half = planes.shape
    count = own // 2
    is_low = s_ref[1] == 1
    code = s_ref[2]
    depthwise = lambda v: jnp.dot(
        basis[s_ref[1]], v, precision=HIGHEST, preferred_element_type=jnp.float32
    )
    into_low, into_high = x_sums(s_ref, run8, part, (got1, got2, got3), log_rho, width)
    gain_low = depthwise(into_low)
    gain_high = depthwise(into_high)
    both[0] = gain_low + gain_high
    both[1] = gain_low - gain_high
    first[width:] = jnp.zeros_like(first[width:])
    first[width : width + 1] = jnp.where(is_low, gain_low[own : own + 1], gain_low[:1])
    first[width + 1 : width + 2] = jnp.where(is_low, gain_high[own : own + 1], gain_high[:1])
    side = width // 16

    def tile(group, nothing):
        rows = pl.ds(pl.multiple_of(group * 8, 8), 8)
        parity = group // side
        scale = across(edge[rows], half)
        rhs = lambda i: scale * both[parity, i : i + 1]
        mine = lambda i: pivots[i - 1, rows]
        other = lambda i: pivots[own + i - 1, rows]
        carry = planes[code, rows] - rhs(0)
        carries = [carry]
        for i in range(1, own):
            carry = mine(i) * (planes[jnp.bitwise_xor(i, code), rows] - rhs(i)) - carry
            carries.append(carry)
        right = rhs(own)
        total = -right
        direct = -mine(own - 1) * right
        for i in range(1, own):
            right = rhs(own + i)
            total = -other(i) * right - total
            term = right if i == own - 1 else mine(own - 1 - i) * right
            direct = direct - term if i % 2 == 0 else direct + term
        total = total + carried[rows]
        value = (carry * other(own) - mine(own - 1) * total) * pivots[3 * own, rows]
        far_first = opening[rows] + (direct + value) * pivots[3 * own + 1, rows]
        solved[jnp.bitwise_xor(own - 1, code), rows] = value
        for i in range(own - 2, -1, -1):
            step = value if i == 0 else mine(i) * value
            value = (carries[i] - step) * pivots[2 * own + i, rows]
            solved[jnp.bitwise_xor(i, code), rows] = value
        first[rows] = jnp.where(is_low, far_first, value)
        return nothing

    lax.fori_loop(0, width // 8, tile, 0)
    table_high = span_t_high[s_ref[0]]
    table_low = span_t_low[s_ref[0]]
    line = times(first[...], table_high, table_low).T
    main = times(line[:, :width], back_high[:width, :width], back_low[:width, :width])
    wall[...] = jnp.concatenate([main, line[:, width:]], axis=1)
    values = solved[count:].reshape(count * width, half)
    for k, cells in enumerate(to_cells(values, table_high, table_low, back_high[...], back_low[...])):
        away[2 * k] = cells[:, :width]
        away[2 * k + 1] = cells[:, width:]
    keep[...] = solved[:count]


def cells_body(s_ref, keep, span_t_high, span_t_low, back_high, back_low, mine):
    count, width, half = keep.shape
    values = keep[...].reshape(count * width, half)
    pairs = to_cells(
        values, span_t_high[s_ref[0]], span_t_low[s_ref[0]], back_high[...], back_low[...]
    )
    for k, cells in enumerate(pairs):
        mine[2 * k] = cells[:, :width]
        mine[2 * k + 1] = cells[:, width:]


def join_planes(s_ref, mine, came, out, held, sems):
    half = mine.shape[1]
    sign = (1 - 2 * s_ref[0]).astype(jnp.float32)
    copies = []
    for z in range(mine.shape[0]):
        ours = mine[z]
        theirs = came[z]
        held[z, :half] = ours + theirs
        held[z, half:] = sign * (ours - theirs)
        copy = pltpu.make_async_copy(held.at[z], out.at[z], sems.at[z])
        copy.start()
        copies.append(copy)
    return copies


def edge_body(s_ref, conductivity, temp, phase, gas, cond, packs, along, packed):
    depth, rows, width = temp.shape
    lane = lax.broadcasted_iota(jnp.int32, (CHUNK, width), 1)
    cold, warm = conductivity[0], conductivity[1]
    packed[...] = jnp.zeros_like(packed)

    def plane(z, nothing):
        for start in range(0, rows, CHUNK):
            at = slice(start, start + CHUNK)
            kept = packed[at]
            value = jnp.where(phase[z, at] == 1, warm, cold)
            cond[z, at] = value
            for k, part in enumerate((temp[z, at], value)):
                spot = 4 * (k * depth + z)
                chosen_lane = (lane >= spot) & (lane < spot + 4)
                kept = jnp.where(chosen_lane, pltpu.roll(part, spot + 2, 1), kept)
                line = 4 * depth * k + z
                if start == 0:
                    along[pl.ds(line + 2 * depth, 1)] = part[:1]
                    along[pl.ds(line + 3 * depth, 1)] = part[1:2]
                if start + CHUNK == rows:
                    along[pl.ds(line, 1)] = part[CHUNK - 2 : CHUNK - 1]
                    along[pl.ds(line + depth, 1)] = part[CHUNK - 1 :]
            packed[at] = kept
        return nothing

    lax.fori_loop(0, depth, plane, 0)
    last = 8 * depth
    turned = packed[...].T
    turned_gas = pltpu.roll(gas[...], 2, 1).T[:8]
    for h, at in pieces(rows):
        base = h * (last + 8)
        packs[base : base + last] = turned[:, at]
        packs[base + last : base + last + 8] = turned_gas[:, at]
    along[last : last + 8] = jnp.concatenate(
        [gas[rows - 2 :], gas[:2], jnp.zeros((4, width), jnp.float32)], axis=0
    )


def pieces(length):
    return [(h, slice(h * 128, h * 128 + 128)) for h in range(length // 128)]


def column(source, depth, kind, k):
    ref, base, size = source
    at = lambda h: pl.ds(base + h * size + 4 * depth * kind + k, depth, stride=4)
    return jnp.concatenate([ref[at(h)] for h in range((ref.shape[0] - base) // size)], axis=1)


def flat(source, row):
    ref, base, size = source
    at = lambda h: base + h * size + row
    count = (ref.shape[0] - base) // size
    return jnp.concatenate([ref[at(h) : at(h) + 1] for h in range(count)], axis=1)


def sources(packs, mixed, far_x, depth):
    size = 8 * depth + 8
    return (packs, 0, size), (mixed, mixed.shape[0] - packs.shape[0], size), (far_x, 0, size)


def interleave(ref, odd, even):
    depth, length = odd.shape
    for h, at in pieces(length):
        ref[h, pl.ds(1, depth, stride=2)] = odd[:, at]
        ref[h, pl.ds(0, depth, stride=2)] = even[:, at]


def side_columns(s_ref, near, far, depth, kind, k, left):
    even = s_ref[8] == 0
    a, b = (far, near) if left else (near, far)
    return jnp.where(even, column(a, depth, kind, k), column(b, depth, kind, k))


def corner_body(s_ref, along, packs, mixed, far, out):
    depth = (along.shape[0] - 8) // 8
    width = along.shape[1]
    _, near_x, far_x = sources(packs, mixed, far, depth)
    out[: along.shape[0]] = along[...]
    lane = lax.broadcasted_iota(jnp.int32, (depth, width), 1)
    block = jnp.zeros((depth, width), jnp.float32)
    rows = packs.shape[0] // (8 * depth + 8) * 128
    spot = 0
    for y in (rows - 1, 0):
        for kind in range(2):
            for k, left in ((1, True), (2, False)):
                value = side_columns(s_ref, near_x, far_x, depth, kind, k, left)
                block = jnp.where(lane == spot, value[:, y : y + 1], block)
                spot += 1
    out[along.shape[0] :] = block


def settle(s_ref, lines, near, far):
    even = s_ref[0] == 0
    lines[0] = jnp.where(even, far[...], near[...])
    lines[1] = jnp.where(even, near[...], far[...])


def to_columns(packed, values):
    for h, at in pieces(packed.shape[1]):
        packed[: values.shape[1], at] = values[h]
    return packed[...].T


def rim(temp, cond, outer, inner, low, high, gas):
    depth, length = temp.shape
    row = lax.broadcasted_iota(jnp.int32, (depth, length), 0)
    lane = lax.broadcasted_iota(jnp.int32, (depth, length), 1)

    def around(value, at_low, at_high):
        return (
            jnp.where(lane == 0, at_low, pltpu.roll(value, 1, 1)),
            jnp.where(lane == length - 1, at_high, pltpu.roll(value, length - 1, 1)),
            jnp.where(row == 0, value, pltpu.roll(value, 1, 0)),
            jnp.where(row == depth - 1, value, pltpu.roll(value, depth - 1, 0)),
        )

    temps = (outer[0], inner[0]) + around(temp, low[0], high[0])
    conds = (outer[1], inner[1]) + around(cond, low[1], high[1])
    total = jnp.zeros_like(temp)
    for side_temp, side_cond in zip(temps, conds):
        total = total + (cond + side_cond) * (side_temp - temp)
    surface = jnp.where(row == 0, (STEP_RATE * HEAT_TRANSFER) * (gas - temp), 0.0)
    return temp + (0.5 * STEP_RATE) * total + surface


def entering(inflow, z, at, lane):
    width = lane.shape[1]
    moved = pltpu.roll(inflow[at], width - (2 * z + 1), 1)
    return jnp.where((lane == 0) | (lane == width - 1), moved, 0.0)


def step_planes(temp, cond, up, down, cond_up, cond_down, inflow, emit, starts, kept=None):
    depth, rows, width = temp.shape
    lane = lax.broadcasted_iota(jnp.int32, (CHUNK, width), 1)
    end = width - 1

    def shifted(ref, z, start, above, below):
        if start == 0:
            upper = jnp.concatenate([above[pl.ds(z, 1)], ref[z, : CHUNK - 1]], axis=0)
        else:
            upper = ref[z, start - 1 : start + CHUNK - 1]
        if start + CHUNK == rows:
            lower = jnp.concatenate([ref[z, start + 1 :], below[pl.ds(z, 1)]], axis=0)
        else:
            lower = ref[z, start + 1 : start + CHUNK + 1]
        return upper, lower

    def plane(z, first):
        before = jnp.maximum(z - 1, 0)
        after = jnp.minimum(z + 1, depth - 1)
        for start in starts:
            at = slice(start, start + CHUNK)
            here = temp[z, at]
            own = cond[z, at]
            pairs = []
            total = None
            sides = list(zip(shifted(temp, z, start, up, down), shifted(cond, z, start, cond_up, cond_down)))
            sides += [(temp[before, at], cond[before, at]), (temp[after, at], cond[after, at])]
            for side_temp, side_cond in sides:
                pair = own + side_cond
                pairs.append(pair)
                term = pair * (side_temp - here)
                total = term if total is None else total + term
            pair = own + pltpu.roll(own, end, 1) if kept is None else kept[z, at]
            pairs.append(pair)
            flow = jnp.where(lane == end, 0.0, pair * (pltpu.roll(here, end, 1) - here))
            total = total + (flow - pltpu.roll(flow, 1, 1))
            if inflow is not None:
                total = total + entering(inflow, z, at, lane)
            emit(z, start, first, here + (0.5 * STEP_RATE) * total, pairs)

    plane(0, True)

    def later(z, nothing):
        plane(z, False)
        return nothing

    lax.fori_loop(1, depth, later, 0)


def inflow_rows(s_ref, packs, near_x, far_x, flow, depth):
    own = lambda kind, k: column(packs, depth, kind, k)
    side = lambda kind, k, left: side_columns(s_ref, near_x, far_x, depth, kind, k, left)
    left_pair = own(1, 2) + side(1, 1, True)
    right_pair = own(1, 1) + side(1, 2, False)
    interleave(
        flow,
        left_pair * (side(0, 1, True) - own(0, 2)),
        right_pair * (side(0, 2, False) - own(0, 1)),
    )
    return left_pair, right_pair


def base_emit(temp, gas, out, kept):
    def emit(z, start, first, value, pairs):
        at = slice(start, start + CHUNK)
        if first:
            value = value + (STEP_RATE * HEAT_TRANSFER) * (gas[at] - temp[0, at])
        out[z, at] = value
        kept[z, at] = pairs[4]

    return emit


def inner_body(s_ref, temp, cond, gas, out, kept):
    rows = temp.shape[1]
    step_planes(
        temp, cond, None, None, None, None, None, base_emit(temp, gas, out, kept),
        range(RIM, rows - RIM, CHUNK),
    )


def tile_rims(mine, near_x, far_x, along, lines, depth, width, side):
    last = 8 * depth
    own = lambda k: tuple(column(mine, depth, kind, k) for kind in range(2))
    left = lambda k: tuple(side(depth, kind, k, True) for kind in range(2))
    right = lambda k: tuple(side(depth, kind, k, False) for kind in range(2))
    zero = jnp.zeros((depth, 1), jnp.float32)
    if lines is None:
        corner = lambda which, spot: (zero, zero)
        at_lane = lambda pair, lane: (zero, zero)
        up_line = down_line = None
    else:
        line = lambda ref, k: tuple(
            ref[4 * depth * kind + depth * k : 4 * depth * kind + depth * (k + 1)] for kind in range(2)
        )
        corner = lambda which, spot: tuple(
            lines[which, last + 8 :][:, at : at + 1] for at in (spot, spot + 2)
        )
        at_lane = lambda pair, lane: tuple(v[:, lane : lane + 1] for v in pair)
        up_line, down_line = line(lines.at[0], 1), line(lines.at[1], 2)
    gas_left, gas_right = side.gas
    out_left = rim(*left(1), left(0), own(2), corner(0, 0), corner(1, 4), gas_left)
    out_right = rim(*right(2), right(3), own(1), corner(0, 1), corner(1, 5), gas_right)
    in_left = rim(
        *own(2), left(1), own(3), at_lane(up_line, 0), at_lane(down_line, 0), flat(mine, last + 2)
    )
    in_right = rim(
        *own(1), right(2), own(0), at_lane(up_line, width - 1), at_lane(down_line, width - 1),
        flat(mine, last + 1),
    )
    if lines is None:
        return out_left - in_left, out_right - in_right, None, None
    upper = rim(
        *up_line, line(lines.at[0], 0), line(along, 2), corner(0, 0), corner(0, 1),
        lines[0, last + 1 : last + 2],
    )
    lower = rim(
        *down_line, line(lines.at[1], 3), line(along, 1), corner(1, 4), corner(1, 5),
        lines[1, last + 2 : last + 3],
    )
    return out_left - in_left, out_right - in_right, upper, lower


class Sides:
    def __init__(self, s_ref, near_x, far_x, depth):
        self.s_ref, self.near_x, self.far_x = s_ref, near_x, far_x
        last = 8 * depth
        even = s_ref[8] == 0
        self.gas = (
            jnp.where(even, flat(far_x, last + 1), flat(near_x, last + 1)),
            jnp.where(even, flat(near_x, last + 2), flat(far_x, last + 2)),
        )

    def __call__(self, depth, kind, k, left):
        return side_columns(self.s_ref, self.near_x, self.far_x, depth, kind, k, left)


def final_emit(temp, gas, face, held, weights, done):
    rows, width = held.shape[1:]
    lane = lax.broadcasted_iota(jnp.int32, (CHUNK, width), 1)
    end = width - 1

    def emit(z, start, first, value, pairs):
        at = slice(start, start + CHUNK)
        if first:
            value = value + (STEP_RATE * HEAT_TRANSFER) * (gas[at] - temp[0, at])
            edge = pltpu.roll(face[at], end, 1)
            across = pairs[4]
            left = jnp.where(lane == 0, edge, pltpu.roll(across, 1, 1))
            right = jnp.where(lane == end, edge, across)
            for k, pair in enumerate((pairs[0], pairs[1], left, right, pairs[3])):
                weights[k, at] = (0.5 * STEP_RATE) * pair
        held[z, at] = value
        done(z, start, first)

    return emit


def middle_body(
    s_ref, base_in, temp, cond, kept, gas, packs, mixed, far, base, held, weights,
    packed, flow, inflow, face,
):
    depth, rows, width = temp.shape
    lane = lax.broadcasted_iota(jnp.int32, (CHUNK, width), 1)
    mine, near_x, far_x = sources(packs, mixed, far, depth)
    left_pair, right_pair = inflow_rows(s_ref, mine, near_x, far_x, flow, depth)
    packed[...] = jnp.zeros_like(packed)
    inflow[...] = to_columns(packed, flow)

    def mend(z, nothing):
        for start in range(RIM, rows - RIM, CHUNK):
            at = slice(start, start + CHUNK)
            base[z, at] = base_in[z, at] + (0.5 * STEP_RATE) * entering(inflow, z, at, lane)
        return nothing

    lax.fori_loop(0, depth, mend, 0)
    side = Sides(s_ref, near_x, far_x, depth)
    left_step, right_step, _, _ = tile_rims(mine, near_x, far_x, None, None, depth, width, side)
    interleave(flow, left_pair * left_step, right_pair * right_step)
    inflow[...] = to_columns(packed, flow)
    interleave(flow, left_pair, right_pair)
    face[...] = to_columns(packed, flow)
    step_planes(
        base, cond, None, None, None, None, inflow,
        final_emit(temp, gas, face, held, weights, lambda z, start, first: None),
        range(MIDDLE, rows - MIDDLE, CHUNK), kept,
    )


def outer_body(
    s_ref, base_in, held_in, weights_in, kept_in, temp, cond, gas, packs, along, mixed, far, near_y, far_y,
    base, held, weights, kept, out, top, sems, packed, flow, inflow, face, lines, base_lines,
):
    depth, rows, width = temp.shape
    settle(s_ref, lines, near_y, far_y)
    mine, near_x, far_x = sources(packs, mixed, far, depth)
    left_pair, right_pair = inflow_rows(s_ref, mine, near_x, far_x, flow, depth)
    packed[...] = jnp.zeros_like(packed)
    inflow[...] = to_columns(packed, flow)
    side = Sides(s_ref, near_x, far_x, depth)
    left_step, right_step, base_lines[0], base_lines[1] = tile_rims(
        mine, near_x, far_x, along, lines, depth, width, side
    )
    span = lambda which, kind, k: lines.at[
        which, 4 * depth * kind + depth * k : 4 * depth * kind + depth * (k + 1)
    ]
    cond_up, cond_down = span(0, 1, 1), span(1, 1, 2)
    step_planes(
        temp, cond, span(0, 0, 1), span(1, 0, 2), cond_up, cond_down, inflow,
        base_emit(temp, gas, base, kept),
        (*range(0, RIM, CHUNK), *range(rows - RIM, rows, CHUNK)),
    )
    interleave(flow, left_pair * left_step, right_pair * right_step)
    inflow[...] = to_columns(packed, flow)
    interleave(flow, left_pair, right_pair)
    face[...] = to_columns(packed, flow)

    def done(z, start, first):
        if not first and start + CHUNK == rows:

            @pl.when(z >= 2)
            def _():
                pltpu.make_async_copy(held.at[z], out.at[z], sems.at[z]).start()

    step_planes(
        base, cond, base_lines.at[0], base_lines.at[1], cond_up, cond_down, inflow,
        final_emit(temp, gas, face, held, weights, done),
        (*range(0, MIDDLE, CHUNK), *range(rows - MIDDLE, rows, CHUNK)), kept,
    )
    top[...] = held[:2]
    for z in range(2, depth):
        pltpu.make_async_copy(held.at[z], out.at[z], sems.at[z]).wait()


def faces(value, row, lane, up, down, left, right):
    rows, width = value.shape
    return (
        jnp.where(row == 0, up, pltpu.roll(value, 1, 0)),
        jnp.where(row == rows - 1, down, pltpu.roll(value, rows - 1, 0)),
        jnp.where(lane == 0, left, pltpu.roll(value, 1, 1)),
        jnp.where(lane == width - 1, right, pltpu.roll(value, width - 1, 1)),
    )


def finish_body(
    s_ref, ours, theirs, weights, base, mine, came, filled, pressure, out, held, sem, joined, sems
):
    half = ours.shape[0]
    rows, width = weights.shape[1:]
    sign = (1 - 2 * s_ref[0]).astype(jnp.float32)
    bottom = (1 - 2 * s_ref[3]).astype(jnp.float32)
    second = s_ref[4] == 1
    factor = STEP_RATE * HEAT_TRANSFER * PRESSURE_WORK

    def lines(start, count, minus):
        our_sign = jnp.where(s_ref[0] == 0, 1.0, minus) * factor
        their_sign = jnp.where(s_ref[0] == 0, minus, 1.0) * factor
        at = pl.ds(start, count)
        return our_sign * ours[at] + their_sign * theirs[at]

    begin = pl.multiple_of(s_ref[4] * rows, rows)
    middle = lines(begin, rows, bottom)
    above = lines(jnp.where(second, rows - 1, half - 1), 1, jnp.where(second, bottom, -bottom))
    below = lines(jnp.where(second, 0, rows), 1, jnp.where(second, -bottom, bottom))
    share = middle[:, :width]
    row = lax.broadcasted_iota(jnp.int32, (rows, width), 0)
    lane = lax.broadcasted_iota(jnp.int32, (rows, width), 1)
    around = faces(
        share, row, lane, above[:, :width], below[:, :width],
        middle[:, width : width + 1], middle[:, width + 1 : width + 2],
    )
    added = 2.0 * share
    for k in range(4):
        added = added + weights[k] * (around[k] - share)
    down = weights[4] * share
    held[0] = base[0] + added - down
    held[1] = base[1] + down
    copy = pltpu.make_async_copy(held, out.at[:2], sem)
    copy.start()
    for other in join_planes(s_ref, mine, came, pressure, joined, sems):
        other.wait()
    copy.wait()


def mover(groups, pencils):
    def move(value, target):
        pairs = []
        for g in range(groups):
            for p in range(pencils):
                to = target(g, p)
                pairs.append((g * pencils + p, to[0] * pencils + to[1]))
        return lax.ppermute(value, ("grp", "pen"), pairs)

    return move


def per_device(pressure_source, solid_temp, gas_wall_temp, phase_map, phase_conductivity):
    groups = lax.axis_size("grp")
    pencils = lax.axis_size("pen")
    group_idx = lax.axis_index("grp")
    pencil_idx = lax.axis_index("pen")
    depth_loc, span_len, width = pressure_source.shape
    depth = depth_loc * groups
    half = span_len // 2
    own = depth // 2
    core = group_idx % 2
    low = group_idx // 2
    zi = pencil_idx % Z_RING
    yl = pencil_idx // Z_RING % Y_PAIR
    place = pencil_idx % (Z_RING * Y_PAIR)
    move = mover(groups, pencils)
    tab = make_tables(span_len, width, depth)
    const = {k: tuple(map(jnp.asarray, v)) if isinstance(v, tuple) else jnp.asarray(v) for k, v in tab.items()}
    code = jnp.where(low == 0, core * 4, 7 - 4 * core)
    scalars = jnp.stack([core, low, code, low, core, zi, yl, place, pencil_idx % 2]).astype(jnp.int32)
    span = list(const["span"])
    into = list(const["into"])
    back = list(const["back"])
    span_t = list(const["span_t"])
    tile_rows = span_len // groups
    flip = lambda mask: lambda g, p: (g ^ mask, p)
    near_pair = lambda g, p: (g, p ^ 1)
    far_pair = lambda g, p: (g, (p + 1 if p % 2 else p - 1) % pencils)

    other_core = lambda g, p: (g ^ 1, p)
    other_half = lambda g, p: (g ^ 2, p)
    halves_of = tile_rows // 128
    column_scratch = pltpu.VMEM((tile_rows, width), jnp.float32)
    row_scratch = pltpu.VMEM((width, tile_rows), jnp.float32)
    (pivots,) = run(
        pivot_body, 1.2, scalars, [], [const["lam"], const["sigma"]], [(3 * own + 2, width, half)]
    )
    folded = jax.ShapeDtypeStruct((depth_loc, half, width), jnp.float32)
    away, kept = run_blocks(
        fold_body, 0.8, scalars, [pivots, pressure_source], [ORDER, plane_of(pressure_source)],
        [folded.shape, folded.shape], [plane_of(folded), plane_of(folded)], depth_loc,
    )
    arrived = move(away, other_core)
    (held,) = run(
        held_body, 2.1, scalars, [], [kept, *into, *span], [(depth_loc, width, half)]
    )
    cond, packs, along = run(
        edge_body, 2.8, scalars, [held], [solid_temp, phase_map, gas_wall_temp],
        [(depth, tile_rows, width), (halves_of * (8 * depth + 8), 128), (8 * depth + 8, width)],
        scratch=[column_scratch], small=[phase_conductivity],
    )
    planes, edges, carried, opening, mixed = run(
        arrived_body, 3.4, scalars, [],
        [arrived, held, *into, *span, pivots, const["edge"], const["basis_t"], const["far"],
         packs],
        [(own, width, half), (2, depth, half), (width, half), (width, half),
         (2 * depth * half // 128 + packs.shape[0], 128)],
        scratch=[pltpu.VMEM((2, depth, 8, half), jnp.float32)],
    )
    mixed = move(mixed, near_pair)
    z_got = [move(edges, lambda g, p, d=d: (g, p ^ d)) for d in range(2, Z_RING)]
    far_x = move(packs, far_pair)
    carried_there = move(carried, other_half)
    log_rho = const["log_rho"]
    pair_shape = edges.shape
    base, sides = run(
        inner_body, 4.5, scalars, [edges], [solid_temp, cond, gas_wall_temp],
        [(depth, tile_rows, width), (depth, tile_rows, width)],
    )
    four, two = run(
        functools.partial(z_body, width=width), 0.6, scalars, [far_x, carried_there, base],
        [edges, mixed, *z_got, log_rho], [(4,) + pair_shape[1:], pair_shape],
    )
    there = move(four, other_half)
    beside1 = move(two, lambda g, p: (g, p ^ Z_RING))
    beside2 = move(two, lambda g, p: (g ^ 2, p ^ Z_RING))
    (lines,) = run(
        corner_body, 0.6, scalars, [two], [along, packs, mixed, far_x], [(9 * depth + 8, width)]
    )
    near_y = [move(lines, flip(1)), move(lines, flip(3))]
    flow_scratch = pltpu.VMEM((halves_of, 2 * depth, 128), jnp.float32)
    tile = (depth, tile_rows, width)
    base, begun, weights = run(
        middle_body, 4.5, scalars, [lines],
        [base, solid_temp, cond, sides, gas_wall_temp, packs, mixed, far_x],
        [tile, tile, (5, tile_rows, width)],
        scratch=[row_scratch, flow_scratch, column_scratch, column_scratch],
        aliases={2: 0},
    )
    run8, part, opening = run(
        functools.partial(y_body, width=width), 0.6, scalars, [base, *near_y],
        [four, there, beside1, beside2, log_rho, opening], [pair_shape, pair_shape, opening.shape],
    )
    block = Z_RING * Y_PAIR
    opening_there = move(opening, other_half)
    x_got = [move(run8, lambda g, p, d=d: (g, (p + block * d) % pencils)) for d in range(1, X_RING)]
    _, _, weights, _, final, top = run(
        outer_body, 5.5, scalars, [run8],
        [base, begun, weights, sides, solid_temp, cond, gas_wall_temp, packs, along, mixed, far_x,
         *near_y],
        [tile, tile, (5, tile_rows, width), tile, solid_temp.shape, (2, tile_rows, width)],
        scratch=[
            pltpu.SemaphoreType.DMA((depth,)),
            row_scratch, flow_scratch, column_scratch, column_scratch,
            pltpu.VMEM((2, 9 * depth + 8, width), jnp.float32),
            pltpu.VMEM((2, depth, width), jnp.float32),
        ],
        out_specs=[FAST, FAST, FAST, FAST, ORDER, FAST], aliases={2: 0, 3: 1, 4: 2, 5: 3},
    )
    wall, away, keep = run(
        solve_body, 6.9, scalars, [weights],
        [planes, carried_there, opening_there, run8, part, *x_got, log_rho, pivots, *span_t, *back,
         const["edge"], const["basis"]],
        [(half, 2 * width), (depth_loc, half, width), (depth_loc, width, half)],
        scratch=[
            pltpu.VMEM((own, width, half), jnp.float32),
            pltpu.VMEM((2, depth, half), jnp.float32),
            pltpu.VMEM((2 * width, half), jnp.float32),
        ],
    )
    wall_came = move(wall, other_core)
    came = move(away, other_core)
    (mine,) = run(cells_body, 2.2, scalars, [], [keep, *span_t, *back], [(depth_loc, half, width)])
    pressure, final = run(
        finish_body, 2.5, scalars, [], [wall, wall_came, weights, top, mine, came, (final, ORDER)],
        [pressure_source.shape, final.shape],
        scratch=[
            pltpu.VMEM(top.shape, jnp.float32), pltpu.SemaphoreType.DMA,
            pltpu.VMEM(pressure_source.shape, jnp.float32), pltpu.SemaphoreType.DMA((depth_loc,)),
        ],
        out_specs=[ORDER, ORDER], aliases={7: 1},
    )
    return (pressure, final)


def solution(mesh):
    in_specs = (
        P("grp", None, "pen"),
        P(None, "grp", "pen"),
        P("grp", "pen"),
        P(None, "grp", "pen"),
        P(),
    )
    out_specs = (P("grp", None, "pen"), P(None, "grp", "pen"))
    return jax.shard_map(
        per_device, mesh=mesh, in_specs=in_specs, out_specs=out_specs, check_vma=False
    )
```

```python
import functools
import math

import jax
import jax.numpy as jnp
import numpy as np
from jax import lax
from jax.experimental import pallas as pl
from jax.experimental.pallas import tpu as pltpu
from jax.sharding import PartitionSpec as P

HIGHEST = lax.Precision.HIGHEST
HEAT_TRANSFER = 1.0
PRESSURE_WORK = 0.5
STEP_RATE = 0.12
Z_RING, Y_PAIR, X_RING = 4, 2, 4
VMEM_LIMIT = 18 * 1024 * 1024
BLOCK_LIMIT = 16 * 1024 * 1024
LANES = 128
CHUNK = 32
RIM = 32
MIDDLE = 64
COST_SCALE = 0.1


def halves(value):
    high = np.asarray(value, np.float32).astype(jnp.bfloat16)
    low = (np.asarray(value, np.float64) - high.astype(np.float64)).astype(jnp.bfloat16)
    return high, low


def make_tables(span_len, width, depth):
    half = span_len // 2
    waves = np.stack([2 * np.arange(half), 2 * np.arange(half) + 1]).astype(np.float64)
    rows = np.arange(half)
    angle = 2 * np.pi * ((rows[None, :, None] * waves[:, None, :]) % span_len) / span_len
    span = np.cos(angle) + np.sin(angle)
    lam = -4 * np.sin(np.pi * waves / span_len) ** 2
    order = np.concatenate([np.arange(0, width, 2), np.arange(1, width, 2)]) + 1.0
    cells = np.arange(width) + 1.0
    sine = np.sqrt(2 / (width + 1)) * np.sin(np.pi * cells[:, None] * order[None, :] / (width + 1))
    sigma = -4 * np.sin(np.pi * order / (2 * (width + 1))) ** 2
    modes = np.arange(depth)
    theta = np.pi * (2 * modes + 1) / (2 * depth + 1)
    basis = np.cos(theta[None, :] * (np.arange(depth)[:, None] + 0.5)) / np.sqrt((2 * depth + 1) / 4)
    mu = -4 * np.sin(theta / 2) ** 2
    stretch = -(mu[None, :, None] + lam[:, None, :])
    log_rho = -2 * np.arcsinh(np.sqrt(stretch) / 2)
    down = np.arange(depth // 2)
    up = depth - 1 - down
    ordered = np.stack([basis[np.concatenate([down, up])], basis[np.concatenate([up, down])]])
    pair = np.kron(np.eye(2), sine)
    f32 = lambda v: np.asarray(v, np.float32)
    lanes = min(LANES, half)
    return {
        "span": halves(span),
        "span_t": halves(np.swapaxes(span, 1, 2)),
        "into": halves(pair / span_len),
        "back": halves(pair.T),
        "lam": f32(lam)[:, None, :],
        "sigma": f32(np.repeat(sigma[:, None], lanes, 1)),
        "edge": f32(np.repeat(sine[0][:, None], lanes, 1)),
        "basis": f32(ordered),
        "basis_t": f32(np.swapaxes(ordered, 1, 2)),
        "log_rho": f32(log_rho),
        "far": f32(np.exp(log_rho * (width + 1))),
    }


def product(first, second):
    return jnp.dot(first, second, preferred_element_type=jnp.float32)


def split(value):
    high = value.astype(jnp.bfloat16)
    return high, (value - high.astype(jnp.float32)).astype(jnp.bfloat16)


def times(value, high, low):
    value_high, value_low = split(value)
    return product(value_high, high) + (product(value_high, low) + product(value_low, high))


def times_turned(high, low, value):
    value_high, value_low = split(value)
    turned = lambda a, b: lax.dot_general(
        a, b, (((1,), (1,)), ((), ())), preferred_element_type=jnp.float32
    )
    return turned(high, value_high) + (turned(low, value_high) + turned(high, value_low))


ORDER = pl.BlockSpec(memory_space=pl.ANY)
SCALARS = pl.BlockSpec(memory_space=pltpu.SMEM)
FAST = pl.BlockSpec(memory_space=pltpu.VMEM)


def plane_of(array):
    rest = array.shape[1:]
    return pl.BlockSpec((1,) + rest, lambda i, s: (i,) + (0,) * len(rest))


def cost(time_us):
    return pl.CostEstimate(flops=1, bytes_accessed=int(time_us * 3.69e6 * COST_SCALE), transcendentals=0)


def run(body, time_us, scalars, ordered, arrays, outs, scratch=(), small=(), out_specs=None, aliases=None):
    outs = [jax.ShapeDtypeStruct(shape, jnp.float32) for shape in outs]
    skip = len(ordered)
    count = len(small)
    kinds = [FAST if spec is None else spec for spec in (a[1] if type(a) is tuple else None for a in arrays)]
    arrays = [a[0] if type(a) is tuple else a for a in arrays]
    specs = [SCALARS] + [SCALARS] * count + [ORDER] * skip + kinds

    def inner(s_ref, *refs):
        body(s_ref, *refs[:count], *refs[count + skip :])

    return pl.pallas_call(
        inner,
        out_shape=outs,
        in_specs=specs,
        out_specs=out_specs or [FAST] * len(outs),
        scratch_shapes=list(scratch),
        input_output_aliases=aliases or {},
        compiler_params=pltpu.CompilerParams(vmem_limit_bytes=VMEM_LIMIT),
        cost_estimate=cost(time_us),
    )(scalars, *small, *ordered, *arrays)


def run_blocks(body, time_us, scalars, arrays, specs, outs, out_specs, steps):
    return pl.pallas_call(
        body,
        out_shape=[jax.ShapeDtypeStruct(out, jnp.float32) for out in outs],
        grid_spec=pltpu.PrefetchScalarGridSpec(
            num_scalar_prefetch=1, grid=(steps,), in_specs=specs, out_specs=out_specs
        ),
        compiler_params=pltpu.CompilerParams(vmem_limit_bytes=BLOCK_LIMIT),
        cost_estimate=cost(time_us),
    )(scalars, *arrays)


def fold_body(s_ref, after, source, away, kept):
    half = source.shape[1] // 2
    sign = (1 - 2 * s_ref[0]).astype(jnp.float32)
    upper = source[:, :half]
    lower = sign * source[:, half:]
    away[...] = upper - lower
    kept[...] = upper + lower


def spectral(planes, into_high, into_low, span_high, span_low):
    turned = []
    for pair in range(0, len(planes), 2):
        cells = jnp.concatenate(planes[pair : pair + 2], axis=1)
        turned.append(times(cells, into_high, into_low).T)
    return times(jnp.concatenate(turned, axis=0), span_high, span_low)


def held_body(s_ref, kept, into_high, into_low, span_high, span_low, out):
    out[...] = spectral(
        [kept[z] for z in range(kept.shape[0])], into_high[...], into_low[...],
        span_high[s_ref[0]], span_low[s_ref[0]],
    ).reshape(out.shape)


def across(value, length):
    return jnp.concatenate([value] * (length // value.shape[1]), axis=1)


def continuants(centre, first, count):
    values = [jnp.ones_like(centre), centre + first]
    for _ in range(1, count):
        values.append(centre * values[-1] - values[-2])
    return values


def pivot_body(s_ref, lam, sigma, out):
    own = (out.shape[0] - 2) // 3
    width = out.shape[1]
    low = s_ref[1].astype(jnp.float32)

    def tile(group, nothing):
        rows = pl.ds(pl.multiple_of(group * 8, 8), 8)
        centre = lam[s_ref[0]] + across(sigma[rows], out.shape[2]) - 2.0
        mine = continuants(centre, 1.0 - low, own)
        other = continuants(centre, low, own)
        for i in range(own):
            out[i, rows] = mine[i + 1]
            out[own + i, rows] = other[i + 1]
            out[2 * own + i, rows] = 1.0 / mine[i + 1]
        out[3 * own, rows] = 1.0 / (mine[own] * other[own] - mine[own - 1] * other[own - 1])
        out[3 * own + 1, rows] = 1.0 / other[own]
        return nothing

    lax.fori_loop(0, width // 16, lambda k, c: tile(2 * k + 1, tile(2 * k, c)), 0)


def arrived_body(
    s_ref, arrived, held, into_high, into_low, span_high, span_low, pivots, edge, basis_t, far, packs,
    planes, edges, carried, opening, mixed, sums,
):
    count = held.shape[0]
    own = 2 * count
    width, half = held.shape[1:]
    planes[:count] = held[...]
    planes[count:] = spectral(
        [arrived[z] for z in range(count)], into_high[...], into_low[...],
        span_high[s_ref[0]], span_low[s_ref[0]],
    ).reshape(held.shape)
    sums[...] = jnp.zeros_like(sums)
    code = s_ref[2]
    side = width // 16

    def tile(group, nothing):
        rows = pl.ds(pl.multiple_of(group * 8, 8), 8)
        parity = group // side
        carry = planes[code, rows]
        carries = [carry]
        for i in range(1, own):
            carry = pivots[i - 1, rows] * planes[jnp.bitwise_xor(i, code), rows] - carry
            carries.append(carry)
        carried[rows] = carry
        shared = carry * pivots[3 * own, rows]
        scale = across(edge[rows], half)
        value = shared * pivots[2 * own - 1, rows]
        sums[parity, own - 1] += scale * value
        for i in range(own - 2, -1, -1):
            step = value if i == 0 else pivots[i - 1, rows] * value
            value = (carries[i] - step) * pivots[2 * own + i, rows]
            sums[parity, i] += scale * value
        opening[rows] = value + pivots[2 * own - 2, rows] * shared * pivots[3 * own - 1, rows]
        shared = scale * shared
        for i in range(own):
            term = shared if i == 0 else pivots[own + i - 1, rows] * shared
            sums[parity, own + i] += term if (own - i) % 2 == 0 else -term
        return nothing

    lax.fori_loop(0, width // 16, lambda k, c: tile(2 * k + 1, tile(2 * k, c)), 0)
    total = jnp.sum(sums[...], axis=2)
    modal = lambda v: jnp.dot(
        basis_t[s_ref[1]], v, precision=HIGHEST, preferred_element_type=jnp.float32
    )
    even = modal(total[0])
    odd = modal(total[1])
    edge_low = even + odd
    edge_high = even - odd
    right = edge_high + far[s_ref[0]] * edge_low
    left = edge_low + far[s_ref[0]] * edge_high
    edges[0] = right
    edges[1] = left
    at = 0
    for value in (right, left):
        for _, lanes in pieces(half):
            mixed[at : at + value.shape[0]] = value[:, lanes]
            at += value.shape[0]
    mixed[at:] = packs[...]


def powers(s_ref, log_rho):
    rate = log_rho[s_ref[0]]
    return lambda n: jnp.exp(rate * n)


def scalar(value):
    return value.astype(jnp.float32)


def z_body(s_ref, edges, mixed, got2, got3, log_rho, four, two, *, width):
    power = powers(s_ref, log_rho)
    zi = s_ref[5]
    wide = float(width)
    right, left = edges[0], edges[1]
    low_sum = jnp.zeros_like(right)
    high_sum = jnp.zeros_like(right)
    right4 = power(wide * scalar(Z_RING - 1 - zi)) * right
    left4 = power(wide * scalar(zi)) * left
    size = right.shape[0]
    lanes = mixed.shape[1]
    pieces_of = right.shape[1] // lanes
    first_right, first_left = (
        jnp.concatenate(
            [mixed[(k * pieces_of + c) * size : (k * pieces_of + c + 1) * size] for c in range(pieces_of)],
            axis=1,
        )
        for k in range(2)
    )
    for d, got_right, got_left in (
        (1, first_right, first_left), (2, got2[0], got2[1]), (3, got3[0], got3[1])
    ):
        source = jnp.bitwise_xor(zi, d)
        before = scalar(source < zi)
        gap = jnp.maximum(zi - source, source - zi) - 1
        step = power(wide * scalar(gap))
        low_sum = low_sum + before * step * got_right
        high_sum = high_sum + (1.0 - before) * step * got_left
        right4 = right4 + power(wide * scalar(Z_RING - 1 - source)) * got_right
        left4 = left4 + power(wide * scalar(source)) * got_left
    hop = power(wide)
    per_rho = power(-1.0)
    four[0] = per_rho * low_sum + left + hop * high_sum
    four[1] = per_rho * high_sum + right + hop * low_sum
    four[2] = right4
    four[3] = left4
    two[0] = right4
    two[1] = left4


def y_body(s_ref, four, there, beside1, beside2, log_rho, opening, run8, part, passed, *, width):
    passed[...] = opening[...]
    power = powers(s_ref, log_rho)
    zi = s_ref[5]
    wide = float(width)
    behind = scalar(s_ref[6])
    other0 = beside1[0] + beside2[0]
    other1 = beside1[1] + beside2[1]
    right4 = four[2] + there[2]
    left4 = four[3] + there[3]
    low_sum = behind * power(wide * scalar(zi)) * other0
    high_sum = (1.0 - behind) * power(wide * scalar(Z_RING - 1 - zi)) * other1
    run4 = power(wide * Z_RING)
    is_behind = s_ref[6] == 1
    run8[0] = jnp.where(is_behind, run4 * other0 + right4, run4 * right4 + other0)
    run8[1] = jnp.where(is_behind, other1 + run4 * left4, left4 + run4 * other1)
    hop = power(wide)
    per_rho = power(-1.0)
    part[0] = four[0] + there[0] + per_rho * low_sum + hop * high_sum
    part[1] = four[1] + there[1] + per_rho * high_sum + hop * low_sum


def x_sums(s_ref, run8, part, gots, log_rho, width):
    power = powers(s_ref, log_rho)
    wide = float(width)
    block = Z_RING * Y_PAIR
    right_sum = power(wide * block * (X_RING - 1)) * run8[0]
    left_sum = power(wide * block * (X_RING - 1)) * run8[1]
    for d, got in enumerate(gots, 1):
        right_sum = right_sum + power(wide * block * (d - 1)) * got[0]
        left_sum = left_sum + power(wide * block * (X_RING - 1 - d)) * got[1]
    periodic = 1.0 / (1.0 - power(wide * block * X_RING))
    low_sum = power(wide * scalar(s_ref[7])) * right_sum * periodic
    high_sum = power(wide * scalar(block - 1 - s_ref[7])) * left_sum * periodic
    rho = power(1.0)
    per_rho = power(-1.0)
    hop = power(wide)
    gain = rho / (1.0 - rho * rho)
    into_low = gain * (part[0] + per_rho * low_sum + hop * high_sum)
    into_high = gain * (part[1] + per_rho * high_sum + hop * low_sum)
    return into_low, into_high


def to_cells(values, span_t_high, span_t_low, back_high, back_low):
    lines = times(values, span_t_high, span_t_low)
    size = back_high.shape[0]
    return [
        times(lines[at : at + size].T, back_high, back_low) for at in range(0, lines.shape[0], size)
    ]


def solve_body(
    s_ref, planes, carried, opening, run8, part, got1, got2, got3, log_rho, pivots,
    span_t_high, span_t_low, back_high, back_low, edge, basis,
    wall, away, keep, solved, both, first,
):
    own, width, half = planes.shape
    count = own // 2
    is_low = s_ref[1] == 1
    code = s_ref[2]
    depthwise = lambda v: jnp.dot(
        basis[s_ref[1]], v, precision=HIGHEST, preferred_element_type=jnp.float32
    )
    into_low, into_high = x_sums(s_ref, run8, part, (got1, got2, got3), log_rho, width)
    gain_low = depthwise(into_low)
    gain_high = depthwise(into_high)
    both[0] = gain_low + gain_high
    both[1] = gain_low - gain_high
    first[width:] = jnp.zeros_like(first[width:])
    first[width : width + 1] = jnp.where(is_low, gain_low[own : own + 1], gain_low[:1])
    first[width + 1 : width + 2] = jnp.where(is_low, gain_high[own : own + 1], gain_high[:1])
    side = width // 16

    def tile(group, nothing):
        rows = pl.ds(pl.multiple_of(group * 8, 8), 8)
        parity = group // side
        scale = across(edge[rows], half)
        rhs = lambda i: scale * both[parity, i : i + 1]
        mine = lambda i: pivots[i - 1, rows]
        other = lambda i: pivots[own + i - 1, rows]
        carry = planes[code, rows] - rhs(0)
        carries = [carry]
        for i in range(1, own):
            carry = mine(i) * (planes[jnp.bitwise_xor(i, code), rows] - rhs(i)) - carry
            carries.append(carry)
        right = rhs(own)
        total = -right
        direct = -mine(own - 1) * right
        for i in range(1, own):
            right = rhs(own + i)
            total = -other(i) * right - total
            term = right if i == own - 1 else mine(own - 1 - i) * right
            direct = direct - term if i % 2 == 0 else direct + term
        total = total + carried[rows]
        value = (carry * other(own) - mine(own - 1) * total) * pivots[3 * own, rows]
        far_first = opening[rows] + (direct + value) * pivots[3 * own + 1, rows]
        solved[jnp.bitwise_xor(own - 1, code), rows] = value
        for i in range(own - 2, -1, -1):
            step = value if i == 0 else mine(i) * value
            value = (carries[i] - step) * pivots[2 * own + i, rows]
            solved[jnp.bitwise_xor(i, code), rows] = value
        first[rows] = jnp.where(is_low, far_first, value)
        return nothing

    lax.fori_loop(0, width // 16, lambda k, c: tile(2 * k + 1, tile(2 * k, c)), 0)
    table_high = span_t_high[s_ref[0]]
    table_low = span_t_low[s_ref[0]]
    line = times(first[...], table_high, table_low).T
    main = times(line[:, :width], back_high[:width, :width], back_low[:width, :width])
    wall[...] = jnp.concatenate([main, line[:, width:]], axis=1)
    values = solved[count:].reshape(count * width, half)
    for k, cells in enumerate(to_cells(values, table_high, table_low, back_high[...], back_low[...])):
        away[2 * k] = cells[:, :width]
        away[2 * k + 1] = cells[:, width:]
    keep[...] = solved[:count]


def cells_body(s_ref, keep, span_t_high, span_t_low, back_high, back_low, mine):
    count, width, half = keep.shape
    values = keep[...].reshape(count * width, half)
    pairs = to_cells(
        values, span_t_high[s_ref[0]], span_t_low[s_ref[0]], back_high[...], back_low[...]
    )
    for k, cells in enumerate(pairs):
        mine[2 * k] = cells[:, :width]
        mine[2 * k + 1] = cells[:, width:]


def join_planes(s_ref, mine, came, out, held, sems):
    half = mine.shape[1]
    sign = (1 - 2 * s_ref[0]).astype(jnp.float32)
    copies = []
    for z in range(mine.shape[0]):
        ours = mine[z]
        theirs = came[z]
        held[z, :half] = ours + theirs
        held[z, half:] = sign * (ours - theirs)
        copy = pltpu.make_async_copy(held.at[z], out.at[z], sems.at[z])
        copy.start()
        copies.append(copy)
    return copies


def edge_body(s_ref, conductivity, temp, phase, gas, cond, packs, along, packed):
    depth, rows, width = temp.shape
    lane = lax.broadcasted_iota(jnp.int32, (CHUNK, width), 1)
    cold, warm = conductivity[0], conductivity[1]
    packed[...] = jnp.zeros_like(packed)

    def plane(z, nothing):
        for start in range(0, rows, CHUNK):
            at = slice(start, start + CHUNK)
            kept = packed[at]
            value = jnp.where(phase[z, at] == 1, warm, cold)
            cond[z, at] = value
            for k, part in enumerate((temp[z, at], value)):
                spot = 4 * (k * depth + z)
                chosen_lane = (lane >= spot) & (lane < spot + 4)
                kept = jnp.where(chosen_lane, pltpu.roll(part, spot + 2, 1), kept)
                line = 4 * depth * k + z
                if start == 0:
                    along[pl.ds(line + 2 * depth, 1)] = part[:1]
                    along[pl.ds(line + 3 * depth, 1)] = part[1:2]
                if start + CHUNK == rows:
                    along[pl.ds(line, 1)] = part[CHUNK - 2 : CHUNK - 1]
                    along[pl.ds(line + depth, 1)] = part[CHUNK - 1 :]
            packed[at] = kept
        return nothing

    lax.fori_loop(0, depth, plane, 0)
    last = 8 * depth
    turned = packed[...].T
    turned_gas = pltpu.roll(gas[...], 2, 1).T[:8]
    for h, at in pieces(rows):
        base = h * (last + 8)
        packs[base : base + last] = turned[:, at]
        packs[base + last : base + last + 8] = turned_gas[:, at]
    along[last : last + 8] = jnp.concatenate(
        [gas[rows - 2 :], gas[:2], jnp.zeros((4, width), jnp.float32)], axis=0
    )


def pieces(length):
    return [(h, slice(h * 128, h * 128 + 128)) for h in range(length // 128)]


def column(source, depth, kind, k):
    ref, base, size = source
    at = lambda h: pl.ds(base + h * size + 4 * depth * kind + k, depth, stride=4)
    return jnp.concatenate([ref[at(h)] for h in range((ref.shape[0] - base) // size)], axis=1)


def flat(source, row):
    ref, base, size = source
    at = lambda h: base + h * size + row
    count = (ref.shape[0] - base) // size
    return jnp.concatenate([ref[at(h) : at(h) + 1] for h in range(count)], axis=1)


def sources(packs, mixed, far_x, depth):
    size = 8 * depth + 8
    return (packs, 0, size), (mixed, mixed.shape[0] - packs.shape[0], size), (far_x, 0, size)


def interleave(ref, odd, even):
    depth, length = odd.shape
    for h, at in pieces(length):
        ref[h, pl.ds(1, depth, stride=2)] = odd[:, at]
        ref[h, pl.ds(0, depth, stride=2)] = even[:, at]


def side_columns(s_ref, near, far, depth, kind, k, left):
    even = s_ref[8] == 0
    a, b = (far, near) if left else (near, far)
    return jnp.where(even, column(a, depth, kind, k), column(b, depth, kind, k))


def corner_body(s_ref, along, packs, mixed, far, out):
    depth = (along.shape[0] - 8) // 8
    width = along.shape[1]
    _, near_x, far_x = sources(packs, mixed, far, depth)
    out[: along.shape[0]] = along[...]
    lane = lax.broadcasted_iota(jnp.int32, (depth, width), 1)
    block = jnp.zeros((depth, width), jnp.float32)
    rows = packs.shape[0] // (8 * depth + 8) * 128
    spot = 0
    for y in (rows - 1, 0):
        for kind in range(2):
            for k, left in ((1, True), (2, False)):
                value = side_columns(s_ref, near_x, far_x, depth, kind, k, left)
                block = jnp.where(lane == spot, value[:, y : y + 1], block)
                spot += 1
    out[along.shape[0] :] = block


def settle(s_ref, lines, near, far):
    even = s_ref[0] == 0
    lines[0] = jnp.where(even, far[...], near[...])
    lines[1] = jnp.where(even, near[...], far[...])


def to_columns(packed, values):
    for h, at in pieces(packed.shape[1]):
        packed[: values.shape[1], at] = values[h]
    return packed[...].T


def rim(temp, cond, outer, inner, low, high, gas):
    depth, length = temp.shape
    row = lax.broadcasted_iota(jnp.int32, (depth, length), 0)
    lane = lax.broadcasted_iota(jnp.int32, (depth, length), 1)

    def around(value, at_low, at_high):
        return (
            jnp.where(lane == 0, at_low, pltpu.roll(value, 1, 1)),
            jnp.where(lane == length - 1, at_high, pltpu.roll(value, length - 1, 1)),
            jnp.where(row == 0, value, pltpu.roll(value, 1, 0)),
            jnp.where(row == depth - 1, value, pltpu.roll(value, depth - 1, 0)),
        )

    temps = (outer[0], inner[0]) + around(temp, low[0], high[0])
    conds = (outer[1], inner[1]) + around(cond, low[1], high[1])
    total = jnp.zeros_like(temp)
    for side_temp, side_cond in zip(temps, conds):
        total = total + (cond + side_cond) * (side_temp - temp)
    surface = jnp.where(row == 0, (STEP_RATE * HEAT_TRANSFER) * (gas - temp), 0.0)
    return temp + (0.5 * STEP_RATE) * total + surface


def entering(inflow, z, at, lane):
    width = lane.shape[1]
    moved = pltpu.roll(inflow[at], width - (2 * z + 1), 1)
    return jnp.where((lane == 0) | (lane == width - 1), moved, 0.0)


def step_planes(temp, cond, up, down, cond_up, cond_down, inflow, emit, starts, kept=None):
    depth, rows, width = temp.shape
    lane = lax.broadcasted_iota(jnp.int32, (CHUNK, width), 1)
    end = width - 1

    def shifted(ref, z, start, above, below):
        if start == 0:
            upper = jnp.concatenate([above[pl.ds(z, 1)], ref[z, : CHUNK - 1]], axis=0)
        else:
            upper = ref[z, start - 1 : start + CHUNK - 1]
        if start + CHUNK == rows:
            lower = jnp.concatenate([ref[z, start + 1 :], below[pl.ds(z, 1)]], axis=0)
        else:
            lower = ref[z, start + 1 : start + CHUNK + 1]
        return upper, lower

    def plane(z, first):
        before = jnp.maximum(z - 1, 0)
        after = jnp.minimum(z + 1, depth - 1)
        for start in starts:
            at = slice(start, start + CHUNK)
            here = temp[z, at]
            own = cond[z, at]
            pairs = []
            total = None
            sides = list(zip(shifted(temp, z, start, up, down), shifted(cond, z, start, cond_up, cond_down)))
            sides += [(temp[before, at], cond[before, at]), (temp[after, at], cond[after, at])]
            for side_temp, side_cond in sides:
                pair = own + side_cond
                pairs.append(pair)
                term = pair * (side_temp - here)
                total = term if total is None else total + term
            pair = own + pltpu.roll(own, end, 1) if kept is None else kept[z, at]
            pairs.append(pair)
            flow = jnp.where(lane == end, 0.0, pair * (pltpu.roll(here, end, 1) - here))
            total = total + (flow - pltpu.roll(flow, 1, 1))
            if inflow is not None:
                total = total + entering(inflow, z, at, lane)
            emit(z, start, first, here + (0.5 * STEP_RATE) * total, pairs)

    plane(0, True)

    def later(z, nothing):
        plane(z, False)
        return nothing

    lax.fori_loop(1, depth, later, 0)


def inflow_rows(s_ref, packs, near_x, far_x, flow, depth):
    own = lambda kind, k: column(packs, depth, kind, k)
    side = lambda kind, k, left: side_columns(s_ref, near_x, far_x, depth, kind, k, left)
    left_pair = own(1, 2) + side(1, 1, True)
    right_pair = own(1, 1) + side(1, 2, False)
    interleave(
        flow,
        left_pair * (side(0, 1, True) - own(0, 2)),
        right_pair * (side(0, 2, False) - own(0, 1)),
    )
    return left_pair, right_pair


def base_emit(temp, gas, out, kept):
    def emit(z, start, first, value, pairs):
        at = slice(start, start + CHUNK)
        if first:
            value = value + (STEP_RATE * HEAT_TRANSFER) * (gas[at] - temp[0, at])
        out[z, at] = value
        kept[z, at] = pairs[4]

    return emit


def inner_body(s_ref, temp, cond, gas, out, kept):
    rows = temp.shape[1]
    step_planes(
        temp, cond, None, None, None, None, None, base_emit(temp, gas, out, kept),
        range(RIM, rows - RIM, CHUNK),
    )


def tile_rims(mine, near_x, far_x, along, lines, depth, width, side):
    last = 8 * depth
    own = lambda k: tuple(column(mine, depth, kind, k) for kind in range(2))
    left = lambda k: tuple(side(depth, kind, k, True) for kind in range(2))
    right = lambda k: tuple(side(depth, kind, k, False) for kind in range(2))
    zero = jnp.zeros((depth, 1), jnp.float32)
    if lines is None:
        corner = lambda which, spot: (zero, zero)
        at_lane = lambda pair, lane: (zero, zero)
        up_line = down_line = None
    else:
        line = lambda ref, k: tuple(
            ref[4 * depth * kind + depth * k : 4 * depth * kind + depth * (k + 1)] for kind in range(2)
        )
        corner = lambda which, spot: tuple(
            lines[which, last + 8 :][:, at : at + 1] for at in (spot, spot + 2)
        )
        at_lane = lambda pair, lane: tuple(v[:, lane : lane + 1] for v in pair)
        up_line, down_line = line(lines.at[0], 1), line(lines.at[1], 2)
    gas_left, gas_right = side.gas
    out_left = rim(*left(1), left(0), own(2), corner(0, 0), corner(1, 4), gas_left)
    out_right = rim(*right(2), right(3), own(1), corner(0, 1), corner(1, 5), gas_right)
    in_left = rim(
        *own(2), left(1), own(3), at_lane(up_line, 0), at_lane(down_line, 0), flat(mine, last + 2)
    )
    in_right = rim(
        *own(1), right(2), own(0), at_lane(up_line, width - 1), at_lane(down_line, width - 1),
        flat(mine, last + 1),
    )
    if lines is None:
        return out_left - in_left, out_right - in_right, None, None
    upper = rim(
        *up_line, line(lines.at[0], 0), line(along, 2), corner(0, 0), corner(0, 1),
        lines[0, last + 1 : last + 2],
    )
    lower = rim(
        *down_line, line(lines.at[1], 3), line(along, 1), corner(1, 4), corner(1, 5),
        lines[1, last + 2 : last + 3],
    )
    return out_left - in_left, out_right - in_right, upper, lower


class Sides:
    def __init__(self, s_ref, near_x, far_x, depth):
        self.s_ref, self.near_x, self.far_x = s_ref, near_x, far_x
        last = 8 * depth
        even = s_ref[8] == 0
        self.gas = (
            jnp.where(even, flat(far_x, last + 1), flat(near_x, last + 1)),
            jnp.where(even, flat(near_x, last + 2), flat(far_x, last + 2)),
        )

    def __call__(self, depth, kind, k, left):
        return side_columns(self.s_ref, self.near_x, self.far_x, depth, kind, k, left)


def final_emit(temp, gas, face, held, weights, done):
    rows, width = held.shape[1:]
    lane = lax.broadcasted_iota(jnp.int32, (CHUNK, width), 1)
    end = width - 1

    def emit(z, start, first, value, pairs):
        at = slice(start, start + CHUNK)
        if first:
            value = value + (STEP_RATE * HEAT_TRANSFER) * (gas[at] - temp[0, at])
            edge = pltpu.roll(face[at], end, 1)
            across = pairs[4]
            left = jnp.where(lane == 0, edge, pltpu.roll(across, 1, 1))
            right = jnp.where(lane == end, edge, across)
            for k, pair in enumerate((pairs[0], pairs[1], left, right, pairs[3])):
                weights[k, at] = (0.5 * STEP_RATE) * pair
        held[z, at] = value
        done(z, start, first)

    return emit


def middle_body(
    s_ref, base_in, temp, cond, kept, gas, packs, mixed, far, base, held, weights,
    packed, flow, inflow, face,
):
    depth, rows, width = temp.shape
    lane = lax.broadcasted_iota(jnp.int32, (CHUNK, width), 1)
    mine, near_x, far_x = sources(packs, mixed, far, depth)
    left_pair, right_pair = inflow_rows(s_ref, mine, near_x, far_x, flow, depth)
    packed[...] = jnp.zeros_like(packed)
    inflow[...] = to_columns(packed, flow)

    def mend(z, nothing):
        for start in range(RIM, rows - RIM, CHUNK):
            at = slice(start, start + CHUNK)
            base[z, at] = base_in[z, at] + (0.5 * STEP_RATE) * entering(inflow, z, at, lane)
        return nothing

    lax.fori_loop(0, depth, mend, 0)
    side = Sides(s_ref, near_x, far_x, depth)
    left_step, right_step, _, _ = tile_rims(mine, near_x, far_x, None, None, depth, width, side)
    interleave(flow, left_pair * left_step, right_pair * right_step)
    inflow[...] = to_columns(packed, flow)
    interleave(flow, left_pair, right_pair)
    face[...] = to_columns(packed, flow)
    step_planes(
        base, cond, None, None, None, None, inflow,
        final_emit(temp, gas, face, held, weights, lambda z, start, first: None),
        range(MIDDLE, rows - MIDDLE, CHUNK), kept,
    )


def outer_body(
    s_ref, base_in, held_in, weights_in, kept_in, temp, cond, gas, packs, along, mixed, far, near_y, far_y,
    base, held, weights, kept, out, top, sems, packed, flow, inflow, face, lines, base_lines,
):
    depth, rows, width = temp.shape
    settle(s_ref, lines, near_y, far_y)
    mine, near_x, far_x = sources(packs, mixed, far, depth)
    left_pair, right_pair = inflow_rows(s_ref, mine, near_x, far_x, flow, depth)
    packed[...] = jnp.zeros_like(packed)
    inflow[...] = to_columns(packed, flow)
    side = Sides(s_ref, near_x, far_x, depth)
    left_step, right_step, base_lines[0], base_lines[1] = tile_rims(
        mine, near_x, far_x, along, lines, depth, width, side
    )
    span = lambda which, kind, k: lines.at[
        which, 4 * depth * kind + depth * k : 4 * depth * kind + depth * (k + 1)
    ]
    cond_up, cond_down = span(0, 1, 1), span(1, 1, 2)
    step_planes(
        temp, cond, span(0, 0, 1), span(1, 0, 2), cond_up, cond_down, inflow,
        base_emit(temp, gas, base, kept),
        (*range(0, RIM, CHUNK), *range(rows - RIM, rows, CHUNK)),
    )
    interleave(flow, left_pair * left_step, right_pair * right_step)
    inflow[...] = to_columns(packed, flow)
    interleave(flow, left_pair, right_pair)
    face[...] = to_columns(packed, flow)

    def done(z, start, first):
        if not first and start + CHUNK == rows:

            @pl.when(z >= 2)
            def _():
                pltpu.make_async_copy(held.at[z], out.at[z], sems.at[z]).start()

    step_planes(
        base, cond, base_lines.at[0], base_lines.at[1], cond_up, cond_down, inflow,
        final_emit(temp, gas, face, held, weights, done),
        (*range(0, MIDDLE, CHUNK), *range(rows - MIDDLE, rows, CHUNK)), kept,
    )
    top[...] = held[:2]
    for z in range(2, depth):
        pltpu.make_async_copy(held.at[z], out.at[z], sems.at[z]).wait()


def faces(value, row, lane, up, down, left, right):
    rows, width = value.shape
    return (
        jnp.where(row == 0, up, pltpu.roll(value, 1, 0)),
        jnp.where(row == rows - 1, down, pltpu.roll(value, rows - 1, 0)),
        jnp.where(lane == 0, left, pltpu.roll(value, 1, 1)),
        jnp.where(lane == width - 1, right, pltpu.roll(value, width - 1, 1)),
    )


def finish_body(
    s_ref, ours, theirs, weights, base, mine, came, filled, pressure, out, held, sem, joined, sems
):
    half = ours.shape[0]
    rows, width = weights.shape[1:]
    sign = (1 - 2 * s_ref[0]).astype(jnp.float32)
    bottom = (1 - 2 * s_ref[3]).astype(jnp.float32)
    second = s_ref[4] == 1
    factor = STEP_RATE * HEAT_TRANSFER * PRESSURE_WORK

    def lines(start, count, minus):
        our_sign = jnp.where(s_ref[0] == 0, 1.0, minus) * factor
        their_sign = jnp.where(s_ref[0] == 0, minus, 1.0) * factor
        at = pl.ds(start, count)
        return our_sign * ours[at] + their_sign * theirs[at]

    begin = pl.multiple_of(s_ref[4] * rows, rows)
    middle = lines(begin, rows, bottom)
    above = lines(jnp.where(second, rows - 1, half - 1), 1, jnp.where(second, bottom, -bottom))
    below = lines(jnp.where(second, 0, rows), 1, jnp.where(second, -bottom, bottom))
    share = middle[:, :width]
    row = lax.broadcasted_iota(jnp.int32, (rows, width), 0)
    lane = lax.broadcasted_iota(jnp.int32, (rows, width), 1)
    around = faces(
        share, row, lane, above[:, :width], below[:, :width],
        middle[:, width : width + 1], middle[:, width + 1 : width + 2],
    )
    added = 2.0 * share
    for k in range(4):
        added = added + weights[k] * (around[k] - share)
    down = weights[4] * share
    held[0] = base[0] + added - down
    held[1] = base[1] + down
    copy = pltpu.make_async_copy(held, out.at[:2], sem)
    copy.start()
    for other in join_planes(s_ref, mine, came, pressure, joined, sems):
        other.wait()
    copy.wait()


def mover(groups, pencils):
    def move(value, target):
        pairs = []
        for g in range(groups):
            for p in range(pencils):
                to = target(g, p)
                pairs.append((g * pencils + p, to[0] * pencils + to[1]))
        return lax.ppermute(value, ("grp", "pen"), pairs)

    return move


def per_device(pressure_source, solid_temp, gas_wall_temp, phase_map, phase_conductivity):
    groups = lax.axis_size("grp")
    pencils = lax.axis_size("pen")
    group_idx = lax.axis_index("grp")
    pencil_idx = lax.axis_index("pen")
    depth_loc, span_len, width = pressure_source.shape
    depth = depth_loc * groups
    half = span_len // 2
    own = depth // 2
    core = group_idx % 2
    low = group_idx // 2
    zi = pencil_idx % Z_RING
    yl = pencil_idx // Z_RING % Y_PAIR
    place = pencil_idx % (Z_RING * Y_PAIR)
    move = mover(groups, pencils)
    tab = make_tables(span_len, width, depth)
    const = {k: tuple(map(jnp.asarray, v)) if isinstance(v, tuple) else jnp.asarray(v) for k, v in tab.items()}
    code = jnp.where(low == 0, core * 4, 7 - 4 * core)
    scalars = jnp.stack([core, low, code, low, core, zi, yl, place, pencil_idx % 2]).astype(jnp.int32)
    span = list(const["span"])
    into = list(const["into"])
    back = list(const["back"])
    span_t = list(const["span_t"])
    tile_rows = span_len // groups
    flip = lambda mask: lambda g, p: (g ^ mask, p)
    near_pair = lambda g, p: (g, p ^ 1)
    far_pair = lambda g, p: (g, (p + 1 if p % 2 else p - 1) % pencils)

    other_core = lambda g, p: (g ^ 1, p)
    other_half = lambda g, p: (g ^ 2, p)
    halves_of = tile_rows // 128
    column_scratch = pltpu.VMEM((tile_rows, width), jnp.float32)
    row_scratch = pltpu.VMEM((width, tile_rows), jnp.float32)
    (pivots,) = run(
        pivot_body, 1.2, scalars, [], [const["lam"], const["sigma"]], [(3 * own + 2, width, half)]
    )
    folded = jax.ShapeDtypeStruct((depth_loc, half, width), jnp.float32)
    away, kept = run_blocks(
        fold_body, 0.8, scalars, [pivots, pressure_source], [ORDER, plane_of(pressure_source)],
        [folded.shape, folded.shape], [plane_of(folded), plane_of(folded)], depth_loc,
    )
    arrived = move(away, other_core)
    (held,) = run(
        held_body, 2.1, scalars, [], [kept, *into, *span], [(depth_loc, width, half)]
    )
    cond, packs, along = run(
        edge_body, 2.8, scalars, [held], [solid_temp, phase_map, gas_wall_temp],
        [(depth, tile_rows, width), (halves_of * (8 * depth + 8), 128), (8 * depth + 8, width)],
        scratch=[column_scratch], small=[phase_conductivity],
    )
    planes, edges, carried, opening, mixed = run(
        arrived_body, 3.4, scalars, [],
        [arrived, held, *into, *span, pivots, const["edge"], const["basis_t"], const["far"],
         packs],
        [(own, width, half), (2, depth, half), (width, half), (width, half),
         (2 * depth * half // 128 + packs.shape[0], 128)],
        scratch=[pltpu.VMEM((2, depth, 8, half), jnp.float32)],
    )
    mixed = move(mixed, near_pair)
    z_got = [move(edges, lambda g, p, d=d: (g, p ^ d)) for d in range(2, Z_RING)]
    far_x = move(packs, far_pair)
    carried_there = move(carried, other_half)
    log_rho = const["log_rho"]
    pair_shape = edges.shape
    base, sides = run(
        inner_body, 4.5, scalars, [edges], [solid_temp, cond, gas_wall_temp],
        [(depth, tile_rows, width), (depth, tile_rows, width)],
    )
    four, two = run(
        functools.partial(z_body, width=width), 0.6, scalars, [far_x, carried_there, base],
        [edges, mixed, *z_got, log_rho], [(4,) + pair_shape[1:], pair_shape],
    )
    there = move(four, other_half)
    beside1 = move(two, lambda g, p: (g, p ^ Z_RING))
    beside2 = move(two, lambda g, p: (g ^ 2, p ^ Z_RING))
    (lines,) = run(
        corner_body, 0.6, scalars, [two], [along, packs, mixed, far_x], [(9 * depth + 8, width)]
    )
    near_y = [move(lines, flip(1)), move(lines, flip(3))]
    flow_scratch = pltpu.VMEM((halves_of, 2 * depth, 128), jnp.float32)
    tile = (depth, tile_rows, width)
    base, begun, weights = run(
        middle_body, 4.5, scalars, [lines],
        [base, solid_temp, cond, sides, gas_wall_temp, packs, mixed, far_x],
        [tile, tile, (5, tile_rows, width)],
        scratch=[row_scratch, flow_scratch, column_scratch, column_scratch],
        aliases={2: 0},
    )
    run8, part, opening = run(
        functools.partial(y_body, width=width), 0.6, scalars, [base, *near_y],
        [four, there, beside1, beside2, log_rho, opening], [pair_shape, pair_shape, opening.shape],
    )
    block = Z_RING * Y_PAIR
    opening_there = move(opening, other_half)
    x_got = [move(run8, lambda g, p, d=d: (g, (p + block * d) % pencils)) for d in range(1, X_RING)]
    _, _, weights, _, final, top = run(
        outer_body, 5.5, scalars, [run8],
        [base, begun, weights, sides, solid_temp, cond, gas_wall_temp, packs, along, mixed, far_x,
         *near_y],
        [tile, tile, (5, tile_rows, width), tile, solid_temp.shape, (2, tile_rows, width)],
        scratch=[
            pltpu.SemaphoreType.DMA((depth,)),
            row_scratch, flow_scratch, column_scratch, column_scratch,
            pltpu.VMEM((2, 9 * depth + 8, width), jnp.float32),
            pltpu.VMEM((2, depth, width), jnp.float32),
        ],
        out_specs=[FAST, FAST, FAST, FAST, ORDER, FAST], aliases={2: 0, 3: 1, 4: 2, 5: 3},
    )
    wall, away, keep = run(
        solve_body, 6.9, scalars, [weights],
        [planes, carried_there, opening_there, run8, part, *x_got, log_rho, pivots, *span_t, *back,
         const["edge"], const["basis"]],
        [(half, 2 * width), (depth_loc, half, width), (depth_loc, width, half)],
        scratch=[
            pltpu.VMEM((own, width, half), jnp.float32),
            pltpu.VMEM((2, depth, half), jnp.float32),
            pltpu.VMEM((2 * width, half), jnp.float32),
        ],
    )
    wall_came = move(wall, other_core)
    came = move(away, other_core)
    (mine,) = run(cells_body, 2.2, scalars, [], [keep, *span_t, *back], [(depth_loc, half, width)])
    pressure, final = run(
        finish_body, 2.5, scalars, [], [wall, wall_came, weights, top, mine, came, (final, ORDER)],
        [pressure_source.shape, final.shape],
        scratch=[
            pltpu.VMEM(top.shape, jnp.float32), pltpu.SemaphoreType.DMA,
            pltpu.VMEM(pressure_source.shape, jnp.float32), pltpu.SemaphoreType.DMA((depth_loc,)),
        ],
        out_specs=[ORDER, ORDER], aliases={7: 1},
    )
    return (pressure, final)


def solution(mesh):
    in_specs = (
        P("grp", None, "pen"),
        P(None, "grp", "pen"),
        P("grp", "pen"),
        P(None, "grp", "pen"),
        P(),
    )
    out_specs = (P("grp", None, "pen"), P(None, "grp", "pen"))
    return jax.shard_map(
        per_device, mesh=mesh, in_specs=in_specs, out_specs=out_specs, check_vma=False
    )
```
